32 devices in a mesh: seq: 2 (over x), ctx: 8 (over z, y), tp: 2 (over core).
Axes of the slice: x: 2, y: 2, z: 4, core: 2. Of those that a mesh axis runs over, the one named last changes fastest.
Arguments:
- tokens: bfloat16 [2048, 2880], P(('seq', 'ctx')), may hold values from -6 to 6
- gain_attn: float32 [2880], replicated, may hold values from 0.5 to 1.5
- w_query: bfloat16 [2880, 4096], P(('seq', 'ctx'), 'tp'), may hold values from -0.109375 to 0.109375
- b_query: float32 [4096], P('tp'), may hold values from -4 to 4
- key_value_weight: bfloat16 [2880, 2, 512], P(('seq', 'ctx'), None, 'tp'), may hold values from -0.109375 to 0.109375
- key_value_bias: float32 [2, 512], P(None, 'tp'), may hold values from -4 to 4
- sinks: float32 [64], P('tp'), may hold values from -1 to 3
- w_out: bfloat16 [4096, 2880], P('tp', ('seq', 'ctx')), may hold values from -1.5 to 1.5
- b_out: float32 [2880], replicated, may hold values from -4 to 4
- gain_moe: float32 [2880], replicated, may hold values from 0.5 to 1.5
- w_router: bfloat16 [2880, 8], replicated, may hold values from -0.0546875 to 0.0546875
- b_router: float32 [8], replicated, may hold values from -3 to 3
- routes: int32 [2048, 4], P(('seq', 'ctx')), may hold values from 0 to 7, all different within a row; in each aligned block of 128 rows (0 to 127, 128 to 255, ...) at most 128 rows name the same one
- w_gate_up: bfloat16 [8, 2880, 2, 2880], P('ctx', None, None, ('seq', 'tp')), may hold values from -0.109375 to 0.109375
- b_gate_up: float32 [8, 2, 2880], P('ctx', None, ('seq', 'tp')), may hold values from -1.5 to 1.5
- w_down: bfloat16 [8, 2880, 2880], P('ctx', ('seq', 'tp')), may hold values from -0.109375 to 0.109375
- b_down: float32 [8, 2880], P('ctx'), may hold values from -1.5 to 1.5
- cotangent: bfloat16 [2048, 2880], P(('seq', 'ctx')), may hold values from -6 to 6
Outputs:
- mixed: bfloat16 [2048, 2880], P(('seq', 'ctx'))
- grad_tokens: bfloat16 [2048, 2880], P(('seq', 'ctx'))
- grad_gain_attn: float32 [2880], replicated
- grad_w_query: float32 [2880, 4096], P(('seq', 'ctx'), 'tp')
- grad_b_query: float32 [4096], P('tp')
- grad_w_key_value: float32 [2880, 2, 512], P(('seq', 'ctx'), None, 'tp')
- grad_b_key_value: float32 [2, 512], P(None, 'tp')
- grad_sinks: float32 [64], P('tp')
- grad_w_out: float32 [4096, 2880], P('tp', ('seq', 'ctx'))
- grad_b_out: float32 [2880], replicated
- grad_gain_moe: float32 [2880], replicated
- grad_w_router: float32 [2880, 8], replicated
- grad_b_router: float32 [8], replicated
- grad_w_gate_up: float32 [8, 2880, 2, 2880], P('ctx', None, None, ('seq', 'tp'))
- grad_b_gate_up: float32 [8, 2, 2880], P('ctx', None, ('seq', 'tp'))
- grad_w_down: float32 [8, 2880, 2880], P('ctx', ('seq', 'tp'))
- grad_b_down: float32 [8, 2880], P('ctx')
The draws below stay inside these ranges and needn't reach their ends.
Inputs may be any that keep to these rules, and one draw needn't show every extreme that they name: `routes`: each row names 4 different experts. In every aligned block of 128 rows (the rows of one index of seq and ctx) no expert is named by more than 128 rows, and in some block some expert is named by exactly 128 rows.
All inputs are finite; a program needn't handle non-finite values.
Results may differ from the reference program's by a relative error of at most 0.03.
Values may be sent and summed in bfloat16 or wider, within the bound.
A program may use at most 320 MiB of HBM per device.

```python
import math
import jax
import jax.numpy as jnp
import numpy as np
from jax import lax

MODEL_DIMENSION = 2880
QUERY_HEADS = 64
KEY_VALUE_HEADS = 8
HEAD_DIMENSION = 64
FF = 2880
TOP = 4
TOK_DEV = 128
EXPERTS = 8
SEQUENCE_LENGTH = 1024
SEQUENCE_COUNT = 2
TOKEN_COUNT = 2048
CAP = 128
N_CTX = 8


def shard_levels(rng, extent, pieces, least, high):
    factor_of, own = 1.0, jax.random.fold_in(rng, 6)
    for position, shards_of in pieces:
        steps = jnp.exp(jax.random.uniform(jax.random.fold_in(own, position), (shards_of,), jnp.float32, least / len(pieces), high / len(pieces)))
        factor_of = factor_of * jnp.repeat(steps, extent[position] // shards_of).reshape([-1 if axis == position else 1 for axis in range(len(extent))])
    return factor_of


def deal_out(key, own, number, rows, count, top, bound, lean):
    sequence = jax.random.permutation(key, count)
    packed, common = portions_of(count, rows * top, bound, lean, True), portions_of(count, rows * top, bound, lean, False)
    places = jnp.arange(count)

    def named(sizes, turn):
        used = int((sizes > 0).sum())
        fixed = max(1, used // 4)
        passed = fixed + (places - fixed + turn * (used - fixed)) % max(1, count - fixed)
        return jnp.zeros((count,), jnp.int32).at[sequence[jnp.where(places < fixed, places, passed)]].set(jnp.asarray(sizes, jnp.int32))

    sizes = jnp.where(number % 4 == 0, named(packed, number // 4), named(common, number - number // 4 - 1))
    mixed = jax.random.permutation(jax.random.fold_in(own, 3), count)
    donor, receiver = mixed[0:count // 2 * 2:2], mixed[1:count // 2 * 2:2]
    room = jnp.minimum(sizes[donor] - 1, bound - sizes[receiver]) // 2
    room = jnp.where((donor == sequence[0]) | (receiver == sequence[0]) | (sizes[receiver] == 0), 0, jnp.maximum(room, 0))
    passed = jax.random.randint(jax.random.fold_in(own, 4), (count // 2,), 0, 1 << 20) % (room + 1)
    sizes = sizes.at[donor].add(-passed).at[receiver].add(passed)
    labels = jnp.searchsorted(jnp.cumsum(sizes), jnp.arange(rows * top), side="right").astype(jnp.int32)
    listing = labels.reshape(top, rows).T
    listing = listing[jax.random.permutation(jax.random.fold_in(own, 1), rows)]
    turn = jax.random.randint(jax.random.fold_in(own, 2), (rows, 1), 0, top)
    return jnp.take_along_axis(listing, (jnp.arange(top)[None, :] + turn) % top, axis=1)


def portions_of(amount, total, most, lean, full):
    weights = [(1 << 20) // math.isqrt(grade ** lean) + 1 for grade in range(1, amount + 1)]
    largest = most if full else min(most, max(-(-total // amount), total * weights[0] // sum(weights)))
    least = 1 if total - largest >= amount - 1 else 0
    given, spare = [largest] + [least] * (amount - 1), total - largest - least * (amount - 1)
    while spare > 0:
        free = [i for i in range(1, amount) if given[i] < largest] or [i for i in range(1, amount) if given[i] < most]
        pool, left = sum([weights[i] for i in free]), spare
        for i in free:
            extra = min(most - given[i], max(1, left * weights[i] // pool), spare)
            given[i] = given[i] + extra
            spare = spare - extra
    return np.array(given)


def bell_draw(rng, shape, spread, bound, pieces=(), held_as=jnp.bfloat16):
    array = jax.random.normal(rng, shape, jnp.float32) * spread
    if len(pieces) > 0:
        array = shard_levels(rng, shape, pieces, -0.22, 0.18) * array
    return jnp.clip(array, min=-bound, max=bound).astype(held_as)


def setup_inputs(seed: int = 0) -> dict:
    splits = jax.random.split(jax.random.key(seed), 19)
    tokens = bell_draw(splits[0], (TOKEN_COUNT, MODEL_DIMENSION), 1.0, 6.0, ((0, 16),))
    gain_attn = jnp.clip(1.0 + 0.1 * jax.random.normal(splits[1], (MODEL_DIMENSION,), jnp.float32), 0.5, 1.5)
    w_query = bell_draw(splits[2], (MODEL_DIMENSION, QUERY_HEADS * HEAD_DIMENSION), MODEL_DIMENSION ** -0.5, 0.109375, ((0, 16), (1, 2)))
    b_query = bell_draw(splits[3], (QUERY_HEADS * HEAD_DIMENSION,), 0.3, 4.0, ((0, 2),), jnp.float32)
    key_value_weight = bell_draw(splits[4], (MODEL_DIMENSION, 2, KEY_VALUE_HEADS * HEAD_DIMENSION), MODEL_DIMENSION ** -0.5, 0.109375, ((0, 16), (2, 2)))
    key_value_bias = bell_draw(splits[5], (2, KEY_VALUE_HEADS * HEAD_DIMENSION), 0.3, 4.0, ((1, 2),), jnp.float32)
    sinks = jnp.clip(-1.0 + 4.0 * jax.random.uniform(splits[6], (QUERY_HEADS,), jnp.float32) ** shard_levels(splits[6], (QUERY_HEADS,), ((0, 2),), -0.2, 0.2), -1.0, 3.0)
    w_out = bell_draw(splits[7], (QUERY_HEADS * HEAD_DIMENSION, MODEL_DIMENSION), (QUERY_HEADS * HEAD_DIMENSION // 256) ** -0.5, 1.5, ((0, 2), (1, 16)))
    b_out = bell_draw(splits[8], (MODEL_DIMENSION,), 0.3, 4.0, (), jnp.float32)
    gain_moe = jnp.clip(1.0 + 0.1 * jax.random.normal(splits[9], (MODEL_DIMENSION,), jnp.float32), 0.5, 1.5)
    w_router = bell_draw(splits[10], (MODEL_DIMENSION, EXPERTS), (4 * MODEL_DIMENSION) ** -0.5, 0.0546875)
    b_router = bell_draw(splits[11], (EXPERTS,), 0.2, 3.0, (), jnp.float32)
    routes_keys = jax.random.split(jax.random.fold_in(splits[12], 1), TOKEN_COUNT // TOK_DEV)
    routes_turns = jax.random.permutation(jax.random.fold_in(splits[12], 3), TOKEN_COUNT // TOK_DEV)
    routes = jax.vmap(lambda own, number: deal_out(jax.random.fold_in(splits[12], 2), own, number, TOK_DEV, EXPERTS, TOP, CAP, 1))(routes_keys, routes_turns).reshape((TOKEN_COUNT, TOP))
    w_gate_up = bell_draw(splits[13], (EXPERTS, MODEL_DIMENSION, 2, FF), MODEL_DIMENSION ** -0.5, 0.109375, ((0, 8), (3, 4)))
    b_gate_up = bell_draw(splits[14], (EXPERTS, 2, FF), 0.1, 1.5, ((0, 8), (2, 4)), jnp.float32)
    w_down = bell_draw(splits[15], (EXPERTS, FF, MODEL_DIMENSION), FF ** -0.5, 0.109375, ((0, 8), (1, 4)))
    b_down = bell_draw(splits[16], (EXPERTS, MODEL_DIMENSION), 0.1, 1.5, ((0, 8),), jnp.float32)
    cotangent = bell_draw(splits[17], (TOKEN_COUNT, MODEL_DIMENSION), 1.0, 6.0, ((0, 16),))
    return dict(tokens=tokens, gain_attn=gain_attn, w_query=w_query, b_query=b_query, key_value_weight=key_value_weight, key_value_bias=key_value_bias, sinks=sinks, w_out=w_out, b_out=b_out, gain_moe=gain_moe, w_router=w_router, b_router=b_router, routes=routes, w_gate_up=w_gate_up, b_gate_up=b_gate_up, w_down=w_down, b_down=b_down, cotangent=cotangent)


@jax.custom_vjp
def low(v):
    return lax.optimization_barrier(v.astype(jnp.bfloat16)).astype(jnp.float32)

@jax.custom_vjp
def low_back(v):
    return v

def low_keep(v):
    return (low(v), None)

def low_pass(kept, grad):
    return (grad,)

def back_keep(v):
    return (v, None)

def back_low(kept, grad):
    return (low(grad),)
low.defvjp(low_keep, low_pass)
low_back.defvjp(back_keep, back_low)
rms_eps = 1e-05
rope_base = 150000.0
clamp_limit = 7.0
glu_alpha = 1.702
masked_score = -1e+30

def norm_rows(row_block, gain_vec):
    return row_block * lax.rsqrt(lax.optimization_barrier(jnp.mean(row_block * row_block, axis=-1, keepdims=True)) + rms_eps) * gain_vec

def highest(left, right):
    return jnp.dot(left, right, precision=lax.Precision.HIGHEST)

def rotary(positions):
    half_size = HEAD_DIMENSION // 2
    frequency = rope_base ** (-2.0 * jnp.arange(half_size, dtype=jnp.float32) / HEAD_DIMENSION)
    angles = positions.astype(jnp.float32)[:, None] * frequency[None, :]
    return (jnp.cos(angles), jnp.sin(angles))

def apply_rotation(heads_in, cosine_lookup, sine_lookup):
    half_size = heads_in.shape[-1] // 2
    lower_half = heads_in[..., :half_size]
    upper_half = heads_in[..., half_size:]
    cosine_part = cosine_lookup[:, None, :]
    sine_part = sine_lookup[:, None, :]
    return jnp.concatenate([lower_half * cosine_part - upper_half * sine_part, upper_half * cosine_part + lower_half * sine_part], axis=-1)

def expert_act(gate_part, up_part):
    gate_soft = clamp_limit * jnp.tanh(gate_part / clamp_limit)
    up_soft = clamp_limit * jnp.tanh(up_part / clamp_limit)
    return (up_soft + 1.0) * gate_soft * jax.nn.sigmoid(glu_alpha * gate_soft)

def attend_sequence(query_rows, key_matrix_rows, value_matrix_rows, sinks):
    token_length = query_rows.shape[0]
    rows_per_block = min(512, token_length)
    query_group_width = QUERY_HEADS // KEY_VALUE_HEADS
    query_block_list = query_rows.reshape(token_length // rows_per_block, rows_per_block, KEY_VALUE_HEADS, query_group_width, HEAD_DIMENSION)
    block_starts = jnp.arange(token_length // rows_per_block, dtype=jnp.int32) * rows_per_block
    key_pos = jnp.arange(token_length, dtype=jnp.int32)
    attention_sink_rows = sinks.reshape(KEY_VALUE_HEADS, query_group_width, 1)

    @jax.checkpoint
    def one_block(item_pack):
        query_blk, start_row = item_pack
        scores = jnp.einsum('qgjd,kgd->gjqk', query_blk, key_matrix_rows, precision=lax.Precision.HIGHEST) / math.sqrt(HEAD_DIMENSION)
        scores = low_back(scores)
        query_pos = start_row + jnp.arange(rows_per_block, dtype=jnp.int32)
        allowed = key_pos[None, :] <= query_pos[:, None]
        scores = jnp.where(allowed, scores, masked_score)
        row_top = jnp.maximum(lax.optimization_barrier(jnp.max(scores, axis=-1)), attention_sink_rows)
        norm_total = jnp.exp(attention_sink_rows - row_top) + lax.optimization_barrier(jnp.sum(jnp.exp(scores - row_top[..., None]), axis=-1))
        log_total = row_top + jnp.log(norm_total)
        probs = low(jnp.exp(scores - log_total[..., None]))
        return jnp.einsum('gjqk,kgd->qgjd', probs, value_matrix_rows, precision=lax.Precision.HIGHEST)
    outputs = lax.map(one_block, (query_block_list, block_starts))
    return outputs.reshape(token_length, QUERY_HEADS, HEAD_DIMENSION)

def block_layer(tokens, gain_attn, w_query, b_query, key_value_weight, key_value_bias, sinks, w_out, b_out, gain_moe, w_router, b_router, w_gate_up, b_gate_up, w_down, b_down, routes):
    key_value_width = KEY_VALUE_HEADS * HEAD_DIMENSION
    normed_attn = low(norm_rows(tokens, gain_attn))
    query_proj = low_back(highest(normed_attn, w_query) + b_query)
    key_value_projected = low_back(highest(normed_attn, key_value_weight.reshape(MODEL_DIMENSION, 2 * key_value_width)) + key_value_bias.reshape(-1))
    positions = jnp.tile(jnp.arange(SEQUENCE_LENGTH, dtype=jnp.int32), SEQUENCE_COUNT)
    cosine_lookup, sine_lookup = rotary(positions)
    query_rows = low(apply_rotation(query_proj.reshape(TOKEN_COUNT, QUERY_HEADS, HEAD_DIMENSION), cosine_lookup, sine_lookup))
    key_matrix_rows = low(apply_rotation(key_value_projected[:, :key_value_width].reshape(TOKEN_COUNT, KEY_VALUE_HEADS, HEAD_DIMENSION), cosine_lookup, sine_lookup))
    value_matrix_rows = low(key_value_projected[:, key_value_width:].reshape(TOKEN_COUNT, KEY_VALUE_HEADS, HEAD_DIMENSION))

    def single_sequence(item_pack):
        return attend_sequence(item_pack[0], item_pack[1], item_pack[2], sinks)
    attention_result = lax.map(single_sequence, (query_rows.reshape(SEQUENCE_COUNT, SEQUENCE_LENGTH, QUERY_HEADS, HEAD_DIMENSION), key_matrix_rows.reshape(SEQUENCE_COUNT, SEQUENCE_LENGTH, KEY_VALUE_HEADS, HEAD_DIMENSION), value_matrix_rows.reshape(SEQUENCE_COUNT, SEQUENCE_LENGTH, KEY_VALUE_HEADS, HEAD_DIMENSION)))
    attention_result = low_back(attention_result.reshape(TOKEN_COUNT, QUERY_HEADS * HEAD_DIMENSION))
    attn_out = low_back(highest(low(attention_result), w_out) + b_out)
    hidden = tokens + attn_out
    normed_moe = low(norm_rows(hidden, gain_moe))
    logits = low_back(highest(normed_moe, w_router) + b_router)
    chosen = jnp.take_along_axis(logits, routes, axis=1)
    gates = jax.nn.softmax(chosen, axis=-1)
    block_count = SEQUENCE_COUNT * N_CTX
    flat_routes = routes.reshape(block_count, TOK_DEV * TOP)
    route_hits = (flat_routes[..., None] == jnp.arange(EXPERTS, dtype=jnp.int32)).astype(jnp.int32)
    slot_rank = lax.optimization_barrier(jnp.sum((jnp.cumsum(route_hits, axis=1) - route_hits) * route_hits, axis=-1))
    anchor = jnp.arange(block_count, dtype=jnp.int32)[:, None]
    target = (flat_routes * (block_count * CAP) + anchor * CAP + slot_rank).reshape(-1)
    buffer_rows = jnp.zeros((EXPERTS * block_count * CAP, MODEL_DIMENSION), jnp.float32).at[target].set(jnp.repeat(normed_moe, TOP, axis=0))
    buffer_rows = low_back(buffer_rows)

    @jax.checkpoint
    def one_expert(item_pack):
        rows_in, gate_up_w, gate_up_b, down_w, down_b = item_pack
        projected = low_back(highest(rows_in, gate_up_w.reshape(MODEL_DIMENSION, 2 * FF)) + gate_up_b.reshape(-1))
        activated = low(expert_act(projected[:, :FF], projected[:, FF:]))
        return low(low_back(highest(activated, down_w) + down_b))
    expert_rows = lax.map(one_expert, (buffer_rows.reshape(EXPERTS, block_count * CAP, MODEL_DIMENSION), w_gate_up, b_gate_up, w_down, b_down))
    returned = expert_rows.reshape(-1, MODEL_DIMENSION)[target].reshape(TOKEN_COUNT, TOP, MODEL_DIMENSION)
    return hidden + lax.optimization_barrier(jnp.sum(gates[..., None] * returned, axis=1))

def reference(tokens, gain_attn, w_query, b_query, key_value_weight, key_value_bias, sinks, w_out, b_out, gain_moe, w_router, b_router, routes, w_gate_up, b_gate_up, w_down, b_down, cotangent):
    params = (tokens, gain_attn, w_query, b_query, key_value_weight, key_value_bias, sinks, w_out, b_out, gain_moe, w_router, b_router, w_gate_up, b_gate_up, w_down, b_down)
    params = tuple((entry.astype(jnp.float32) for entry in params))

    def forward(*floats):
        return block_layer(*floats, routes)
    output, pullback = jax.vjp(forward, *params)
    grads = pullback(cotangent.astype(jnp.float32))
    return (output.astype(jnp.bfloat16), grads[0].astype(jnp.bfloat16), grads[1], grads[2], grads[3], grads[4], grads[5], grads[6], grads[7], grads[8], grads[9], grads[10], grads[11], grads[12], grads[13], grads[14], grads[15])
```

```python
import functools
import math

import jax
import jax.numpy as jnp
from jax import lax
from jax.experimental import pallas as pl
from jax.experimental.pallas import tpu as pltpu
from jax.sharding import PartitionSpec as P

HEAD_DIMENSION = 64

rms_eps = 1e-05
rope_base = 150000.0
clamp_limit = 7.0
glu_alpha = 1.702
masked_score = -1e30
vmem_bytes = 56 * 1024 * 1024
vmem_most = 63 * 1024 * 1024
bf16 = jnp.bfloat16
f32 = jnp.float32


def across(left, right):
    return lax.dot_general(left, right, (((1,), (1,)), ((), ())), preferred_element_type=f32)


def down(left, right):
    return lax.dot_general(left, right, (((0,), (0,)), ((), ())), preferred_element_type=f32)


def ring_place(index, size):
    half = index // 2
    return jnp.where(index % 2 == 0, half, size - 1 - half)


def ring_index(place, size):
    place = lax.rem(place + size, size)
    return jnp.where(place < size // 2, 2 * place, 2 * (size - 1 - place) + 1)


def greet(devices):
    barrier = pltpu.get_barrier_semaphore()
    for device in devices:
        pl.semaphore_signal(barrier, inc=1, device_id=device, device_id_type=pl.DeviceIdType.MESH)
    pl.semaphore_wait(barrier, len(devices))


def remote(src, dst, send_sem, recv_sem, device):
    copy = pltpu.make_async_remote_copy(
        src_ref=src,
        dst_ref=dst,
        send_sem=send_sem,
        recv_sem=recv_sem,
        device_id=device,
        device_id_type=pl.DeviceIdType.MESH,
    )
    copy.start()
    return copy


def rows_at(start, count):
    return pl.ds(pl.multiple_of(start, count), count)


class Around:
    def __init__(self, size):
        self.size = size
        self.seq = lax.axis_index("seq")
        self.ctx = lax.axis_index("ctx")
        self.core = lax.axis_index("tp")
        self.place = ring_place(self.ctx, size)
        self.right = (self.seq, ring_index(self.place + 1, size), self.core)
        self.left = (self.seq, ring_index(self.place - 1, size), self.core)
        self.across = (1 - self.seq, self.ctx, self.core)
        self.sibling = (self.seq, self.ctx, 1 - self.core)

    def index(self, offset):
        return ring_index(self.place + offset, self.size)

    def at(self, offset):
        return (self.seq, self.index(offset), self.core)


class RingGather:
    def __init__(self, around, both, x_ref, o_ref, ring_s, ring_r, cross_s, cross_r, core_s, core_r, loc):
        self.a, self.both, self.x, self.o = around, both, x_ref, o_ref
        self.rs, self.rr, self.cs, self.cr = ring_s, ring_r, cross_s, cross_r
        self.ts, self.tr, self.loc = core_s, core_r, loc
        self.rows = x_ref.shape[0]
        self.chunk = self.rows // 4
        size = around.size
        far, near = size // 2, size - 1 - size // 2
        if both:
            self.items = [(1, False, far, near), (0, False, near, far), (0, True, far, near)]
        else:
            self.items = [(0, False, far, near), (1, False, near, far)]

    def partners(self):
        a = self.a
        return [a.right, a.left, a.sibling] + ([a.across] if self.both else [])

    def spot(self, other, index, chunk):
        a = self.a
        if self.both:
            block = (1 - a.seq if other else a.seq) * a.size + index + a.core * 2 * a.size
            return rows_at(block * (2 * self.chunk) + chunk * self.chunk, self.chunk)
        return rows_at(index * self.rows + a.core * (2 * self.chunk) + chunk * self.chunk, self.chunk)

    def own(self, chunk):
        return self.x.at[rows_at(self.a.core * (2 * self.chunk) + chunk * self.chunk, self.chunk)]

    def hop(self, item, way, step, src, where):
        device = self.a.right if way == 0 else self.a.left
        copy = remote(
            src, self.o.at[where], self.rs.at[item, way, step], self.rr.at[item, way, step], device
        )
        self.ring[item, way, step] = copy
        self.sent.append(copy)

    def cross(self, slot, src, where):
        copy = remote(src, self.o.at[where], self.cs.at[slot], self.cr.at[slot], self.a.across)
        self.crossed[slot] = copy
        self.sent.append(copy)

    def share(self, where):
        slot = len(self.shared)
        src = self.o.at[where]
        copy = remote(src, src, self.ts.at[slot], self.tr.at[slot], self.a.sibling)
        self.shared.append(copy)
        self.sent.append(copy)

    def start(self):
        a = self.a
        self.ring, self.crossed, self.shared, self.sent = {}, {}, [], []
        if self.both:
            half = 2 * self.chunk
            block = a.seq * a.size + a.ctx
            pairs = [
                (self.x.at[pl.ds(core * half, half)], rows_at((core * 2 * a.size + block) * half, half))
                for core in range(2)
            ]
        else:
            pairs = [(self.x, rows_at(a.ctx * self.rows, self.rows))]
        self.local = [
            pltpu.make_async_copy(src, self.o.at[where], self.loc.at[at])
            for at, (src, where) in enumerate(pairs)
        ]
        for copy in self.local:
            copy.start()
        if self.both:
            self.cross(0, self.own(0), self.spot(False, a.ctx, 0))
        for item, (chunk, other, _, _) in enumerate(self.items):
            if not other:
                for way in range(2):
                    self.hop(item, way, 0, self.own(chunk), self.spot(False, a.ctx, chunk))
        self.landed = []
        if self.both:
            self.cross(1, self.own(1), self.spot(False, a.ctx, 1))
            self.landed.append((1, a.ctx))
            self.crossed[0].wait_recv()
            where = self.spot(True, a.ctx, 0)
            for way in range(2):
                self.hop(2, way, 0, self.o.at[where], where)
            self.share(where)

    def step(self, k):
        a = self.a
        for item, (chunk, other, right, left) in enumerate(self.items):
            for way, hops in ((0, right), (1, left)):
                if k >= hops:
                    continue
                self.ring[item, way, k].wait_recv()
                index = a.index(-(k + 1) if way == 0 else k + 1)
                where = self.spot(other, index, chunk)
                if k + 1 < hops:
                    self.hop(item, way, k + 1, self.o.at[where], where)
                if self.both and item == 0:
                    slot = 1 + len(self.landed)
                    self.cross(slot, self.o.at[where], where)
                    self.landed.append((slot, index))
                self.share(where)

    def finish(self):
        for slot, index in self.landed:
            self.crossed[slot].wait_recv()
            self.share(self.spot(True, index, 1))
        for copy in self.shared:
            copy.wait_recv()
        for copy in self.sent:
            copy.wait_send()
        for copy in self.local:
            copy.wait()

    @staticmethod
    def semaphores(size, both):
        items = 3 if both else 2
        shares = 2 * (size - 1) + (2 * size if both else 0)
        dma = pltpu.SemaphoreType.DMA
        return [
            dma((items, 2, size // 2)),
            dma((items, 2, size // 2)),
            dma((1 + size,)),
            dma((1 + size,)),
            dma((shares,)),
            dma((shares,)),
            dma((2,)),
        ]


def gather_kernel(size, both, *refs):
    if both:
        x_ref, half_ref, o_ref, whole_ref, held, half_s, half_r, half_l, *sems = refs
    else:
        x_ref, o_ref, *sems = refs
    ring = RingGather(Around(size), both, x_ref, o_ref, *sems)
    greet(ring.partners())
    ring.start()
    if both:
        where = whole_ref.at[rows_at(ring.a.core * half_ref.shape[0], half_ref.shape[0])]
        other = remote(half_ref, where, half_s, half_r, ring.a.sibling)
        here = pltpu.make_async_copy(half_ref, held, half_l.at[0])
        here.start()
        here.wait()
        here = pltpu.make_async_copy(held, where, half_l.at[1])
        here.start()
    for k in range(size // 2):
        ring.step(k)
    ring.finish()
    if both:
        here.wait()
        other.wait()


def ring_gather(x, size, ident, half=None):
    hbm = pl.BlockSpec(memory_space=pl.ANY)
    both = half is not None
    blocks = (2 if both else 1) * size
    shapes = [jax.ShapeDtypeStruct((blocks * x.shape[0], x.shape[1]), x.dtype)]
    if both:
        shapes.append(jax.ShapeDtypeStruct((2 * half.shape[0], half.shape[1]), half.dtype))
    dma = pltpu.SemaphoreType.DMA
    extra = [pltpu.VMEM(half.shape, half.dtype), dma(()), dma(()), dma((2,))] if both else []
    out = pl.pallas_call(
        functools.partial(gather_kernel, size, both),
        out_shape=shapes,
        in_specs=[hbm, hbm] if both else [hbm],
        out_specs=[hbm] * len(shapes),
        scratch_shapes=extra + RingGather.semaphores(size, both),
        compiler_params=pltpu.CompilerParams(
            collective_id=ident, has_side_effects=True, vmem_limit_bytes=vmem_bytes
        ),
        name="gather_all" if both else "gather_ctx",
    )(*((x, half) if both else (x,)))
    return out if both else out[0]


def enter_kernel(size, x_ref, w_ref, o_ref, wo_ref, w_s, w_r, wx_s, wx_r, wl, *sems):
    a = Around(size)
    ring = RingGather(a, False, x_ref, o_ref, *sems)
    order = []
    for d in range(1, size // 2 + 1):
        order += [d] if 2 * d == size else [d, size - d]
    greet(ring.partners() + [a.across] + [a.at(d) for d in order if 1 < d < size - 1])
    mine = a.seq * size + a.ctx
    local = pltpu.make_async_copy(w_ref.at[a.ctx], wo_ref.at[mine], wl)
    local.start()
    ring.start()
    crossed = [remote(w_ref.at[a.ctx], wo_ref.at[mine], wx_s.at[0], wx_r.at[0], a.across)]
    sent = {}
    for d in order:
        sent[d] = remote(w_ref.at[a.index(d)], wo_ref.at[mine], w_s.at[d], w_r.at[d], a.at(d))
    taken = 0

    def take():
        d = order[len(crossed) - 1]
        sent[d].wait_recv()
        block = wo_ref.at[a.seq * size + a.index(-d)]
        crossed.append(remote(block, block, wx_s.at[d], wx_r.at[d], a.across))

    for k in range(size // 2):
        ring.step(k)
        for _ in range(2):
            if len(crossed) < size:
                take()
    ring.finish()
    for copy in crossed:
        copy.wait()
    for copy in sent.values():
        copy.wait_send()
    local.wait()


def enter(x, w, size, ident):
    dma = pltpu.SemaphoreType.DMA
    hbm = pl.BlockSpec(memory_space=pl.ANY)
    return pl.pallas_call(
        functools.partial(enter_kernel, size),
        out_shape=(
            jax.ShapeDtypeStruct((size * x.shape[0], x.shape[1]), x.dtype),
            jax.ShapeDtypeStruct((2 * size,) + w.shape[1:], w.dtype),
        ),
        in_specs=[hbm, hbm],
        out_specs=(hbm, hbm),
        scratch_shapes=[dma((size,)), dma((size,)), dma((size,)), dma((size,)), dma(())]
        + RingGather.semaphores(size, False),
        compiler_params=pltpu.CompilerParams(collective_id=ident, has_side_effects=True),
        name="enter_rows_and_weights",
    )(x, w)


class RingSum:
    def __init__(
        self, around, both, p_ref, o_ref, acc, met, ringbuf, crossbuf, lastbuf,
        ring_s, ring_r, cross_s, cross_r, core_s, core_r, out_s, out_r, loc,
    ):
        self.a, self.both, self.p, self.o = around, both, p_ref, o_ref
        self.acc, self.met, self.ringbuf = acc, met, ringbuf
        self.crossbuf, self.lastbuf = crossbuf, lastbuf
        self.rs, self.rr, self.cs, self.cr = ring_s, ring_r, cross_s, cross_r
        self.ts, self.tr, self.os, self.or_, self.loc = core_s, core_r, out_s, out_r, loc
        self.rows = o_ref.shape[0]
        self.half, self.chunk = self.rows // 2, self.rows // 4
        size = around.size
        far, near = size // 2, size - 1 - size // 2
        if both:
            self.items = [(0, 1, far, near), (0, 0, near, far), (1, 0, far, near)]
        else:
            self.items = [(0, 0, far, near), (1, 0, near, far)]
        order = []
        for d in range(size // 2, 0, -1):
            order += [d] if 2 * d == size else [d, size - d]
        self.order = order + [0]

    def partners(self):
        a = self.a
        return [a.right, a.left, a.sibling] + ([a.across] if self.both else [])

    def spot(self, other, offset, core):
        a = self.a
        block = a.index(offset)
        if self.both:
            block = core * 2 * a.size + (1 - a.seq if other else a.seq) * a.size + block
        else:
            block = 2 * block + core
        return rows_at(block * self.half, self.half)

    def start(self):
        a = self.a
        self.pending, self.sent, self.ring, self.crossed = {}, [], {}, {}
        for other in ((1, 0) if self.both else (0,)):
            for j in self.order:
                away = remote(
                    self.p.at[self.spot(other, j, 1 - a.core)],
                    self.met.at[other, j],
                    self.ts.at[other, j],
                    self.tr.at[other, j],
                    a.sibling,
                )
                here = pltpu.make_async_copy(
                    self.p.at[self.spot(other, j, a.core)], self.acc.at[other, j], self.loc.at[other, j]
                )
                here.start()
                self.pending[other, j] = (away, here)
                self.sent.append(away)
        if self.both:
            for j in self.order:
                self.ready(1, j)
                self.crossed[j] = remote(
                    self.part(self.acc, 1, j, 1), self.crossbuf.at[j], self.cs.at[j], self.cr.at[j], a.across
                )
                self.sent.append(self.crossed[j])

    def part(self, ref, other, j, chunk):
        return ref.at[other, j, pl.ds(chunk * self.chunk, self.chunk)]

    def ready(self, other, j):
        if (other, j) in self.pending:
            away, here = self.pending.pop((other, j))
            away.wait_recv()
            here.wait()
            self.add(self.acc.at[other, j], self.met.at[other, j])

    def add(self, into, more):
        into[...] = (into[...].astype(f32) + more[...].astype(f32)).astype(into.dtype)

    def prepare(self, other, j, chunk):
        self.ready(other, j)
        if self.both and chunk == 1 and j in self.crossed:
            self.crossed.pop(j).wait_recv()
            self.add(self.part(self.acc, 0, j, 1), self.crossbuf.at[j])

    def step(self, k):
        a = self.a
        for item, (chunk, other, right, left) in enumerate(self.items):
            for way, hops in ((0, right), (1, left)):
                d = hops - k
                if d < 1:
                    continue
                j = d if way == 0 else a.size - d
                self.prepare(other, j, chunk)
                block = self.part(self.acc, other, j, chunk)
                if k > 0:
                    self.ring[item, way, d].wait_recv()
                    self.add(block, self.ringbuf.at[item, way, d])
                copy = remote(
                    block,
                    self.ringbuf.at[item, way, d - 1],
                    self.rs.at[item, way, d - 1],
                    self.rr.at[item, way, d - 1],
                    a.right if way == 0 else a.left,
                )
                self.ring[item, way, d - 1] = copy
                self.sent.append(copy)

    def finish(self):
        a = self.a
        last = []
        for item, (chunk, other, _, _) in enumerate(self.items):
            self.prepare(other, 0, chunk)
            block = self.part(self.acc, other, 0, chunk)
            for way in range(2):
                self.ring[item, way, 0].wait_recv()
                self.add(block, self.ringbuf.at[item, way, 0])
            if other:
                slot = a.size
                final = remote(block, self.lastbuf, self.cs.at[slot], self.cr.at[slot], a.across)
                self.sent.append(final)
            else:
                last.append((chunk, block))
        for chunk, block in sorted(last, key=lambda entry: -entry[0]):
            if self.both and chunk == 0:
                final.wait_recv()
                self.add(block, self.lastbuf)
            where = rows_at(a.core * self.half + chunk * self.chunk, self.chunk)
            self.o[where] = block[...]
            copy = remote(
                self.o.at[where], self.o.at[where], self.os.at[chunk], self.or_.at[chunk], a.sibling
            )
            self.sent.append(copy)
            last_copy = copy
            self.outs = getattr(self, "outs", []) + [last_copy]
        for copy in self.outs:
            copy.wait_recv()
        for copy in self.sent:
            copy.wait_send()

    @staticmethod
    def scratch(size, both, rows, width, dtype):
        items = 3 if both else 2
        plane = 2 if both else 1
        half, chunk = rows // 2, rows // 4
        dma = pltpu.SemaphoreType.DMA
        few = size if both else 1
        return [
            pltpu.VMEM((plane, size, half, width), dtype),
            pltpu.VMEM((plane, size, half, width), dtype),
            pltpu.VMEM((items, 2, size // 2, chunk, width), dtype),
            pltpu.VMEM((few, chunk, width), dtype),
            pltpu.VMEM((chunk, width), dtype),
            dma((items, 2, size // 2)),
            dma((items, 2, size // 2)),
            dma((few + 1,)),
            dma((few + 1,)),
            dma((plane, size)),
            dma((plane, size)),
            dma((2,)),
            dma((2,)),
            dma((plane, size)),
        ]


def sum_kernel(size, both, p_ref, o_ref, *scratch):
    ring = RingSum(Around(size), both, p_ref, o_ref, *scratch)
    greet(ring.partners())
    ring.start()
    for k in range(size // 2):
        ring.step(k)
    ring.finish()


def ring_sum(p, size, both, ident):
    blocks = (2 if both else 1) * size
    rows, width = p.shape[0] // blocks, p.shape[1]
    return pl.pallas_call(
        functools.partial(sum_kernel, size, both),
        out_shape=jax.ShapeDtypeStruct((rows, width), p.dtype),
        in_specs=[pl.BlockSpec(memory_space=pl.ANY)],
        out_specs=pl.BlockSpec(memory_space=pltpu.VMEM),
        scratch_shapes=RingSum.scratch(size, both, rows, width, p.dtype),
        compiler_params=pltpu.CompilerParams(
            collective_id=ident, has_side_effects=True, vmem_limit_bytes=vmem_bytes
        ),
        name="sum_all" if both else "sum_ctx",
    )(p)


def leave_kernel(
    size, shared, p_ref, g_ref, v_ref, o_ref, go_ref, vo_ref,
    gacc, gmet, vmet, gx_s, gx_r, g_s, g_r, gl, v_s, v_r, *scratch,
):
    a = Around(size)
    ring = RingSum(a, False, p_ref, o_ref, *scratch)
    order = ring.order
    greet(ring.partners() + [a.across] + [a.at(d) for d in order if 1 < d < size - 1])

    swaps = [remote(v_ref, vmet.at[0], v_s.at[0], v_r.at[0], a.across)]

    def swap(slot, device):
        return remote(vo_ref, vmet.at[slot], v_s.at[slot], v_r.at[slot], device)

    crossed, here = {}, {}
    for d in order:
        index = a.index(d)
        crossed[d] = remote(
            g_ref.at[(1 - a.seq) * size + index], gmet.at[d], gx_s.at[d], gx_r.at[d], a.across
        )
        here[d] = pltpu.make_async_copy(g_ref.at[a.seq * size + index], gacc.at[d], gl.at[d])
        here[d].start()
    ring.start()
    sent = {}

    def pass_on(d):
        crossed[d].wait_recv()
        here[d].wait()
        ring.add(gacc.at[d], gmet.at[d])
        if d:
            sent[d] = remote(gacc.at[d], go_ref.at[a.ctx], g_s.at[d], g_r.at[d], a.at(d))
        else:
            go_ref[a.ctx] = gacc[d]

    todo = list(order)
    pair = a.ctx + 1 - 2 * (a.ctx % 2)
    for k in range(size // 2):
        ring.step(k)
        if k == 0:
            swaps[0].wait()
            vo_ref[...] = v_ref[...] + vmet[0]
            swaps = [swap(1, (a.seq, pair, a.core))]
        elif k == 2:
            swaps[0].wait()
            vo_ref[...] += vmet[1]
            swaps = [
                swap(1 + d, (a.seq, lax.rem(a.ctx + 2 * d, size), a.core)) for d in range(1, size // 2)
            ]
        for _ in range(2):
            pass_on(todo.pop(0))
    ring.finish()
    while todo:
        pass_on(todo.pop(0))
    for copy in swaps:
        copy.wait()
    for d in range(1, size // 2):
        vo_ref[...] += vmet[1 + d]
    head = pl.ds(0, shared)
    last = 1 + size // 2
    copy = remote(vo_ref.at[head], vmet.at[last, head], v_s.at[last], v_r.at[last], a.sibling)
    copy.wait()
    vo_ref[head] += vmet[last, head]
    for copy in crossed.values():
        copy.wait_send()
    for copy in sent.values():
        copy.wait()


def leave(p, g, small, shared, size, ident):
    rows, width = p.shape[0] // size, p.shape[1]
    dma = pltpu.SemaphoreType.DMA
    hbm = pl.BlockSpec(memory_space=pl.ANY)
    vmem = pl.BlockSpec(memory_space=pltpu.VMEM)
    block = (size,) + g.shape[1:]
    steps = 2 + size // 2
    return pl.pallas_call(
        functools.partial(leave_kernel, size, shared),
        out_shape=(
            jax.ShapeDtypeStruct((rows, width), p.dtype),
            jax.ShapeDtypeStruct(block, g.dtype),
            jax.ShapeDtypeStruct(small.shape, small.dtype),
        ),
        in_specs=[hbm, hbm, vmem],
        out_specs=(vmem, vmem, vmem),
        scratch_shapes=[
            pltpu.VMEM(block, g.dtype),
            pltpu.VMEM(block, g.dtype),
            pltpu.VMEM((steps,) + small.shape, small.dtype),
            dma((size,)),
            dma((size,)),
            dma((size,)),
            dma((size,)),
            dma((size,)),
            dma((steps,)),
            dma((steps,)),
        ]
        + RingSum.scratch(size, False, rows, width, p.dtype),
        compiler_params=pltpu.CompilerParams(
            collective_id=ident, has_side_effects=True, vmem_limit_bytes=vmem_bytes
        ),
        name="leave_rows_and_weights",
    )(p, g, small)


def plain_enter(x, w):
    rows = lax.all_gather(x, "ctx", axis=0, tiled=True)
    mine = lax.all_to_all(w, "ctx", split_axis=0, concat_axis=0, tiled=True)
    return rows, lax.all_gather(mine, "seq", axis=0, tiled=True)


def plain_sum(p, axes):
    part = lax.psum_scatter(p, axes, scatter_dimension=0, tiled=True)
    return lax.psum(part, "tp")


def plain_leave(p, g, small, shared):
    kept = lax.psum_scatter(g, "seq", scatter_dimension=0, tiled=True)
    owned = lax.all_to_all(kept, "ctx", split_axis=0, concat_axis=0, tiled=True)
    small = jnp.concatenate([lax.psum(small[:shared], "tp"), small[shared:]])
    return plain_sum(p, "ctx"), owned, lax.psum(small, ("seq", "ctx"))


def expert_kernel(
    units, model, lead_ref, x_ref, dy_ref, wt_ref, bias_ref, wd_ref, bd_ref, pick_ref, place_ref,
    out_ref, back_ref, act_ref, dgu_ref, gbias_ref, dbias_ref,
):
    step = pl.program_id(0)
    tail = model // 128 * 128
    rows = x_ref.shape[0]
    x = x_ref[:, :model]
    dy = dy_ref[...]
    ends = x_ref[:, tail:]
    gate_row = across(pick_ref[...], ends)[:1]
    gate_col = across(ends, pick_ref[...])[:, :1]

    gate = clamp_limit * jnp.tanh((across(wt_ref[:units], x) + bias_ref[:units]) / clamp_limit)
    up = clamp_limit * jnp.tanh((across(wt_ref[units:], x) + bias_ref[units:]) / clamp_limit)
    squash = jax.nn.sigmoid(glu_alpha * gate)
    swish = gate * squash
    act = (up + 1.0) * swish
    out = down(act.astype(bf16), wd_ref[...]) + lead_ref[0, 0] * bd_ref[...]
    out_ref[...] = (gate_col * out).astype(bf16)

    act_grad = across(wd_ref[...], dy)
    high = bd_ref[...].astype(bf16)
    low = (bd_ref[...] - high.astype(f32)).astype(bf16)
    bias_dot = across(jnp.concatenate([high, low] + [jnp.zeros_like(high)] * 14, axis=0), dy)
    gate_grad = jnp.sum(act * act_grad, axis=0, keepdims=True) + lead_ref[0, 0] * (
        bias_dot[0:1] + bias_dot[1:2]
    )
    gate_grad = jnp.where(gate_row > 0, gate_grad, 0.0)
    act_grad = act_grad * gate_row
    slope = 1.0 - (gate / clamp_limit) * (gate / clamp_limit)
    dgate = (
        act_grad * (up + 1.0) * (squash + glu_alpha * swish * (1.0 - squash)) * slope
    ).astype(bf16)
    dup = (act_grad * swish * (1.0 - (up / clamp_limit) * (up / clamp_limit))).astype(bf16)
    act_ref[...] = (act * gate_row).astype(bf16)
    dgu_ref[:units] = dgate
    dgu_ref[units:] = dup

    back = down(dgate, wt_ref[:units]) + down(dup, wt_ref[units:])
    back_ref[:, :model] = back.astype(bf16)
    top = gate_grad.astype(bf16)
    rest = (gate_grad - top.astype(f32)).astype(bf16)
    sent = jnp.concatenate([top, rest] + [jnp.zeros_like(top)] * 14, axis=0)
    ends_out = down(sent, place_ref[...]).astype(bf16)
    back_ref[:, model:] = ends_out[:, model - tail :]

    @pl.when(step == 0)
    def _():
        gbias_ref[...] = jnp.zeros_like(gbias_ref)
        dbias_ref[...] = jnp.zeros_like(dbias_ref)

    gbias_ref[:units] += jnp.sum(dgate.astype(f32), axis=1, keepdims=True)
    gbias_ref[units:] += jnp.sum(dup.astype(f32), axis=1, keepdims=True)
    gate_high = gate_row.astype(bf16)
    gate_low = (gate_row - gate_high.astype(f32)).astype(bf16)
    gates = jnp.concatenate([gate_high, gate_low] + [jnp.zeros_like(gate_high)] * 14, axis=0)
    sums = jnp.dot(gates, dy, preferred_element_type=f32)
    dbias_ref[...] += sums[0:1] + sums[1:2]


def expert_rows(lead, x, dy, wt, bias, wd, bd, pick, place):
    count, wide = x.shape
    model = dy.shape[1]
    units = wd.shape[0]
    rows = min(256, count)
    tail = model // 128 * 128
    back_wide = tail + place.shape[1]
    row = lambda i: (i, 0)
    col = lambda i: (0, i)
    fixed = lambda i: (0, 0)
    whole = lambda v: pl.BlockSpec(v.shape, fixed)
    return pl.pallas_call(
        functools.partial(expert_kernel, units, model),
        grid=(count // rows,),
        out_shape=(
            jax.ShapeDtypeStruct((count, model), bf16),
            jax.ShapeDtypeStruct((count, back_wide), bf16),
            jax.ShapeDtypeStruct((units, count), bf16),
            jax.ShapeDtypeStruct((2 * units, count), bf16),
            jax.ShapeDtypeStruct((2 * units, 1), f32),
            jax.ShapeDtypeStruct((1, model), f32),
        ),
        in_specs=[
            pl.BlockSpec(memory_space=pltpu.SMEM),
            pl.BlockSpec((rows, wide), row),
            pl.BlockSpec((rows, model), row),
            whole(wt),
            whole(bias),
            whole(wd),
            whole(bd),
            whole(pick),
            whole(place),
        ],
        out_specs=(
            pl.BlockSpec((rows, model), row),
            pl.BlockSpec((rows, back_wide), row),
            pl.BlockSpec((units, rows), col),
            pl.BlockSpec((2 * units, rows), col),
            pl.BlockSpec((2 * units, 1), fixed),
            pl.BlockSpec((1, model), fixed),
        ),
        compiler_params=pltpu.CompilerParams(vmem_limit_bytes=vmem_bytes),
        name="expert_rows",
    )(lead, x, dy, wt, bias, wd, bd, pick, place)


def unit_order(size):
    order = [size // 2]
    for d in range(size // 2 - 1, 0, -1):
        order += [d, size - d]
    return order + [0]


def unit_slots(size):
    return {j: slot for slot, j in enumerate(unit_order(size))}


def expert_in_kernel(
    size, units, model, wide,
    x_ref, wt_ref, wd_ref, bias_ref, extra_ref, pick_ref,
    x_all, act_all, dgu_all, dg_ref, gbias_ref,
    xbuf, wt, wd, act_buf, dgu_buf,
    load_s, ring_s, ring_r, cross_s, cross_r, core_s, core_r, keep_s,
):
    a = Around(size)
    rows = x_ref.shape[0]
    half, chunk = rows // 2, rows // 4
    far, near = size // 2, size - 1 - size // 2
    items = [(1, 0, far, near), (0, 0, near, far), (0, 1, far, near)]
    slot_of = unit_slots(size)
    tail = model // 128 * 128

    loads = [
        pltpu.make_async_copy(wt_ref, wt, load_s.at[0]),
        pltpu.make_async_copy(wd_ref, wd.at[pl.ds(0, units)], load_s.at[1]),
    ]
    for copy in loads:
        copy.start()
    wd[units:] = extra_ref[...]
    gbias_ref[...] = jnp.zeros_like(gbias_ref)
    greet([a.right, a.left, a.sibling, a.across])

    def spot(j, other, core, piece):
        return xbuf.at[slot_of[j], pl.ds(other * rows + core * half + piece * chunk, chunk)]

    sent, ring, crossed, shared = [], {}, {}, {}

    def hop(item, way, k, src):
        piece, other, _, _ = items[item]
        j = size - (k + 1) if way == 0 else k + 1
        copy = remote(
            src, spot(j, other, 0, piece), ring_s.at[item, way, k], ring_r.at[item, way, k],
            a.right if way == 0 else a.left,
        )
        ring[item, way, k] = copy
        sent.append(copy)

    def cross(j, piece, src):
        at = slot_of[j] if piece else size
        copy = remote(src, spot(j, 1, 0, piece), cross_s.at[at], cross_r.at[at], a.across)
        crossed[j, piece] = copy
        sent.append(copy)

    def share(j, other, piece):
        at = (slot_of[j], other, piece)
        copy = remote(
            spot(j, other, 0, piece), spot(j, other, 1, piece), core_s.at[at], core_r.at[at], a.sibling
        )
        shared[j, other, piece] = copy
        sent.append(copy)

    def own(core, piece, count):
        return x_ref.at[rows_at(core * half + piece * chunk, count)]

    mine = [
        pltpu.make_async_copy(
            own(a.core if here == 0 else 1 - a.core, 0, half),
            xbuf.at[slot_of[0], pl.ds(here * half, half)],
            load_s.at[2 + here],
        )
        for here in range(2)
    ]
    for copy in mine:
        copy.start()
    cross(0, 0, own(a.core, 0, chunk))
    for item in range(2):
        for way in range(2):
            hop(item, way, 0, own(a.core, items[item][0], chunk))
    cross(0, 1, own(a.core, 1, chunk))

    def unit(slot, carry):
        x = xbuf[slot, :, :model]
        dy = xbuf[slot, :, wide : wide + model]
        ends = xbuf[slot, :, tail:wide]
        columns = pl.ds(pl.multiple_of(slot * 2 * rows, 2 * rows), 2 * rows)
        gate_row = across(pick_ref[...], ends)[:1]
        gate = clamp_limit * jnp.tanh((across(wt[:units], x) + bias_ref[:units]) / clamp_limit)
        up = clamp_limit * jnp.tanh((across(wt[units:], x) + bias_ref[units:]) / clamp_limit)
        squash = jax.nn.sigmoid(glu_alpha * gate)
        swish = gate * squash
        act = (up + 1.0) * swish
        act_grad = across(wd[...], dy)
        bias_dot = act_grad[units : units + 1] + act_grad[units + 1 : units + 2]
        act_grad = act_grad[:units]
        gate_grad = jnp.sum(act * act_grad, axis=0, keepdims=True) + bias_dot
        gate_grad = jnp.where(gate_row > 0, gate_grad, 0.0)
        act_grad = act_grad * gate_row
        slope = 1.0 - (gate / clamp_limit) * (gate / clamp_limit)
        dgate = (
            act_grad * (up + 1.0) * (squash + glu_alpha * swish * (1.0 - squash)) * slope
        ).astype(bf16)
        dup = (act_grad * swish * (1.0 - (up / clamp_limit) * (up / clamp_limit))).astype(bf16)
        dgu_buf[:units, columns] = dgate
        dgu_buf[units:, columns] = dup
        gbias_ref[:units] += jnp.sum(dgate.astype(f32), axis=1, keepdims=True)
        gbias_ref[units:] += jnp.sum(dup.astype(f32), axis=1, keepdims=True)
        high = gate_row.astype(bf16)
        low = (gate_row - high.astype(f32)).astype(bf16)
        act_buf[:units, columns] = (act * gate_row).astype(bf16)
        act_buf[units:, columns] = jnp.concatenate([high, high, low] + [jnp.zeros_like(high)] * 13, axis=0)
        top = gate_grad.astype(bf16)
        rest = (gate_grad - top.astype(f32)).astype(bf16)
        dg_ref[:, columns] = jnp.concatenate([top, rest] + [jnp.zeros_like(top)] * 14, axis=0)
        return carry

    kept = []

    def compute(js):
        for j in js:
            if j == 0:
                for copy in mine:
                    copy.wait()
            else:
                crossed[j, 1].wait_recv()
                share(j, 1, 1)
            for key in [(j, 0, 0), (j, 0, 1), (j, 1, 0), (j, 1, 1)]:
                if key in shared:
                    shared[key].wait_recv()
        slots = [slot_of[j] for j in js]
        lax.fori_loop(slots[0], slots[-1] + 1, unit, 0)
        for slot in slots:
            columns = pl.ds(slot * 2 * rows, 2 * rows)
            for at, (src, dst) in enumerate(
                (
                    (xbuf.at[slot], x_all.at[slot]),
                    (act_buf.at[:, columns], act_all.at[:, columns]),
                    (dgu_buf.at[:, columns], dgu_all.at[:, columns]),
                )
            ):
                copy = pltpu.make_async_copy(src, dst, keep_s.at[at, slot])
                copy.start()
                kept.append(copy)

    crossed[0, 0].wait_recv()
    for way in range(2):
        hop(2, way, 0, spot(0, 1, 0, 0))
    share(0, 1, 0)
    crossed[0, 1].wait_recv()
    share(0, 1, 1)
    for copy in loads:
        copy.wait()
    ready = [0]
    for k in range(size // 2):
        compute(ready)
        for item, (piece, other, right, left) in enumerate(items):
            for way, hops in ((0, right), (1, left)):
                if k >= hops:
                    continue
                ring[item, way, k].wait_recv()
                j = size - (k + 1) if way == 0 else k + 1
                if k + 1 < hops:
                    hop(item, way, k + 1, spot(j, other, 0, piece))
                if item == 0:
                    cross(j, 1, spot(j, 0, 0, 1))
                share(j, other, piece)
        ready = [k + 1] if 2 * (k + 1) == size else [k + 1, size - (k + 1)]
    compute(ready)
    for copy in sent:
        copy.wait_send()
    for copy in kept:
        copy.wait()


def expert_in(x, wt, wd, bias, extra, pick, model, wide, size, ident):
    rows, width = x.shape
    units = wd.shape[0]
    deep = units + extra.shape[0]
    count = 2 * size * rows
    dma = pltpu.SemaphoreType.DMA
    hbm = pl.BlockSpec(memory_space=pl.ANY)
    vmem = pl.BlockSpec(memory_space=pltpu.VMEM)
    return pl.pallas_call(
        functools.partial(expert_in_kernel, size, units, model, wide),
        out_shape=(
            jax.ShapeDtypeStruct((size, 2 * rows, width), bf16),
            jax.ShapeDtypeStruct((deep, count), bf16),
            jax.ShapeDtypeStruct((2 * units, count), bf16),
            jax.ShapeDtypeStruct((16, count), bf16),
            jax.ShapeDtypeStruct((2 * units, 1), f32),
        ),
        in_specs=[hbm, hbm, hbm, vmem, vmem, vmem],
        out_specs=(hbm, hbm, hbm, vmem, vmem),
        scratch_shapes=[
            pltpu.VMEM((size, 2 * rows, width), bf16),
            pltpu.VMEM((2 * units, model), bf16),
            pltpu.VMEM((deep, model), bf16),
            pltpu.VMEM((deep, count), bf16),
            pltpu.VMEM((2 * units, count), bf16),
            dma((4,)),
            dma((3, 2, size // 2)),
            dma((3, 2, size // 2)),
            dma((size + 1,)),
            dma((size + 1,)),
            dma((size, 2, 2)),
            dma((size, 2, 2)),
            dma((3, size)),
        ],
        compiler_params=pltpu.CompilerParams(
            collective_id=ident, has_side_effects=True, vmem_limit_bytes=vmem_most
        ),
        name="expert_in",
    )(x, wt, wd, bias, extra, pick)


def expert_out_kernel(
    size, rows, units, model, start, tiles, more, *refs,
):
    if more:
        lhs_ref, w_ref, x_ref, dg_ref, place_ref, o_ref, grad_ref, *refs = refs
    else:
        lhs_ref, w_ref, x_ref, extra_ref, o_ref, grad_ref, grad_extra, *refs = refs
    (
        lhs, w, x, acc, own, out, ringbuf, crossbuf, lastbuf, tile,
        load_s, ring_s, ring_r, cross_s, cross_r, core_s, core_r, out_s, out_r, tile_s,
    ) = refs
    a = Around(size)
    half, chunk = rows // 2, rows // 4
    far, near = size // 2, size - 1 - size // 2
    items = [(0, 1, far, near), (0, 0, near, far), (1, 0, far, near)]
    slot_of = unit_slots(size)
    tail = model // 128 * 128
    step_rows = units // tiles

    loads = [
        pltpu.make_async_copy(w_ref, w.at[pl.ds(0, units)], load_s.at[0]),
        pltpu.make_async_copy(lhs_ref, lhs, load_s.at[1]),
        pltpu.make_async_copy(
            x_ref.at[:, :, pl.ds(start, x.shape[2])], x, load_s.at[2]
        ),
    ]
    for copy in loads:
        copy.start()
    if not more:
        w[units:] = extra_ref[...]
    greet([a.right, a.left, a.sibling, a.across])
    for copy in loads[:2]:
        copy.wait()

    def handed(slot, other):
        return pltpu.make_async_remote_copy(
            src_ref=out.at[slot % 2, other],
            dst_ref=acc.at[other, slot],
            send_sem=core_s.at[other, slot],
            recv_sem=core_r.at[other, slot],
            device_id=a.sibling,
            device_id_type=pl.DeviceIdType.MESH,
        )

    def over(slot):
        return pltpu.make_async_remote_copy(
            src_ref=acc.at[1, slot, pl.ds(chunk, chunk)],
            dst_ref=crossbuf.at[slot],
            send_sem=cross_s.at[slot],
            recv_sem=cross_r.at[slot],
            device_id=a.across,
            device_id_type=pl.DeviceIdType.MESH,
        )

    def add(into, other):
        into[...] = (into[...].astype(f32) + other[...].astype(f32)).astype(bf16)

    def settle(slot):
        for other in range(2):
            handed(slot, other).wait_recv()
            add(acc.at[other, slot], own.at[slot % 2, other])
        over(slot).start()

    def produce(slot, carry):
        @pl.when(slot >= 2)
        def _():
            for other in range(2):
                handed(slot - 2, other).wait_send()

        columns = pl.ds(pl.multiple_of(slot * 2 * rows, 2 * rows), 2 * rows)
        y = down(lhs[:, columns], w[...])
        for other in range(2):
            for place, into in ((0, own), (half, out)):
                part = y[other * rows + place : other * rows + place + half]
                into[slot % 2, other, :, :model] = part.astype(bf16)
        if more:
            ends = down(dg_ref[:, columns], place_ref[...])[:, model - tail :].astype(bf16)
            for other in range(2):
                for place, into in ((0, own), (half, out)):
                    part = ends[other * rows + place : other * rows + place + half]
                    into[slot % 2, other, :, model:] = part
        for other in range(2):
            handed(slot, other).start()

        @pl.when(slot >= 1)
        def _():
            settle(slot - 1)

        return carry

    def tile_copy(i):
        return pltpu.make_async_copy(
            tile.at[i % 2], grad_ref.at[pl.ds(pl.multiple_of(i * step_rows, 16), step_rows)], tile_s.at[i % 2]
        )

    def weight_grad(i, carry):
        @pl.when(i >= 2)
        def _():
            tile_copy(i - 2).wait()

        left = lhs[pl.ds(pl.multiple_of(i * step_rows, 16), step_rows)]
        total = None
        for at in range(size):
            piece = jnp.dot(
                left[:, at * 2 * rows : (at + 1) * 2 * rows], x[at, :, :model], preferred_element_type=f32
            )
            total = piece if total is None else total + piece
        tile[i % 2] = total
        tile_copy(i).start()
        return carry

    ring, sent = {}, []

    def part(other, j, piece):
        return acc.at[other, slot_of[j], pl.ds(piece * chunk, chunk)]

    joined = set()

    def join(j):
        if j not in joined:
            joined.add(j)
            over(slot_of[j]).wait_recv()
            add(part(0, j, 1), crossbuf.at[slot_of[j]])

    def step(k):
        for item, (piece, other, right, left) in enumerate(items):
            for way, hops in ((0, right), (1, left)):
                d = hops - k
                if d < 1:
                    continue
                j = d if way == 0 else size - d
                if piece == 1:
                    join(j)
                block = part(other, j, piece)
                if k > 0:
                    ring[item, way, d].wait_recv()
                    add(block, ringbuf.at[item, way, d])
                copy = remote(
                    block, ringbuf.at[item, way, d - 1], ring_s.at[item, way, d - 1],
                    ring_r.at[item, way, d - 1], a.right if way == 0 else a.left,
                )
                ring[item, way, d - 1] = copy
                sent.append(copy)

    made, graded = [0], [0]

    def make(upto):
        lax.fori_loop(made[0], upto, produce, 0)
        made[0] = upto

    def grade(count):
        upto = min(tiles, graded[0] + count)
        if upto > graded[0]:
            lax.fori_loop(graded[0], upto, weight_grad, 0)
            graded[0] = upto

    steps = size // 2
    per = -(-tiles // steps)
    make(4)
    step(0)
    make(min(6, size))
    loads[2].wait()
    for k in range(1, steps):
        upto = min(size, 4 + 2 * (k + 1))
        if k > 1 and made[0] < upto:
            make(upto)
        if k == steps - 1:
            settle(size - 1)
        if k == 1 and steps > 2:
            grade(per)
            step(k)
            make(min(size, 8))
            continue
        grade(per)
        step(k)
    grade(tiles)

    last = []
    for item, (piece, other, _, _) in enumerate(items):
        if piece == 1:
            join(0)
        block = part(other, 0, piece)
        for way in range(2):
            ring[item, way, 0].wait_recv()
            add(block, ringbuf.at[item, way, 0])
        if other:
            final = remote(block, lastbuf, cross_s.at[size], cross_r.at[size], a.across)
            sent.append(final)
        else:
            last.append((piece, block))
    outs = []
    for piece, block in sorted(last, key=lambda entry: -entry[0]):
        if piece == 0:
            final.wait_recv()
            add(block, lastbuf)
        where = o_ref.at[rows_at(a.core * half + piece * chunk, chunk)]
        where[...] = block[...]
        outs.append(remote(where, where, out_s.at[piece], out_r.at[piece], a.sibling))
    if not more:
        left = lhs[pl.ds(units, lhs.shape[0] - units)]
        total = None
        for at in range(size):
            piece = jnp.dot(
                left[:, at * 2 * rows : (at + 1) * 2 * rows], x[at, :, :model], preferred_element_type=f32
            )
            total = piece if total is None else total + piece
        grad_extra[...] = total
    for copy in outs:
        copy.wait()
    for copy in sent:
        copy.wait_send()
    for slot in range(size):
        over(slot).wait_send()
    for slot in range(size - 2, size):
        for other in range(2):
            handed(slot, other).wait_send()
    for i in range(max(0, tiles - 2), tiles):
        tile_copy(i).wait()


def expert_out(lhs, w, x, start, tiles, size, ident, dg=None, place=None, extra=None):
    units, model = w.shape
    rows = x.shape[1] // 2
    half, chunk = rows // 2, rows // 4
    more = dg is not None
    padded = -(-model // 128) * 128
    width = model // 128 * 128 + place.shape[1] if more else model
    dma = pltpu.SemaphoreType.DMA
    hbm = pl.BlockSpec(memory_space=pl.ANY)
    vmem = pl.BlockSpec(memory_space=pltpu.VMEM)
    shapes = [
        jax.ShapeDtypeStruct((rows, width), bf16),
        jax.ShapeDtypeStruct((units, model), f32),
    ]
    if not more:
        shapes.append(jax.ShapeDtypeStruct((extra.shape[0], model), f32))
    return pl.pallas_call(
        functools.partial(expert_out_kernel, size, rows, units, model, start, tiles, more),
        out_shape=shapes,
        in_specs=[hbm, hbm, hbm] + [vmem] * (2 if more else 1),
        out_specs=[vmem, hbm] + ([] if more else [vmem]),
        scratch_shapes=[
            pltpu.VMEM(lhs.shape, bf16),
            pltpu.VMEM((lhs.shape[0], model), bf16),
            pltpu.VMEM((size, 2 * rows, padded), bf16),
            pltpu.VMEM((2, size, half, width), bf16),
            pltpu.VMEM((2, 2, half, width), bf16),
            pltpu.VMEM((2, 2, half, width), bf16),
            pltpu.VMEM((3, 2, size // 2, chunk, width), bf16),
            pltpu.VMEM((size, chunk, width), bf16),
            pltpu.VMEM((chunk, width), bf16),
            pltpu.VMEM((2, units // tiles, model), f32),
            dma((3,)),
            dma((3, 2, size // 2)),
            dma((3, 2, size // 2)),
            dma((size + 1,)),
            dma((size + 1,)),
            dma((2, size)),
            dma((2, size)),
            dma((2,)),
            dma((2,)),
            dma((2,)),
        ],
        compiler_params=pltpu.CompilerParams(
            collective_id=ident, has_side_effects=True, vmem_limit_bytes=vmem_most
        ),
        name="expert_back" if more else "expert_out",
    )(lhs, w, x, *((dg, place) if more else (extra,)))


def turn(x, cosine, sine):
    half = HEAD_DIMENSION // 2
    width = x.shape[-1]
    if width % 128:
        starts = [start for at in range(0, width, 2 * half) for start in (at + half, at)]
        swapped = jnp.concatenate([x[:, start : start + half] for start in starts], axis=1)
    else:
        lane = lax.broadcasted_iota(jnp.int32, x.shape, 1)
        swapped = jnp.where(
            lane % HEAD_DIMENSION < half, pltpu.roll(x, width - half, 1), pltpu.roll(x, half, 1)
        )
    return x * cosine + swapped * sine


def spread(table, width):
    pieces = [table] * (width // 128) + ([table[:, : width % 128]] if width % 128 else [])
    return jnp.concatenate(pieces, axis=1) if len(pieces) > 1 else pieces[0]


def project_kernel(heads, x_ref, w_ref, b_ref, cos_ref, sin_ref, q_ref, k_ref, v_ref):
    width = heads * HEAD_DIMENSION
    y = jnp.dot(x_ref[...], w_ref[...], preferred_element_type=f32) + b_ref[...]
    cosine, sine = cos_ref[...], sin_ref[...]
    pad = 128
    q_ref[...] = turn(y[:, :width], spread(cosine, width), spread(sine, width)).astype(bf16)
    kv = y[:, width : width + pad]
    k_ref[...] = turn(kv, cosine, sine)[:, :HEAD_DIMENSION].astype(bf16)
    v_ref[...] = kv[:, HEAD_DIMENSION:].astype(bf16)


def project(x, w, bias, cosine, sine, heads):
    length, model = x.shape
    rows = min(256, length)
    width = heads * HEAD_DIMENSION
    row = lambda i: (i, 0)
    fixed = lambda i: (0, 0)
    return pl.pallas_call(
        functools.partial(project_kernel, heads),
        grid=(length // rows,),
        out_shape=(
            jax.ShapeDtypeStruct((length, width), bf16),
            jax.ShapeDtypeStruct((length, HEAD_DIMENSION), bf16),
            jax.ShapeDtypeStruct((length, HEAD_DIMENSION), bf16),
        ),
        in_specs=[
            pl.BlockSpec((rows, model), row),
            pl.BlockSpec(w.shape, fixed),
            pl.BlockSpec(bias.shape, fixed),
            pl.BlockSpec((rows, 128), row),
            pl.BlockSpec((rows, 128), row),
        ],
        out_specs=(
            pl.BlockSpec((rows, width), row),
            pl.BlockSpec((rows, HEAD_DIMENSION), row),
            pl.BlockSpec((rows, HEAD_DIMENSION), row),
        ),
        compiler_params=pltpu.CompilerParams(vmem_limit_bytes=vmem_bytes),
        name="project_rows",
    )(x, w, bias, cosine, sine)


def each_reach(block, rows, length, run):
    classes = min(4, length // rows)
    per = length // rows // classes
    for level in range(classes):
        pl.when(block // per == level)(functools.partial(run, (level + 1) * per * rows))


def attend_kernel(heads, length, sink_ref, q_ref, k_ref, v_ref, w_ref, o_ref, low_ref, lse_ref, p_ref):
    rows = q_ref.shape[0]
    block = pl.program_id(0)
    scale = 1.0 / math.sqrt(HEAD_DIMENSION)

    def run(reach):
        keys, values = k_ref[:reach], v_ref[:reach]
        row = block * rows + lax.broadcasted_iota(jnp.int32, (rows, reach), 0)
        allowed = lax.broadcasted_iota(jnp.int32, (rows, reach), 1) <= row
        outs, totals = [], []
        for head in range(heads):
            query = q_ref[:, head * HEAD_DIMENSION : (head + 1) * HEAD_DIMENSION]
            scores = jnp.where(allowed, across(query, keys) * scale, masked_score)
            sink = sink_ref[0, head]
            top = jnp.maximum(jnp.max(scores, axis=1, keepdims=True), sink)
            weights = jnp.exp(scores - top)
            total = jnp.sum(weights, axis=1, keepdims=True) + jnp.exp(sink - top)
            mixed = jnp.dot(weights.astype(bf16), values, preferred_element_type=f32)
            outs.append(mixed / total)
            totals.append(top + jnp.log(total))
        joined = jnp.concatenate(outs, axis=1)
        o_ref[...] = joined
        joined_low = joined.astype(bf16)
        low_ref[...] = joined_low
        p_ref[...] = across(joined_low, w_ref[...]).astype(bf16)
        lse_ref[...] = jnp.concatenate(totals, axis=1)

    each_reach(block, rows, length, run)


def attend(sinks, q, k, v, w):
    length, width = q.shape
    model = w.shape[0]
    heads = width // HEAD_DIMENSION
    rows = min(256, length)
    row = lambda i: (i, 0)
    fixed = lambda i: (0, 0)
    return pl.pallas_call(
        functools.partial(attend_kernel, heads, length),
        grid=(length // rows,),
        out_shape=(
            jax.ShapeDtypeStruct((length, width), f32),
            jax.ShapeDtypeStruct((length, width), bf16),
            jax.ShapeDtypeStruct((length, heads), f32),
            jax.ShapeDtypeStruct((length, model), bf16),
        ),
        in_specs=[
            pl.BlockSpec(memory_space=pltpu.SMEM),
            pl.BlockSpec((rows, width), row),
            pl.BlockSpec(k.shape, fixed),
            pl.BlockSpec(v.shape, fixed),
            pl.BlockSpec(w.shape, fixed),
        ],
        out_specs=(
            pl.BlockSpec((rows, width), row),
            pl.BlockSpec((rows, width), row),
            pl.BlockSpec((rows, heads), row),
            pl.BlockSpec((rows, model), row),
        ),
        compiler_params=pltpu.CompilerParams(vmem_limit_bytes=vmem_bytes),
        name="attend_rows",
    )(sinks, q, k, v, w)


def spread_kernel(x_ref, w_ref, o_ref):
    o_ref[...] = across(x_ref[...], w_ref[...]).astype(o_ref.dtype)


def spread_rows(x, w):
    count, width = x.shape
    rows = min(256, count)
    return pl.pallas_call(
        spread_kernel,
        grid=(count // rows,),
        out_shape=jax.ShapeDtypeStruct((count, w.shape[0]), bf16),
        in_specs=[
            pl.BlockSpec((rows, width), lambda i: (i, 0)),
            pl.BlockSpec(w.shape, lambda i: (0, 0)),
        ],
        out_specs=pl.BlockSpec((rows, w.shape[0]), lambda i: (i, 0)),
        compiler_params=pltpu.CompilerParams(vmem_limit_bytes=vmem_bytes),
        name="spread_rows",
    )(x, w)


def attend_back_kernel(
    heads, length, sink_ref, q_ref, k_ref, v_ref, o_ref, lse_ref, do_ref, cos_ref, sin_ref,
    kcos_ref, ksin_ref, dq_ref, dkv_ref, dsink_ref, dk_acc, dv_acc, sink_acc,
):
    rows = q_ref.shape[0]
    block = pl.program_id(0)
    scale = 1.0 / math.sqrt(HEAD_DIMENSION)

    @pl.when(block == 0)
    def _():
        dk_acc[...] = jnp.zeros_like(dk_acc)
        dv_acc[...] = jnp.zeros_like(dv_acc)
        sink_acc[...] = jnp.zeros_like(sink_acc)

    def run(reach):
        keys, values = k_ref[:reach], v_ref[:reach]
        row = block * rows + lax.broadcasted_iota(jnp.int32, (rows, reach), 0)
        allowed = lax.broadcasted_iota(jnp.int32, (rows, reach), 1) <= row
        parts, sink_parts = [], []
        key_sum = jnp.zeros((reach, HEAD_DIMENSION), f32)
        value_sum = jnp.zeros((reach, HEAD_DIMENSION), f32)
        for head in range(heads):
            span = slice(head * HEAD_DIMENSION, (head + 1) * HEAD_DIMENSION)
            query, grad = q_ref[:, span], do_ref[:, span]
            lse = lse_ref[:, head : head + 1]
            delta = jnp.sum(grad.astype(f32) * o_ref[:, span], axis=1, keepdims=True)
            scores = jnp.where(allowed, across(query, keys) * scale, masked_score)
            probs = jnp.exp(scores - lse)
            value_sum = value_sum + down(probs.astype(bf16), grad)
            score_grad = (probs * (across(grad, values) - delta)).astype(bf16)
            parts.append(jnp.dot(score_grad, keys, preferred_element_type=f32) * scale)
            key_sum = key_sum + down(score_grad, query)
            share = jnp.exp(sink_ref[0, head] - lse) * delta
            sink_parts.append(jnp.sum(share, axis=0, keepdims=True))
        dq = jnp.concatenate(parts, axis=1)
        wide = dq.shape[1]
        dq_ref[...] = turn(dq, spread(cos_ref[...], wide), -spread(sin_ref[...], wide)).astype(bf16)
        dk_acc[:reach] += key_sum * scale
        dv_acc[:reach] += value_sum
        sink_acc[...] -= jnp.concatenate(sink_parts, axis=1)

    each_reach(block, rows, length, run)

    @pl.when(block == pl.num_programs(0) - 1)
    def _():
        both = jnp.concatenate([dk_acc[...], dv_acc[...]], axis=1)
        turned = turn(both, kcos_ref[...], -ksin_ref[...])
        lane = lax.broadcasted_iota(jnp.int32, both.shape, 1)
        dkv_ref[...] = jnp.where(lane < HEAD_DIMENSION, turned, both).astype(bf16)
        dsink_ref[...] = sink_acc[...]


def attend_back(sinks, q, k, v, o, lse, do, cosine, sine):
    length, width = q.shape
    heads = width // HEAD_DIMENSION
    rows = min(256, length)
    row = lambda i: (i, 0)
    fixed = lambda i: (0, 0)
    return pl.pallas_call(
        functools.partial(attend_back_kernel, heads, length),
        grid=(length // rows,),
        out_shape=(
            jax.ShapeDtypeStruct((length, width), bf16),
            jax.ShapeDtypeStruct((length, 2 * HEAD_DIMENSION), bf16),
            jax.ShapeDtypeStruct((1, heads), f32),
        ),
        in_specs=[
            pl.BlockSpec(memory_space=pltpu.SMEM),
            pl.BlockSpec((rows, width), row),
            pl.BlockSpec(k.shape, fixed),
            pl.BlockSpec(v.shape, fixed),
            pl.BlockSpec((rows, width), row),
            pl.BlockSpec((rows, heads), row),
            pl.BlockSpec((rows, width), row),
            pl.BlockSpec((rows, 128), row),
            pl.BlockSpec((rows, 128), row),
            pl.BlockSpec((length, 128), fixed),
            pl.BlockSpec((length, 128), fixed),
        ],
        out_specs=(
            pl.BlockSpec((rows, width), row),
            pl.BlockSpec((length, 2 * HEAD_DIMENSION), fixed),
            pl.BlockSpec((1, heads), fixed),
        ),
        scratch_shapes=[
            pltpu.VMEM((length, HEAD_DIMENSION), f32),
            pltpu.VMEM((length, HEAD_DIMENSION), f32),
            pltpu.VMEM((1, heads), f32),
        ],
        compiler_params=pltpu.CompilerParams(vmem_limit_bytes=vmem_bytes),
        name="attend_rows_back",
    )(sinks, q, k, v, o, lse, do, cosine, sine, cosine, sine)


def rms_norm(row_block, gain_vec):
    return (
        row_block
        * lax.rsqrt(jnp.mean(row_block * row_block, axis=-1, keepdims=True) + rms_eps)
        * gain_vec
    )


def rotary(length):
    half_size = HEAD_DIMENSION // 2
    frequency = rope_base ** (-2.0 * jnp.arange(half_size, dtype=f32) / HEAD_DIMENSION)
    angles = jnp.arange(length, dtype=f32)[:, None] * frequency[None, :]
    cosine, sine = jnp.cos(angles), jnp.sin(angles)
    return (
        jnp.concatenate([cosine] * 4, axis=1),
        jnp.concatenate([-sine, sine, -sine, sine], axis=1),
    )


def project_grad(left, right):
    return lax.dot_general(left, right, (((0,), (0,)), ((), ())), preferred_element_type=f32)


def on_device(
    tokens,
    gain_attn,
    w_query,
    b_query,
    key_value_weight,
    key_value_bias,
    sinks,
    w_out,
    b_out,
    gain_moe,
    w_router,
    b_router,
    routes,
    w_gate_up,
    b_gate_up,
    w_down,
    b_down,
    cotangent,
):
    tok_rows, model = tokens.shape
    ctx_size, ctx_rank = lax.axis_size("ctx"), lax.axis_index("ctx")
    seq_size, seq_rank = lax.axis_size("seq"), lax.axis_index("seq")
    tp_size, tp_rank = lax.axis_size("tp"), lax.axis_index("tp")
    local_heads = sinks.shape[0]
    kv_width = key_value_weight.shape[2]
    kv_heads = kv_width // HEAD_DIMENSION
    group = local_heads // kv_heads
    heads = local_heads // ctx_size
    width = heads * HEAD_DIMENSION
    experts = w_router.shape[1]
    weight_rows = w_query.shape[0]
    padded_rows = -(-weight_rows // 16) * 16
    length = ctx_size * tok_rows
    blocks = seq_size * ctx_size
    kernels = (
        seq_size == 2 and tp_size == 2 and tok_rows % 64 == 0
        and 3 * blocks * tok_rows * model * 2 <= vmem_bytes
    )

    kv_of = [(index * heads) // group for index in range(ctx_size)]
    kv_mine = (ctx_rank * heads) // group

    kv_split = key_value_weight.reshape(weight_rows, 2, kv_heads, HEAD_DIMENSION)
    send = []
    for index in range(ctx_size):
        cols = slice(index * width, (index + 1) * width)
        send.append(
            jnp.concatenate(
                [
                    w_query[:, cols],
                    kv_split[:, 0, kv_of[index]],
                    kv_split[:, 1, kv_of[index]],
                    w_out[cols].T,
                ],
                axis=1,
            )
        )
    send = jnp.pad(jnp.stack(send), ((0, 0), (0, padded_rows - weight_rows), (0, 0)))

    residual = tokens.astype(f32)
    normed_attn, attn_norm_back = jax.vjp(rms_norm, residual, gain_attn)
    normed_low = normed_attn.astype(bf16)
    if kernels:
        rows_all, weights = enter(normed_low, send, ctx_size, 1)
    else:
        rows_all, weights = plain_enter(normed_low, send)
    weights = weights[:, :weight_rows].reshape(model, 2 * width + 2 * HEAD_DIMENSION)
    proj_width = width + 2 * HEAD_DIMENSION
    w_in, w_back = weights[:, :proj_width], weights[:, proj_width:]

    cosine, sine = rotary(length)
    bias = jnp.concatenate(
        [
            lax.dynamic_slice_in_dim(b_query, ctx_rank * width, width),
            lax.dynamic_slice_in_dim(key_value_bias[0], kv_mine * HEAD_DIMENSION, HEAD_DIMENSION),
            lax.dynamic_slice_in_dim(key_value_bias[1], kv_mine * HEAD_DIMENSION, HEAD_DIMENSION),
        ]
    )[None]
    sinks_mine = lax.dynamic_slice_in_dim(sinks, ctx_rank * heads, heads)[None]
    query, keys, values = project(rows_all, w_in, bias, cosine, sine, heads)
    attended, attended_low, log_total, out_part = attend(sinks_mine, query, keys, values, w_back)
    attn_out = ring_sum(out_part, ctx_size, False, 2) if kernels else plain_sum(out_part, "ctx")
    hidden = residual + attn_out.astype(f32) + b_out

    normed_moe, moe_norm_back = jax.vjp(rms_norm, hidden, gain_moe)
    moe_input = normed_moe.astype(bf16)
    logits = jnp.dot(moe_input, w_router, preferred_element_type=f32) + b_router
    onehot = (routes[..., None] == jnp.arange(experts, dtype=jnp.int32)).astype(f32)
    chosen = jnp.sum(onehot * logits[:, None, :], axis=-1)
    gates = jax.nn.softmax(chosen, axis=-1)
    gate_table = jnp.sum(onehot * gates[..., None], axis=1)
    gate_high = lax.reduce_precision(gate_table, 8, 7)
    gate_low = (gate_table - gate_high).astype(bf16)
    wide = -(-(model + 2 * experts) // 128) * 128
    payload = jnp.concatenate(
        [moe_input, gate_high.astype(bf16), gate_low, jnp.zeros((tok_rows, wide - model - 2 * experts), bf16)],
        axis=1,
    )

    gate_up_rows = jnp.transpose(w_gate_up[0], (1, 2, 0)).reshape(-1, model)
    down_weight = w_down[0]
    units = down_weight.shape[0]
    splits = seq_size * tp_size
    lead = ((seq_rank == 0) & (tp_rank == 0)).astype(f32).reshape(1, 1)
    tail = model // 128 * 128
    at = jnp.arange(wide - tail)[None] + tail - model
    pick = ((at == ctx_rank) | (at == experts + ctx_rank)).astype(bf16)
    pick = jnp.concatenate([pick, jnp.zeros((15, wide - tail), bf16)])
    back_wide = -(-(model + 2 * splits * experts) // 128) * 128
    column = 2 * (ctx_rank * splits + seq_rank * tp_size + tp_rank)
    at = jnp.arange(back_wide - tail)[None] + tail - model
    place = jnp.concatenate([at == column, at == column + 1]).astype(bf16)
    place = jnp.concatenate([place, jnp.zeros((14, back_wide - tail), bf16)])

    def expert(rows, upstream):
        return expert_rows(
            lead, rows, upstream, gate_up_rows, b_gate_up[0].reshape(-1, 1), down_weight, b_down, pick, place
        )

    def weight_grads(rows, upstream, gated_act, proj_grad):
        return (
            jnp.dot(proj_grad, rows[:, :model], preferred_element_type=f32),
            jnp.dot(gated_act, upstream, preferred_element_type=f32),
        )

    if kernels:
        dy_wide = -(-model // 128) * 128
        payload = jnp.concatenate([payload, jnp.pad(cotangent, ((0, 0), (0, dy_wide - model)))], axis=1)
        bias_high = lax.reduce_precision(lead * b_down, 8, 7)
        bias_low = lead * b_down - bias_high
        extra_rows = jnp.concatenate([bias_high, bias_low, bias_high, jnp.zeros((13, model), f32)]).astype(bf16)
        rows_all_units, gated_act, proj_grad, dg_rows, gate_bias = expert_in(
            payload, gate_up_rows, down_weight, b_gate_up[0].reshape(-1, 1), extra_rows, pick,
            model, wide, ctx_size, 3,
        )
        back_rows, gate_up_grad = expert_out(
            proj_grad, gate_up_rows, rows_all_units, 0, 5, ctx_size, 4, dg=dg_rows, place=place
        )
        expert_out_sum, down_grad, down_extra = expert_out(
            gated_act, down_weight, rows_all_units, wide, 3, ctx_size, 5, extra=extra_rows
        )
        down_bias = down_extra[0:1] + down_extra[2:3]
    else:
        pieces = blocks * tok_rows // math.gcd(blocks * tok_rows, 2048)

        def one_piece(total, packed):
            rows, upstream = (
                lax.all_gather(part, ("seq", "ctx"), axis=0, tiled=True) for part in packed
            )
            expert_part, back_part, gated_act, proj_grad, gate_bias, down_bias = expert(rows, upstream)
            more = weight_grads(rows, upstream, gated_act, proj_grad) + (gate_bias, down_bias)
            total = jax.tree.map(jnp.add, total, more)
            return total, (plain_sum(expert_part, ("seq", "ctx")), plain_sum(back_part, ("seq", "ctx")))

        start = tuple(
            jnp.zeros(shape, f32) for shape in ((2 * units, model), (units, model), (2 * units, 1), (1, model))
        )
        cut = lambda v: v.reshape(pieces, tok_rows // pieces, v.shape[1])
        total, (expert_out_sum, back_rows) = lax.scan(one_piece, start, (cut(payload), cut(cotangent)))
        gate_up_grad, down_grad, gate_bias, down_bias = total
        expert_out_sum, back_rows = (part.reshape(tok_rows, -1) for part in (expert_out_sum, back_rows))
    grad_w_gate_up = jnp.transpose(gate_up_grad.reshape(2, units, model), (2, 0, 1))[None]
    grad_b_gate_up = gate_bias.reshape(1, 2, units)
    grad_w_down = down_grad[None]
    grad_b_down = down_bias
    mixed = (hidden + expert_out_sum.astype(f32)).astype(bf16)

    upstream = cotangent.astype(f32)
    gate_grad = back_rows[:, model : model + 2 * splits * experts].astype(f32)
    gate_grad = jnp.sum(gate_grad.reshape(tok_rows, experts, 2 * splits), axis=-1)
    gate_grad = jnp.sum(onehot * gate_grad[:, None], axis=-1)
    chosen_grad = gates * (gate_grad - jnp.sum(gates * gate_grad, axis=1, keepdims=True))
    logit_grad = jnp.sum(onehot * chosen_grad[..., None], axis=1).astype(bf16)
    grad_w_router = project_grad(moe_input, logit_grad)
    grad_b_router = jnp.sum(logit_grad, axis=0, dtype=f32)
    moe_grad = back_rows[:, :model].astype(f32) + across(logit_grad, w_router)
    hidden_norm_grad, grad_gain_moe = moe_norm_back(moe_grad)
    hidden_grad = upstream + hidden_norm_grad
    branch_grad = hidden_grad.astype(bf16)
    grad_b_out = jnp.sum(branch_grad, axis=0, dtype=f32)
    if kernels:
        branch_all = ring_gather(branch_grad, ctx_size, 6)
    else:
        branch_all = lax.all_gather(branch_grad, "ctx", axis=0, tiled=True)

    out_grad = jnp.dot(branch_all, w_back, preferred_element_type=f32).astype(bf16)
    dq, dkv, dsinks = attend_back(
        sinks_mine, query, keys, values, attended, log_total, out_grad, cosine, sine
    )
    both = jnp.concatenate([dq, dkv], axis=1)
    input_rows = spread_rows(both, w_in)
    grad_in = project_grad(rows_all, both)
    grad_out = project_grad(branch_all, attended_low)
    gain_part = jnp.sum(grad_in * w_in.astype(f32), axis=1) / gain_attn
    grads = jnp.concatenate([grad_in, grad_out], axis=1).astype(bf16).reshape(blocks, weight_rows, -1)
    grads = jnp.pad(grads, ((0, 0), (0, padded_rows - weight_rows), (0, 0)))

    sum_q = jnp.sum(dq, axis=0, dtype=f32)
    sum_kv = jnp.sum(dkv, axis=0, dtype=f32).reshape(2, HEAD_DIMENSION)
    at_q = lax.dynamic_update_slice_in_dim(jnp.zeros_like(b_query), sum_q, ctx_rank * width, 0)
    at_kv = lax.dynamic_update_slice_in_dim(
        jnp.zeros_like(key_value_bias), sum_kv, kv_mine * HEAD_DIMENSION, 1
    )
    at_sinks = lax.dynamic_update_slice_in_dim(jnp.zeros_like(sinks), dsinks[0], ctx_rank * heads, 0)
    parts = (gain_part, grad_gain_moe, grad_b_out, grad_w_router, grad_b_router, at_q, at_kv, at_sinks)
    packed, starts = [], []
    for part in parts:
        flat = part.reshape(-1)
        starts.append(sum(piece.shape[0] for piece in packed))
        packed.append(jnp.pad(flat, (0, -flat.shape[0] % 1024)))
    shared = packed[0].shape[0] // 128
    small = jnp.concatenate(packed).reshape(-1, 128)
    if kernels:
        normed_grad, owned, small = leave(input_rows, grads, small, shared, ctx_size, 7)
    else:
        normed_grad, owned, small = plain_leave(input_rows, grads, small, shared)
    small = small.reshape(-1)
    sums = [
        small[start : start + part.size].reshape(part.shape) for start, part in zip(starts, parts)
    ]
    tokens_norm_grad, _ = attn_norm_back(normed_grad.astype(f32))
    grad_tokens = (hidden_grad + tokens_norm_grad).astype(bf16)

    owned = owned[:, :weight_rows].astype(f32)
    grad_w_query = jnp.transpose(owned[:, :, :width], (1, 0, 2)).reshape(weight_rows, -1)
    grad_kv = owned[:, :, width:proj_width].reshape(kv_heads, -1, weight_rows, 2, HEAD_DIMENSION)
    grad_w_key_value = jnp.transpose(jnp.sum(grad_kv, axis=1), (1, 2, 0, 3)).reshape(
        weight_rows, 2, kv_width
    )
    grad_w_out = jnp.transpose(owned[:, :, proj_width:], (0, 2, 1)).reshape(-1, weight_rows)

    return (
        mixed,
        grad_tokens,
        sums[0],
        grad_w_query,
        sums[5],
        grad_w_key_value,
        sums[6],
        sums[7],
        grad_w_out,
        sums[2],
        sums[1],
        sums[3],
        sums[4],
        grad_w_gate_up,
        grad_b_gate_up,
        grad_w_down,
        grad_b_down,
    )


def solution(mesh):
    in_specs = (
        P(("seq", "ctx"), None),
        P(),
        P(("seq", "ctx"), "tp"),
        P("tp"),
        P(("seq", "ctx"), None, "tp"),
        P(None, "tp"),
        P("tp"),
        P("tp", ("seq", "ctx")),
        P(),
        P(),
        P(),
        P(),
        P(("seq", "ctx"), None),
        P("ctx", None, None, ("seq", "tp")),
        P("ctx", None, ("seq", "tp")),
        P("ctx", ("seq", "tp"), None),
        P("ctx", None),
        P(("seq", "ctx"), None),
    )
    out_specs = (
        P(("seq", "ctx"), None),
        P(("seq", "ctx"), None),
        P(),
        P(("seq", "ctx"), "tp"),
        P("tp"),
        P(("seq", "ctx"), None, "tp"),
        P(None, "tp"),
        P("tp"),
        P("tp", ("seq", "ctx")),
        P(),
        P(),
        P(),
        P(),
        P("ctx", None, None, ("seq", "tp")),
        P("ctx", None, ("seq", "tp")),
        P("ctx", ("seq", "tp"), None),
        P("ctx", None),
    )
    return jax.shard_map(
        on_device, mesh=mesh, in_specs=in_specs, out_specs=out_specs, check_vma=False
    )
```

```python
import functools
import math

import jax
import jax.numpy as jnp
import numpy as np
from jax import lax
from jax.experimental import pallas as pl
from jax.experimental.pallas import tpu as pltpu
from jax.sharding import PartitionSpec as P

HEAD_DIMENSION = 64

rms_eps = 1e-05
rope_base = 150000.0
clamp_limit = 7.0
glu_alpha = 1.702
masked_score = -1e30
vmem_bytes = 56 * 1024 * 1024
vmem_most = 63 * 1024 * 1024
bf16 = jnp.bfloat16
f32 = jnp.float32


def across(left, right):
    return lax.dot_general(left, right, (((1,), (1,)), ((), ())), preferred_element_type=f32)


def down(left, right):
    return lax.dot_general(left, right, (((0,), (0,)), ((), ())), preferred_element_type=f32)


def ring_place(index, size):
    half = index // 2
    return jnp.where(index % 2 == 0, half, size - 1 - half)


def ring_index(place, size):
    place = lax.rem(place + size, size)
    return jnp.where(place < size // 2, 2 * place, 2 * (size - 1 - place) + 1)


def greet(devices):
    barrier = pltpu.get_barrier_semaphore()
    for device in devices:
        pl.semaphore_signal(barrier, inc=1, device_id=device, device_id_type=pl.DeviceIdType.MESH)
    pl.semaphore_wait(barrier, len(devices))


def remote(src, dst, send_sem, recv_sem, device):
    copy = pltpu.make_async_remote_copy(
        src_ref=src,
        dst_ref=dst,
        send_sem=send_sem,
        recv_sem=recv_sem,
        device_id=device,
        device_id_type=pl.DeviceIdType.MESH,
    )
    copy.start()
    return copy


def rows_at(start, count):
    return pl.ds(pl.multiple_of(start, count), count)


class Around:
    def __init__(self, size):
        self.size = size
        self.seq = lax.axis_index("seq")
        self.ctx = lax.axis_index("ctx")
        self.core = lax.axis_index("tp")
        self.place = ring_place(self.ctx, size)
        self.right = (self.seq, ring_index(self.place + 1, size), self.core)
        self.left = (self.seq, ring_index(self.place - 1, size), self.core)
        self.across = (1 - self.seq, self.ctx, self.core)
        self.sibling = (self.seq, self.ctx, 1 - self.core)

    def index(self, offset):
        return ring_index(self.place + offset, self.size)

    def at(self, offset):
        return (self.seq, self.index(offset), self.core)


class RingGather:
    def __init__(self, around, both, x_ref, o_ref, ring_s, ring_r, cross_s, cross_r, core_s, core_r, loc):
        self.a, self.both, self.x, self.o = around, both, x_ref, o_ref
        self.rs, self.rr, self.cs, self.cr = ring_s, ring_r, cross_s, cross_r
        self.ts, self.tr, self.loc = core_s, core_r, loc
        self.rows = x_ref.shape[0]
        self.chunk = self.rows // 4
        size = around.size
        far, near = size // 2, size - 1 - size // 2
        if both:
            self.items = [(1, False, far, near), (0, False, near, far), (0, True, far, near)]
        else:
            self.items = [(0, False, far, near), (1, False, near, far)]

    def partners(self):
        a = self.a
        return [a.right, a.left, a.sibling] + ([a.across] if self.both else [])

    def spot(self, other, index, chunk):
        a = self.a
        if self.both:
            block = (1 - a.seq if other else a.seq) * a.size + index + a.core * 2 * a.size
            return rows_at(block * (2 * self.chunk) + chunk * self.chunk, self.chunk)
        return rows_at(index * self.rows + a.core * (2 * self.chunk) + chunk * self.chunk, self.chunk)

    def own(self, chunk):
        return self.x.at[rows_at(self.a.core * (2 * self.chunk) + chunk * self.chunk, self.chunk)]

    def hop(self, item, way, step, src, where):
        device = self.a.right if way == 0 else self.a.left
        copy = remote(
            src, self.o.at[where], self.rs.at[item, way, step], self.rr.at[item, way, step], device
        )
        self.ring[item, way, step] = copy
        self.sent.append(copy)

    def cross(self, slot, src, where):
        copy = remote(src, self.o.at[where], self.cs.at[slot], self.cr.at[slot], self.a.across)
        self.crossed[slot] = copy
        self.sent.append(copy)

    def share(self, where):
        slot = len(self.shared)
        src = self.o.at[where]
        copy = remote(src, src, self.ts.at[slot], self.tr.at[slot], self.a.sibling)
        self.shared.append(copy)
        self.sent.append(copy)

    def start(self):
        a = self.a
        self.ring, self.crossed, self.shared, self.sent = {}, {}, [], []
        if self.both:
            half = 2 * self.chunk
            block = a.seq * a.size + a.ctx
            pairs = [
                (self.x.at[pl.ds(core * half, half)], rows_at((core * 2 * a.size + block) * half, half))
                for core in range(2)
            ]
        else:
            pairs = [(self.x, rows_at(a.ctx * self.rows, self.rows))]
        self.local = [
            pltpu.make_async_copy(src, self.o.at[where], self.loc.at[at])
            for at, (src, where) in enumerate(pairs)
        ]
        for copy in self.local:
            copy.start()
        if self.both:
            self.cross(0, self.own(0), self.spot(False, a.ctx, 0))
        for item, (chunk, other, _, _) in enumerate(self.items):
            if not other:
                for way in range(2):
                    self.hop(item, way, 0, self.own(chunk), self.spot(False, a.ctx, chunk))
        self.landed = []
        if self.both:
            self.cross(1, self.own(1), self.spot(False, a.ctx, 1))
            self.landed.append((1, a.ctx))
            self.crossed[0].wait_recv()
            where = self.spot(True, a.ctx, 0)
            for way in range(2):
                self.hop(2, way, 0, self.o.at[where], where)
            self.share(where)

    def step(self, k):
        a = self.a
        for item, (chunk, other, right, left) in enumerate(self.items):
            for way, hops in ((0, right), (1, left)):
                if k >= hops:
                    continue
                self.ring[item, way, k].wait_recv()
                index = a.index(-(k + 1) if way == 0 else k + 1)
                where = self.spot(other, index, chunk)
                if k + 1 < hops:
                    self.hop(item, way, k + 1, self.o.at[where], where)
                if self.both and item == 0:
                    slot = 1 + len(self.landed)
                    self.cross(slot, self.o.at[where], where)
                    self.landed.append((slot, index))
                self.share(where)

    def finish(self):
        for slot, index in self.landed:
            self.crossed[slot].wait_recv()
            self.share(self.spot(True, index, 1))
        for copy in self.shared:
            copy.wait_recv()
        for copy in self.sent:
            copy.wait_send()
        for copy in self.local:
            copy.wait()

    @staticmethod
    def semaphores(size, both):
        items = 3 if both else 2
        shares = 2 * (size - 1) + (2 * size if both else 0)
        dma = pltpu.SemaphoreType.DMA
        return [
            dma((items, 2, size // 2)),
            dma((items, 2, size // 2)),
            dma((1 + size,)),
            dma((1 + size,)),
            dma((shares,)),
            dma((shares,)),
            dma((2,)),
        ]


def gather_kernel(size, both, *refs):
    if both:
        x_ref, half_ref, o_ref, whole_ref, held, half_s, half_r, half_l, *sems = refs
    else:
        x_ref, o_ref, *sems = refs
    ring = RingGather(Around(size), both, x_ref, o_ref, *sems)
    greet(ring.partners())
    ring.start()
    if both:
        where = whole_ref.at[rows_at(ring.a.core * half_ref.shape[0], half_ref.shape[0])]
        other = remote(half_ref, where, half_s, half_r, ring.a.sibling)
        here = pltpu.make_async_copy(half_ref, held, half_l.at[0])
        here.start()
        here.wait()
        here = pltpu.make_async_copy(held, where, half_l.at[1])
        here.start()
    for k in range(size // 2):
        ring.step(k)
    ring.finish()
    if both:
        here.wait()
        other.wait()


def ring_gather(x, size, ident, half=None):
    hbm = pl.BlockSpec(memory_space=pl.ANY)
    both = half is not None
    blocks = (2 if both else 1) * size
    shapes = [jax.ShapeDtypeStruct((blocks * x.shape[0], x.shape[1]), x.dtype)]
    if both:
        shapes.append(jax.ShapeDtypeStruct((2 * half.shape[0], half.shape[1]), half.dtype))
    dma = pltpu.SemaphoreType.DMA
    extra = [pltpu.VMEM(half.shape, half.dtype), dma(()), dma(()), dma((2,))] if both else []
    out = pl.pallas_call(
        functools.partial(gather_kernel, size, both),
        out_shape=shapes,
        in_specs=[hbm, hbm] if both else [hbm],
        out_specs=[hbm] * len(shapes),
        scratch_shapes=extra + RingGather.semaphores(size, both),
        compiler_params=pltpu.CompilerParams(
            collective_id=ident, has_side_effects=True, vmem_limit_bytes=vmem_bytes
        ),
        name="gather_all" if both else "gather_ctx",
    )(*((x, half) if both else (x,)))
    return out if both else out[0]


class RingSum:
    def __init__(
        self, around, both, p_ref, o_ref, acc, met, ringbuf, crossbuf, lastbuf,
        ring_s, ring_r, cross_s, cross_r, core_s, core_r, out_s, out_r, loc,
    ):
        self.a, self.both, self.p, self.o = around, both, p_ref, o_ref
        self.acc, self.met, self.ringbuf = acc, met, ringbuf
        self.crossbuf, self.lastbuf = crossbuf, lastbuf
        self.rs, self.rr, self.cs, self.cr = ring_s, ring_r, cross_s, cross_r
        self.ts, self.tr, self.os, self.or_, self.loc = core_s, core_r, out_s, out_r, loc
        self.rows = o_ref.shape[0]
        self.half, self.chunk = self.rows // 2, self.rows // 4
        size = around.size
        far, near = size // 2, size - 1 - size // 2
        if both:
            self.items = [(0, 1, far, near), (0, 0, near, far), (1, 0, far, near)]
        else:
            self.items = [(0, 0, far, near), (1, 0, near, far)]
        order = []
        for d in range(size // 2, 0, -1):
            order += [d] if 2 * d == size else [d, size - d]
        self.order = order + [0]

    def partners(self):
        a = self.a
        return [a.right, a.left, a.sibling] + ([a.across] if self.both else [])

    def spot(self, other, offset, core):
        a = self.a
        block = a.index(offset)
        if self.both:
            block = core * 2 * a.size + (1 - a.seq if other else a.seq) * a.size + block
        else:
            block = 2 * block + core
        return rows_at(block * self.half, self.half)

    def start(self):
        a = self.a
        self.pending, self.sent, self.ring, self.crossed = {}, [], {}, {}
        for other in ((1, 0) if self.both else (0,)):
            for j in self.order:
                away = remote(
                    self.p.at[self.spot(other, j, 1 - a.core)],
                    self.met.at[other, j],
                    self.ts.at[other, j],
                    self.tr.at[other, j],
                    a.sibling,
                )
                here = pltpu.make_async_copy(
                    self.p.at[self.spot(other, j, a.core)], self.acc.at[other, j], self.loc.at[other, j]
                )
                here.start()
                self.pending[other, j] = (away, here)
                self.sent.append(away)
        if self.both:
            for j in self.order:
                self.ready(1, j)
                self.crossed[j] = remote(
                    self.part(self.acc, 1, j, 1), self.crossbuf.at[j], self.cs.at[j], self.cr.at[j], a.across
                )
                self.sent.append(self.crossed[j])

    def part(self, ref, other, j, chunk):
        return ref.at[other, j, pl.ds(chunk * self.chunk, self.chunk)]

    def ready(self, other, j):
        if (other, j) in self.pending:
            away, here = self.pending.pop((other, j))
            away.wait_recv()
            here.wait()
            self.add(self.acc.at[other, j], self.met.at[other, j])

    def add(self, into, more):
        into[...] = (into[...].astype(f32) + more[...].astype(f32)).astype(into.dtype)

    def prepare(self, other, j, chunk):
        self.ready(other, j)
        if self.both and chunk == 1 and j in self.crossed:
            self.crossed.pop(j).wait_recv()
            self.add(self.part(self.acc, 0, j, 1), self.crossbuf.at[j])

    def step(self, k):
        a = self.a
        for item, (chunk, other, right, left) in enumerate(self.items):
            for way, hops in ((0, right), (1, left)):
                d = hops - k
                if d < 1:
                    continue
                j = d if way == 0 else a.size - d
                self.prepare(other, j, chunk)
                block = self.part(self.acc, other, j, chunk)
                if k > 0:
                    self.ring[item, way, d].wait_recv()
                    self.add(block, self.ringbuf.at[item, way, d])
                copy = remote(
                    block,
                    self.ringbuf.at[item, way, d - 1],
                    self.rs.at[item, way, d - 1],
                    self.rr.at[item, way, d - 1],
                    a.right if way == 0 else a.left,
                )
                self.ring[item, way, d - 1] = copy
                self.sent.append(copy)

    def finish(self):
        a = self.a
        last = []
        for item, (chunk, other, _, _) in enumerate(self.items):
            self.prepare(other, 0, chunk)
            block = self.part(self.acc, other, 0, chunk)
            for way in range(2):
                self.ring[item, way, 0].wait_recv()
                self.add(block, self.ringbuf.at[item, way, 0])
            if other:
                slot = a.size
                final = remote(block, self.lastbuf, self.cs.at[slot], self.cr.at[slot], a.across)
                self.sent.append(final)
            else:
                last.append((chunk, block))
        for chunk, block in sorted(last, key=lambda entry: -entry[0]):
            if self.both and chunk == 0:
                final.wait_recv()
                self.add(block, self.lastbuf)
            where = rows_at(a.core * self.half + chunk * self.chunk, self.chunk)
            self.o[where] = block[...]
            copy = remote(
                self.o.at[where], self.o.at[where], self.os.at[chunk], self.or_.at[chunk], a.sibling
            )
            self.sent.append(copy)
            last_copy = copy
            self.outs = getattr(self, "outs", []) + [last_copy]
        for copy in self.outs:
            copy.wait_recv()
        for copy in self.sent:
            copy.wait_send()

    @staticmethod
    def scratch(size, both, rows, width, dtype):
        items = 3 if both else 2
        plane = 2 if both else 1
        half, chunk = rows // 2, rows // 4
        dma = pltpu.SemaphoreType.DMA
        few = size if both else 1
        return [
            pltpu.VMEM((plane, size, half, width), dtype),
            pltpu.VMEM((plane, size, half, width), dtype),
            pltpu.VMEM((items, 2, size // 2, chunk, width), dtype),
            pltpu.VMEM((few, chunk, width), dtype),
            pltpu.VMEM((chunk, width), dtype),
            dma((items, 2, size // 2)),
            dma((items, 2, size // 2)),
            dma((few + 1,)),
            dma((few + 1,)),
            dma((plane, size)),
            dma((plane, size)),
            dma((2,)),
            dma((2,)),
            dma((plane, size)),
        ]


def sum_kernel(size, both, p_ref, o_ref, *scratch):
    ring = RingSum(Around(size), both, p_ref, o_ref, *scratch)
    greet(ring.partners())
    ring.start()
    for k in range(size // 2):
        ring.step(k)
    ring.finish()


def ring_sum(p, size, both, ident):
    blocks = (2 if both else 1) * size
    rows, width = p.shape[0] // blocks, p.shape[1]
    return pl.pallas_call(
        functools.partial(sum_kernel, size, both),
        out_shape=jax.ShapeDtypeStruct((rows, width), p.dtype),
        in_specs=[pl.BlockSpec(memory_space=pl.ANY)],
        out_specs=pl.BlockSpec(memory_space=pltpu.VMEM),
        scratch_shapes=RingSum.scratch(size, both, rows, width, p.dtype),
        compiler_params=pltpu.CompilerParams(
            collective_id=ident, has_side_effects=True, vmem_limit_bytes=vmem_bytes
        ),
        name="sum_all" if both else "sum_ctx",
    )(p)


def leave_kernel(
    size, halves, p_ref, g_ref, v_ref, o_ref, go_ref, vo_ref, gmet, vmet, g_s, g_r, gl, v_s, v_r, *scratch
):
    a = Around(size)
    ring = RingSum(a, False, p_ref, o_ref, *scratch)
    pair = a.ctx + 1 - 2 * (a.ctx % 2)
    peers = [(a.seq, lax.rem(a.ctx + 2 * d, size), a.core) for d in range(1, size // 2)]
    load = pltpu.make_async_copy(g_ref.at[0], go_ref, gl)
    greet([a.right, a.left, a.sibling, a.across, (a.seq, pair, a.core)] + peers)
    swaps = [remote(v_ref, vmet.at[0], v_s.at[0], v_r.at[0], a.across)]
    crossed = [remote(g_ref.at[1, i], gmet.at[i], g_s.at[i], g_r.at[i], a.across) for i in range(size)]
    ring.start()
    load.start()
    last = 3 + size // 2

    def take(first, upto):
        for i in range(first, upto):
            crossed[i].wait_recv()
            ring.add(go_ref.at[i], gmet.at[i])

    for k in range(size // 2):
        ring.step(k)
        if k == 0:
            swaps[0].wait()
            vmet[1] = v_ref[...] + vmet[0]
            swaps = [remote(vmet.at[1], vmet.at[2], v_s.at[1], v_r.at[1], (a.seq, pair, a.core))]
            load.wait()
        elif k == 1:
            swaps[0].wait()
            vmet[3] = vmet[1] + vmet[2]
            swaps = [
                remote(vmet.at[3], vmet.at[3 + d], v_s.at[1 + d], v_r.at[1 + d], peers[d - 1])
                for d in range(1, size // 2)
            ]
        take(2 * k, 2 * k + 1 if k == size // 2 - 1 else 2 * (k + 1))
    for copy in swaps:
        copy.wait()
    total = vmet[3]
    for d in range(1, size // 2):
        total = total + vmet[3 + d]
    vmet[last] = total
    copy = remote(vmet.at[last], vmet.at[last + 1], v_s.at[size // 2 + 1], v_r.at[size // 2 + 1], a.sibling)
    ring.finish()
    take(size - 1, size)
    copy.wait()
    own, other = vmet[last], vmet[last + 1]
    vo_ref[...] = jnp.zeros_like(vo_ref)
    vo_ref[0:1] = own[0:1] + other[0:1]
    vo_ref[1:2] = own[1:2]
    core = lax.broadcasted_iota(jnp.int32, (halves, own.shape[1]), 0) * 0 + a.core
    first, second = own[2 : 2 + halves], other[2 : 2 + halves]
    vo_ref[2 : 2 + halves] = jnp.where(core == 0, first, second)
    vo_ref[2 + halves : 2 + 2 * halves] = jnp.where(core == 0, second, first)
    for copy in crossed:
        copy.wait_send()


def leave(p, g, small, halves, size, ident):
    rows, model = p.shape[0] // size, p.shape[1]
    dma = pltpu.SemaphoreType.DMA
    hbm = pl.BlockSpec(memory_space=pl.ANY)
    vmem = pl.BlockSpec(memory_space=pltpu.VMEM)
    steps = size // 2 + 2
    out_rows = -(-(2 + 2 * halves) // 8) * 8
    return pl.pallas_call(
        functools.partial(leave_kernel, size, halves),
        out_shape=(
            jax.ShapeDtypeStruct((rows, model), p.dtype),
            jax.ShapeDtypeStruct(g.shape[1:], g.dtype),
            jax.ShapeDtypeStruct((out_rows, small.shape[1]), small.dtype),
        ),
        in_specs=[hbm, hbm, vmem],
        out_specs=(vmem, vmem, vmem),
        scratch_shapes=[
            pltpu.VMEM(g.shape[1:], g.dtype),
            pltpu.VMEM((size // 2 + 5,) + small.shape, small.dtype),
            dma((size,)),
            dma((size,)),
            dma(()),
            dma((steps,)),
            dma((steps,)),
        ]
        + RingSum.scratch(size, False, rows, model, p.dtype),
        compiler_params=pltpu.CompilerParams(
            collective_id=ident, has_side_effects=True, vmem_limit_bytes=vmem_bytes
        ),
        name="leave_rows",
    )(p, g, small)


def settle_kernel(width, kv_of, spans, g_ref, v_ref, q_ref, kv_ref, wo_ref, *small_refs):
    proj = width + 2 * HEAD_DIMENSION
    weight_rows = q_ref.shape[0]
    by_head = {}
    for index, head_at in enumerate(kv_of):
        block = g_ref[index, :weight_rows].astype(f32)
        span = slice(index * width, (index + 1) * width)
        q_ref[:, span] = block[:, :width]
        wo_ref[:, span] = block[:, proj:]
        piece = block[:, width:proj]
        by_head[head_at] = by_head[head_at] + piece if head_at in by_head else piece
    for head_at, piece in by_head.items():
        kv_ref[:, head_at * 2 * HEAD_DIMENSION : (head_at + 1) * 2 * HEAD_DIMENSION] = piece
    for ref, (row, start) in zip(small_refs, spans):
        ref[...] = v_ref[row : row + ref.shape[0], start : start + ref.shape[1]]


def settle_gradients(g, v, width, weight_rows, kv_of, spans, shapes):
    kv_wide = (max(kv_of) + 1) * 2 * HEAD_DIMENSION
    large = [(weight_rows, len(kv_of) * width), (weight_rows, kv_wide), (weight_rows, len(kv_of) * width)]
    vmem = pl.BlockSpec(memory_space=pltpu.VMEM)
    return pl.pallas_call(
        functools.partial(settle_kernel, width, kv_of, spans),
        out_shape=[jax.ShapeDtypeStruct(shape, f32) for shape in large + shapes],
        in_specs=[vmem] * 2,
        out_specs=[vmem] * (3 + len(shapes)),
        compiler_params=pltpu.CompilerParams(vmem_limit_bytes=vmem_bytes),
        name="settle_gradients",
    )(g, v)


def plain_enter(x, w):
    rows = lax.all_gather(x, "ctx", axis=0, tiled=True)
    mine = lax.all_to_all(w, "ctx", split_axis=0, concat_axis=0, tiled=True)
    return rows, lax.all_gather(mine, "seq", axis=0, tiled=True)


def plain_sum(p, axes):
    part = lax.psum_scatter(p, axes, scatter_dimension=0, tiled=True)
    return lax.psum(part, "tp")


def plain_leave(p, g, small):
    kept = lax.psum_scatter(g, "seq", scatter_dimension=0, tiled=True)
    owned = lax.all_to_all(kept, "ctx", split_axis=0, concat_axis=0, tiled=True)
    small = jnp.concatenate([lax.psum(small[:1], "tp"), small[1:]])
    return plain_sum(p, "ctx"), owned, lax.psum(small, ("seq", "ctx"))


def expert_kernel(
    units, model, lead_ref, x_ref, dy_ref, wt_ref, bias_ref, wd_ref, bd_ref, pick_ref, place_ref,
    out_ref, back_ref, act_ref, dgu_ref, gbias_ref, dbias_ref,
):
    step = pl.program_id(0)
    tail = model // 128 * 128
    rows = x_ref.shape[0]
    x = x_ref[:, :model]
    dy = dy_ref[...]
    ends = x_ref[:, tail:]
    gate_row = across(pick_ref[...], ends)[:1]
    gate_col = across(ends, pick_ref[...])[:, :1]

    gate = clamp_limit * jnp.tanh((across(wt_ref[:units], x) + bias_ref[:units]) / clamp_limit)
    up = clamp_limit * jnp.tanh((across(wt_ref[units:], x) + bias_ref[units:]) / clamp_limit)
    squash = jax.nn.sigmoid(glu_alpha * gate)
    swish = gate * squash
    act = (up + 1.0) * swish
    out = down(act.astype(bf16), wd_ref[...]) + lead_ref[0, 0] * bd_ref[...]
    out_ref[...] = (gate_col * out).astype(bf16)

    act_grad = across(wd_ref[...], dy)
    high = bd_ref[...].astype(bf16)
    low = (bd_ref[...] - high.astype(f32)).astype(bf16)
    bias_dot = across(jnp.concatenate([high, low] + [jnp.zeros_like(high)] * 14, axis=0), dy)
    gate_grad = jnp.sum(act * act_grad, axis=0, keepdims=True) + lead_ref[0, 0] * (
        bias_dot[0:1] + bias_dot[1:2]
    )
    gate_grad = jnp.where(gate_row > 0, gate_grad, 0.0)
    act_grad = act_grad * gate_row
    slope = 1.0 - (gate / clamp_limit) * (gate / clamp_limit)
    dgate = (
        act_grad * (up + 1.0) * (squash + glu_alpha * swish * (1.0 - squash)) * slope
    ).astype(bf16)
    dup = (act_grad * swish * (1.0 - (up / clamp_limit) * (up / clamp_limit))).astype(bf16)
    act_ref[...] = (act * gate_row).astype(bf16)
    dgu_ref[:units] = dgate
    dgu_ref[units:] = dup

    back = down(dgate, wt_ref[:units]) + down(dup, wt_ref[units:])
    back_ref[:, :model] = back.astype(bf16)
    top = gate_grad.astype(bf16)
    rest = (gate_grad - top.astype(f32)).astype(bf16)
    sent = jnp.concatenate([top, rest] + [jnp.zeros_like(top)] * 14, axis=0)
    ends_out = down(sent, place_ref[...]).astype(bf16)
    back_ref[:, model:] = ends_out[:, model - tail :]

    @pl.when(step == 0)
    def _():
        gbias_ref[...] = jnp.zeros_like(gbias_ref)
        dbias_ref[...] = jnp.zeros_like(dbias_ref)

    gbias_ref[:units] += jnp.sum(dgate.astype(f32), axis=1, keepdims=True)
    gbias_ref[units:] += jnp.sum(dup.astype(f32), axis=1, keepdims=True)
    gate_high = gate_row.astype(bf16)
    gate_low = (gate_row - gate_high.astype(f32)).astype(bf16)
    gates = jnp.concatenate([gate_high, gate_low] + [jnp.zeros_like(gate_high)] * 14, axis=0)
    sums = jnp.dot(gates, dy, preferred_element_type=f32)
    dbias_ref[...] += sums[0:1] + sums[1:2]


def expert_rows(lead, x, dy, wt, bias, wd, bd, pick, place):
    count, wide = x.shape
    model = dy.shape[1]
    units = wd.shape[0]
    rows = min(256, count)
    tail = model // 128 * 128
    back_wide = tail + place.shape[1]
    row = lambda i: (i, 0)
    col = lambda i: (0, i)
    fixed = lambda i: (0, 0)
    whole = lambda v: pl.BlockSpec(v.shape, fixed)
    return pl.pallas_call(
        functools.partial(expert_kernel, units, model),
        grid=(count // rows,),
        out_shape=(
            jax.ShapeDtypeStruct((count, model), bf16),
            jax.ShapeDtypeStruct((count, back_wide), bf16),
            jax.ShapeDtypeStruct((units, count), bf16),
            jax.ShapeDtypeStruct((2 * units, count), bf16),
            jax.ShapeDtypeStruct((2 * units, 1), f32),
            jax.ShapeDtypeStruct((1, model), f32),
        ),
        in_specs=[
            pl.BlockSpec(memory_space=pltpu.SMEM),
            pl.BlockSpec((rows, wide), row),
            pl.BlockSpec((rows, model), row),
            whole(wt),
            whole(bias),
            whole(wd),
            whole(bd),
            whole(pick),
            whole(place),
        ],
        out_specs=(
            pl.BlockSpec((rows, model), row),
            pl.BlockSpec((rows, back_wide), row),
            pl.BlockSpec((units, rows), col),
            pl.BlockSpec((2 * units, rows), col),
            pl.BlockSpec((2 * units, 1), fixed),
            pl.BlockSpec((1, model), fixed),
        ),
        compiler_params=pltpu.CompilerParams(vmem_limit_bytes=vmem_bytes),
        name="expert_rows",
    )(lead, x, dy, wt, bias, wd, bd, pick, place)


def unit_order(size):
    order = [size // 2]
    for d in range(size // 2 - 1, 0, -1):
        order += [d, size - d]
    return order + [0]


def unit_slots(size):
    return {j: slot for slot, j in enumerate(unit_order(size))}


class UnitGather:
    def __init__(self, around, x_ref, buf, sems, first):
        self.a, self.x, self.buf = around, x_ref, buf
        self.own_s, self.ring_s, self.ring_r, self.cross_s, self.cross_r, self.core_s, self.core_r = sems
        self.rows = x_ref.shape[0]
        self.half = self.rows // 2
        self.starts, self.counts = (0, first), (first, self.half - first)
        size = around.size
        far, near = size // 2, size - 1 - size // 2
        self.items = [(1, 0, far, near), (0, 0, near, far), (0, 1, far, near)]
        self.slot_of = unit_slots(size)
        self.sent, self.ring, self.crossed, self.shared = [], {}, {}, {}

    @staticmethod
    def semaphores(size):
        dma = pltpu.SemaphoreType.DMA
        return [
            dma((2,)),
            dma((3, 2, size // 2)),
            dma((3, 2, size // 2)),
            dma((size + 1,)),
            dma((size + 1,)),
            dma((size, 2, 2)),
            dma((size, 2, 2)),
        ]

    def spot(self, j, other, core, piece):
        start = other * self.rows + core * self.half + self.starts[piece]
        return self.buf.at[self.slot_of[j], pl.ds(start, self.counts[piece])]

    def hop(self, item, way, k, src):
        a = self.a
        piece, other, _, _ = self.items[item]
        j = a.size - (k + 1) if way == 0 else k + 1
        copy = remote(
            src, self.spot(j, other, 0, piece), self.ring_s.at[item, way, k], self.ring_r.at[item, way, k],
            a.right if way == 0 else a.left,
        )
        self.ring[item, way, k] = copy
        self.sent.append(copy)

    def cross(self, j, piece, src):
        at = self.slot_of[j] if piece else self.a.size
        copy = remote(src, self.spot(j, 1, 0, piece), self.cross_s.at[at], self.cross_r.at[at], self.a.across)
        self.crossed[j, piece] = copy
        self.sent.append(copy)

    def share(self, j, other, piece):
        at = (self.slot_of[j], other, piece)
        copy = remote(
            self.spot(j, other, 0, piece), self.spot(j, other, 1, piece), self.core_s.at[at],
            self.core_r.at[at], self.a.sibling,
        )
        self.shared[j, other, piece] = copy
        self.sent.append(copy)

    def start(self):
        a, half = self.a, self.half

        def own(core, start, count):
            return self.x.at[pl.ds(pl.multiple_of(core * half + start, 16), count)]

        pieces = [own(a.core, start, count) for start, count in zip(self.starts, self.counts)]
        self.cross(0, 0, pieces[0])
        for item in range(2):
            for way in range(2):
                self.hop(item, way, 0, pieces[self.items[item][0]])
        self.cross(0, 1, pieces[1])
        self.mine = [
            pltpu.make_async_copy(
                own(a.core if here == 0 else 1 - a.core, 0, half),
                self.buf.at[self.slot_of[0], pl.ds(here * half, half)],
                self.own_s.at[here],
            )
            for here in range(2)
        ]
        for copy in self.mine:
            copy.start()

    def first(self):
        self.crossed[0, 0].wait_recv()
        for way in range(2):
            self.hop(2, way, 0, self.spot(0, 1, 0, 0))
        self.share(0, 1, 0)
        self.crossed[0, 1].wait_recv()
        self.share(0, 1, 1)

    def step(self, k):
        size = self.a.size
        for item, (piece, other, right, left) in enumerate(self.items):
            for way, hops in ((0, right), (1, left)):
                if k >= hops:
                    continue
                self.ring[item, way, k].wait_recv()
                j = size - (k + 1) if way == 0 else k + 1
                if k + 1 < hops:
                    self.hop(item, way, k + 1, self.spot(j, other, 0, piece))
                if item == 0:
                    self.cross(j, 1, self.spot(j, 0, 0, 1))
                self.share(j, other, piece)

    def after(self, k):
        if k < 0:
            return [0]
        return [k + 1] if 2 * (k + 1) == self.a.size else [k + 1, self.a.size - (k + 1)]

    def collect(self, js):
        for j in js:
            if j == 0:
                for copy in self.mine:
                    copy.wait()
            else:
                self.crossed[j, 1].wait_recv()
                self.share(j, 1, 1)
        for j in js:
            for key in [(j, 0, 0), (j, 0, 1), (j, 1, 0), (j, 1, 1)]:
                if key in self.shared:
                    self.shared[key].wait_recv()

    def finish(self):
        for copy in self.sent:
            copy.wait_send()


class UnitSum:
    def __init__(self, around, rows, lhs, w, ends, o_ref, scratch, first):
        (
            self.acc, self.own, self.out, self.ringbuf, self.crossbuf, self.lastbuf,
            self.ring_s, self.ring_r, self.cross_s, self.cross_r, self.core_s, self.core_r,
            self.out_s, self.out_r,
        ) = scratch
        self.a, self.rows, self.lhs, self.w, self.ends, self.o = around, rows, lhs, w, ends, o_ref
        self.half = rows // 2
        self.starts, self.counts = (0, first), (first, self.half - first)
        size = around.size
        far, near = size // 2, size - 1 - size // 2
        self.items = [(0, 1, far, near), (0, 0, near, far), (1, 0, far, near)]
        self.slot_of = unit_slots(size)
        self.ring, self.sent, self.joined, self.made = {}, [], set(), 0

    @staticmethod
    def scratch(size, rows, width, first):
        half = rows // 2
        dma = pltpu.SemaphoreType.DMA
        return [
            pltpu.VMEM((2, size, half, width), bf16),
            pltpu.VMEM((2, 2, half, width), bf16),
            pltpu.VMEM((2, 2, half, width), bf16),
            pltpu.VMEM((2, size // 2, half + first, width), bf16),
            pltpu.VMEM((size, half - first, width), bf16),
            pltpu.VMEM((first, width), bf16),
            dma((3, 2, size // 2)),
            dma((3, 2, size // 2)),
            dma((size + 1,)),
            dma((size + 1,)),
            dma((2, size)),
            dma((2, size)),
            dma((2,)),
            dma((2,)),
        ]

    def arrived(self, item, way, d):
        first, second = self.counts
        start, count = ((0, first), (first, first), (2 * first, second))[item]
        return self.ringbuf.at[way, d, pl.ds(start, count)]

    def handed(self, slot, other):
        return pltpu.make_async_remote_copy(
            src_ref=self.out.at[slot % 2, other],
            dst_ref=self.acc.at[other, slot],
            send_sem=self.core_s.at[other, slot],
            recv_sem=self.core_r.at[other, slot],
            device_id=self.a.sibling,
            device_id_type=pl.DeviceIdType.MESH,
        )

    def over(self, slot):
        return pltpu.make_async_remote_copy(
            src_ref=self.acc.at[1, slot, pl.ds(self.starts[1], self.counts[1])],
            dst_ref=self.crossbuf.at[slot],
            send_sem=self.cross_s.at[slot],
            recv_sem=self.cross_r.at[slot],
            device_id=self.a.across,
            device_id_type=pl.DeviceIdType.MESH,
        )

    def add(self, into, more):
        into[...] = (into[...].astype(f32) + more[...].astype(f32)).astype(bf16)

    def settle(self, slot):
        for other in range(2):
            self.handed(slot, other).wait_recv()
            self.add(self.acc.at[other, slot], self.own.at[slot % 2, other])
        self.over(slot).start()

    def produce(self, slot, carry):
        @pl.when(slot >= 2)
        def _():
            for other in range(2):
                self.handed(slot - 2, other).wait_send()

        rows, half = self.rows, self.half
        model = self.w.shape[1]
        columns = pl.ds(pl.multiple_of(slot * 2 * rows, 2 * rows), 2 * rows)
        y = down(self.lhs[:, columns], self.w[...])
        spots = [(other, place, into) for other in range(2) for place, into in ((0, self.own), (half, self.out))]
        for other, place, into in spots:
            start = other * rows + place
            into[slot % 2, other, :, :model] = y[start : start + half].astype(bf16)
        if self.ends is not None:
            dg_ref, place_ref = self.ends
            ends = down(dg_ref[:, columns], place_ref[...])[:, model % 128 :].astype(bf16)
            for other, place, into in spots:
                start = other * rows + place
                into[slot % 2, other, :, model:] = ends[start : start + half]
        for other in range(2):
            self.handed(slot, other).start()

        @pl.when(slot >= 1)
        def _():
            self.settle(slot - 1)

        return carry

    def make(self, upto):
        upto = min(upto, self.a.size)
        if upto > self.made:
            lax.fori_loop(self.made, upto, self.produce, 0)
            self.made = upto

    def part(self, other, j, piece):
        return self.acc.at[other, self.slot_of[j], pl.ds(self.starts[piece], self.counts[piece])]

    def join(self, j):
        if j not in self.joined:
            self.joined.add(j)
            self.over(self.slot_of[j]).wait_recv()
            self.add(self.part(0, j, 1), self.crossbuf.at[self.slot_of[j]])

    def begin(self):
        self.make(2)
        self.leave(0, 0)
        self.make(3)
        self.leave(1, 0)
        self.leave(0, 1)
        self.make(4)
        self.leave(2, 0)
        self.leave(1, 1)
        self.leave(2, 1)

    def leave(self, slot, piece):
        for item, (part, other, right, left) in enumerate(self.items):
            for way, d in ((0, right), (1, left)):
                j = d if way == 0 else self.a.size - d
                if part == piece and self.slot_of[j] == slot:
                    if piece == 1:
                        self.join(j)
                    self.send(item, way, d, self.part(other, j, piece))

    def send(self, item, way, d, block):
        copy = remote(
            block, self.arrived(item, way, d - 1), self.ring_s.at[item, way, d - 1],
            self.ring_r.at[item, way, d - 1], self.a.right if way == 0 else self.a.left,
        )
        self.ring[item, way, d - 1] = copy
        self.sent.append(copy)

    def step(self, k):
        a = self.a
        for item, (piece, other, right, left) in enumerate(self.items):
            for way, hops in ((0, right), (1, left)):
                d = hops - k
                if d < 1:
                    continue
                j = d if way == 0 else a.size - d
                if piece == 1:
                    self.join(j)
                block = self.part(other, j, piece)
                self.ring[item, way, d].wait_recv()
                self.add(block, self.arrived(item, way, d))
                self.send(item, way, d, block)

    def finish(self):
        a, size = self.a, self.a.size
        last = []
        for item, (piece, other, _, _) in enumerate(self.items):
            if piece == 1:
                self.join(0)
            block = self.part(other, 0, piece)
            for way in range(2):
                self.ring[item, way, 0].wait_recv()
                self.add(block, self.arrived(item, way, 0))
            if other:
                final = remote(block, self.lastbuf, self.cross_s.at[size], self.cross_r.at[size], a.across)
                self.sent.append(final)
            else:
                last.append((piece, block))
        outs = []
        for piece, block in sorted(last, key=lambda entry: -entry[0]):
            if piece == 0:
                final.wait_recv()
                self.add(block, self.lastbuf)
            start = pl.multiple_of(a.core * self.half + self.starts[piece], 16)
            where = self.o.at[pl.ds(start, self.counts[piece])]
            where[...] = block[...]
            outs.append(remote(where, where, self.out_s.at[piece], self.out_r.at[piece], a.sibling))
        for copy in outs:
            copy.wait()
        for copy in self.sent:
            copy.wait_send()
        for slot in range(size):
            self.over(slot).wait_send()
        for slot in range(size - 2, size):
            for other in range(2):
                self.handed(slot, other).wait_send()


def expert_kernel_all(
    size, units, model, experts,
    x_ref, dy_all, wt_ref, wd_ref, bias_ref, bd_ref,
    x_all, act_all, dgu_all, extra_all, o_ref, gbias_ref,
    xbuf, dybuf, wt, wd, act_buf, dgu_buf, dg_ref, pick_ref, place_ref, load_s, dy_s, keep_s, *scratch,
):
    a = Around(size)
    tail = model // 128 * 128
    few = len(UnitGather.semaphores(size))
    gather = UnitGather(a, x_ref, xbuf, scratch[:few], x_ref.shape[0] // 8)
    total = UnitSum(
        a, x_ref.shape[0], dgu_buf, wt, (dg_ref, place_ref), o_ref, scratch[few:], x_ref.shape[0] // 4
    )
    lane = lax.broadcasted_iota(jnp.int32, pick_ref.shape, 1) + tail - model
    line = lax.broadcasted_iota(jnp.int32, pick_ref.shape, 0)
    wanted = (lane == a.ctx) | (lane == experts + a.ctx)
    pick_ref[...] = jnp.where((line == 0) & wanted, 1.0, 0.0).astype(bf16)
    lane = lax.broadcasted_iota(jnp.int32, place_ref.shape, 1) + tail - model
    line = lax.broadcasted_iota(jnp.int32, place_ref.shape, 0)
    column = 2 * (4 * a.ctx + 2 * a.seq + a.core)
    place_ref[...] = jnp.where((line < 2) & (lane == column + line), 1.0, 0.0).astype(bf16)
    rows = x_ref.shape[0]
    wide = x_ref.shape[1]
    slot_of = gather.slot_of

    loads = [
        pltpu.make_async_copy(wt_ref, wt, load_s.at[0]),
        pltpu.make_async_copy(wd_ref, wd.at[pl.ds(0, units)], load_s.at[1]),
    ]
    greet([a.right, a.left, a.sibling, a.across])
    gather.start()

    def fetch(js):
        for j in js:
            slot = slot_of[j]
            copy = pltpu.make_async_copy(dy_all.at[slot], dybuf.at[slot % 2], dy_s.at[slot])
            copy.start()
            fetched[j] = copy

    fetched = {}
    for copy in loads:
        copy.start()
    fetch(gather.after(-1))
    lead = jnp.where((a.seq == 0) & (a.core == 0), 1.0, 0.0)
    bias = bd_ref[...] * lead
    bias_high = bias.astype(bf16)
    bias_low = (bias - bias_high.astype(f32)).astype(bf16)
    wd[units:] = jnp.concatenate([bias_high, bias_low, bias_high] + [jnp.zeros_like(bias_high)] * 13, axis=0)
    keep_extra = pltpu.make_async_copy(wd.at[pl.ds(units, 16)], extra_all, load_s.at[2])
    keep_extra.start()
    gbias_ref[...] = jnp.zeros_like(gbias_ref)

    def unit(slot, carry):
        x = xbuf[slot, :, :model]
        dy = dybuf[lax.rem(slot, 2), :, :model]
        ends = xbuf[slot, :, tail:wide]
        columns = pl.ds(pl.multiple_of(slot * 2 * rows, 2 * rows), 2 * rows)
        gate_row = across(pick_ref[...], ends)[:1]
        gate_tanh = jnp.tanh((across(wt[:units], x) + bias_ref[:units]) * (1.0 / clamp_limit))
        up_tanh = jnp.tanh((across(wt[units:], x) + bias_ref[units:]) * (1.0 / clamp_limit))
        squash = 0.5 + 0.5 * jnp.tanh((0.5 * glu_alpha * clamp_limit) * gate_tanh)
        swish = clamp_limit * gate_tanh * squash
        up = clamp_limit * up_tanh + 1.0
        act = up * swish
        act_grad = across(wd[...], dy)
        bias_dot = act_grad[units : units + 1] + act_grad[units + 1 : units + 2]
        act_grad = act_grad[:units]
        gate_grad = jnp.sum(act * act_grad, axis=0, keepdims=True) + bias_dot
        gate_grad = jnp.where(gate_row > 0, gate_grad, 0.0)
        act_grad = act_grad * gate_row
        slope = (squash + glu_alpha * swish * (1.0 - squash)) * (1.0 - gate_tanh * gate_tanh)
        dgate = (act_grad * up * slope).astype(bf16)
        dup = (act_grad * swish * (1.0 - up_tanh * up_tanh)).astype(bf16)
        dgu_buf[:units, columns] = dgate
        dgu_buf[units:, columns] = dup
        gbias_ref[:units] += jnp.sum(dgate.astype(f32), axis=1, keepdims=True)
        gbias_ref[units:] += jnp.sum(dup.astype(f32), axis=1, keepdims=True)
        high = gate_row.astype(bf16)
        low = (gate_row - high.astype(f32)).astype(bf16)
        act_buf[:units, columns] = (act * gate_row).astype(bf16)
        act_buf[units:, columns] = jnp.concatenate([high, high, low] + [jnp.zeros_like(high)] * 13, axis=0)
        top = gate_grad.astype(bf16)
        rest = (gate_grad - top.astype(f32)).astype(bf16)
        dg_ref[:, columns] = jnp.concatenate([top, rest] + [jnp.zeros_like(top)] * 14, axis=0)
        return carry

    kept = []

    def compute(js):
        gather.collect(js)
        for j in js:
            fetched[j].wait()
        slots = [slot_of[j] for j in js]
        lax.fori_loop(slots[0], slots[-1] + 1, unit, 0)
        for slot in slots:
            columns = pl.ds(slot * 2 * rows, 2 * rows)
            for at, (src, dst) in enumerate(
                (
                    (xbuf.at[slot], x_all.at[slot]),
                    (act_buf.at[:, columns], act_all.at[:, columns]),
                    (dgu_buf.at[:, columns], dgu_all.at[:, columns]),
                )
            ):
                copy = pltpu.make_async_copy(src, dst, keep_s.at[at, slot])
                copy.start()
                kept.append(copy)

    gather.first()
    for copy in loads:
        copy.wait()
    for k in range(size // 2):
        gather.step(k)
        compute(gather.after(k - 1))
        fetch(gather.after(k))
    compute(gather.after(size // 2 - 1))
    total.begin()
    gather.finish()
    total.make(6)
    for k in range(1, size // 2):
        if k == size // 2 - 1:
            total.settle(size - 1)
        total.step(k)
        total.make(6 + 2 * k)
    total.finish()
    for copy in kept:
        copy.wait()
    keep_extra.wait()


def expert_all(x, dy, wt, wd, bias, bd, experts, width, size, ident):
    rows, wide = x.shape
    units, model = wd.shape
    deep = units + 16
    count = 2 * size * rows
    tail = model // 128 * 128
    dma = pltpu.SemaphoreType.DMA
    hbm = pl.BlockSpec(memory_space=pl.ANY)
    vmem = pl.BlockSpec(memory_space=pltpu.VMEM)
    return pl.pallas_call(
        functools.partial(expert_kernel_all, size, units, model, experts),
        out_shape=(
            jax.ShapeDtypeStruct((size, 2 * rows, wide), bf16),
            jax.ShapeDtypeStruct((deep, count), bf16),
            jax.ShapeDtypeStruct((2 * units, count), bf16),
            jax.ShapeDtypeStruct((16, model), bf16),
            jax.ShapeDtypeStruct((rows, width), bf16),
            jax.ShapeDtypeStruct((2 * units, 1), f32),
        ),
        in_specs=[hbm, hbm, hbm, hbm, vmem, vmem],
        out_specs=(hbm, hbm, hbm, hbm, vmem, vmem),
        scratch_shapes=[
            pltpu.VMEM((size, 2 * rows, wide), bf16),
            pltpu.VMEM((2,) + dy.shape[1:], bf16),
            pltpu.VMEM((2 * units, model), bf16),
            pltpu.VMEM((deep, model), bf16),
            pltpu.VMEM((deep, count), bf16),
            pltpu.VMEM((2 * units, count), bf16),
            pltpu.VMEM((16, count), bf16),
            pltpu.VMEM((16, wide - tail), bf16),
            pltpu.VMEM((16, width - tail), bf16),
            dma((3,)),
            dma((size,)),
            dma((3, size)),
        ]
        + UnitGather.semaphores(size)
        + UnitSum.scratch(size, rows, width, rows // 4),
        compiler_params=pltpu.CompilerParams(
            collective_id=ident, has_side_effects=True, vmem_limit_bytes=vmem_most
        ),
        name="expert_all",
    )(x, dy, wt, wd, bias, bd)


def weights_kernel(model, first_ref, second_ref, x_ref, dy_ref, one_ref, two_ref, extra_ref):
    units = two_ref.shape[0]
    one_ref[...] = jnp.dot(first_ref[...], x_ref[...], preferred_element_type=f32)
    both = jnp.dot(second_ref[...], dy_ref[...], preferred_element_type=f32)
    two_ref[...] = both[:units]
    extra_ref[...] = both[units : units + 1] + both[units + 2 : units + 3]


def weight_gradients(first, second, x, dy, model, units):
    count = x.shape[0]
    cols = 384
    col = lambda i: (0, i)
    fixed = lambda i: (0, 0)
    once = pl.Buffered(1)
    return pl.pallas_call(
        functools.partial(weights_kernel, model),
        grid=(-(-model // cols),),
        out_shape=(
            jax.ShapeDtypeStruct((first.shape[0], model), f32),
            jax.ShapeDtypeStruct((units, model), f32),
            jax.ShapeDtypeStruct((1, model), f32),
        ),
        in_specs=[
            pl.BlockSpec(first.shape, fixed, pipeline_mode=once),
            pl.BlockSpec(second.shape, fixed, pipeline_mode=once),
            pl.BlockSpec((count, cols), col),
            pl.BlockSpec((count, cols), col),
        ],
        out_specs=(
            pl.BlockSpec((first.shape[0], cols), col),
            pl.BlockSpec((units, cols), col),
            pl.BlockSpec((1, cols), col),
        ),
        compiler_params=pltpu.CompilerParams(vmem_limit_bytes=vmem_bytes),
        cost_estimate=pl.CostEstimate(
            flops=2 * count * (first.shape[0] + second.shape[0]) * model,
            bytes_accessed=4 * (first.shape[0] + second.shape[0]) * model + 4 * count * model,
            transcendentals=0,
        ),
        name="weight_gradients",
    )(first, second, x, dy)


def turn(x, cosine, sine):
    half = HEAD_DIMENSION // 2
    width = x.shape[-1]
    if width % 128:
        starts = [start for at in range(0, width, 2 * half) for start in (at + half, at)]
        swapped = jnp.concatenate([x[:, start : start + half] for start in starts], axis=1)
    else:
        lane = lax.broadcasted_iota(jnp.int32, x.shape, 1)
        swapped = jnp.where(
            lane % HEAD_DIMENSION < half, pltpu.roll(x, width - half, 1), pltpu.roll(x, half, 1)
        )
    return x * cosine + swapped * sine


def spread(table, width):
    pieces = [table] * (width // 128) + ([table[:, : width % 128]] if width % 128 else [])
    return jnp.concatenate(pieces, axis=1) if len(pieces) > 1 else pieces[0]


def project_kernel(heads, x_ref, w_ref, b_ref, cos_ref, sin_ref, q_ref, k_ref, v_ref):
    width = heads * HEAD_DIMENSION
    y = jnp.dot(x_ref[...], w_ref[...], preferred_element_type=f32) + b_ref[...]
    cosine, sine = cos_ref[...], sin_ref[...]
    pad = 128
    q_ref[...] = turn(y[:, :width], spread(cosine, width), spread(sine, width)).astype(bf16)
    kv = y[:, width : width + pad]
    k_ref[...] = turn(kv, cosine, sine)[:, :HEAD_DIMENSION].astype(bf16)
    v_ref[...] = kv[:, HEAD_DIMENSION:].astype(bf16)


def project(x, w, bias, cosine, sine, heads):
    length, model = x.shape
    rows = min(256, length)
    width = heads * HEAD_DIMENSION
    row = lambda i: (i, 0)
    fixed = lambda i: (0, 0)
    return pl.pallas_call(
        functools.partial(project_kernel, heads),
        grid=(length // rows,),
        out_shape=(
            jax.ShapeDtypeStruct((length, width), bf16),
            jax.ShapeDtypeStruct((length, HEAD_DIMENSION), bf16),
            jax.ShapeDtypeStruct((length, HEAD_DIMENSION), bf16),
        ),
        in_specs=[
            pl.BlockSpec((rows, model), row),
            pl.BlockSpec(w.shape, fixed),
            pl.BlockSpec(bias.shape, fixed),
            pl.BlockSpec((rows, 128), row),
            pl.BlockSpec((rows, 128), row),
        ],
        out_specs=(
            pl.BlockSpec((rows, width), row),
            pl.BlockSpec((rows, HEAD_DIMENSION), row),
            pl.BlockSpec((rows, HEAD_DIMENSION), row),
        ),
        compiler_params=pltpu.CompilerParams(vmem_limit_bytes=vmem_bytes),
        name="project_rows",
    )(x, w, bias, cosine, sine)


def each_reach(block, rows, length, run):
    classes = min(4, length // rows)
    per = length // rows // classes
    for level in range(classes):
        pl.when(block // per == level)(functools.partial(run, (level + 1) * per * rows))


def attend_block(block, reach, heads, sink_ref, q, k_ref, v_ref):
    rows = q.shape[0]
    scale = 1.0 / math.sqrt(HEAD_DIMENSION)
    keys, values = k_ref[:reach], v_ref[:reach]
    row = block * rows + lax.broadcasted_iota(jnp.int32, (rows, reach), 0)
    allowed = lax.broadcasted_iota(jnp.int32, (rows, reach), 1) <= row
    outs, totals = [], []
    for head in range(heads):
        query = q[:, head * HEAD_DIMENSION : (head + 1) * HEAD_DIMENSION]
        scores = jnp.where(allowed, across(query, keys) * scale, masked_score)
        sink = sink_ref[0, head]
        top = jnp.maximum(jnp.max(scores, axis=1, keepdims=True), sink)
        weights = jnp.exp(scores - top)
        total = jnp.sum(weights, axis=1, keepdims=True) + jnp.exp(sink - top)
        mixed = jnp.dot(weights.astype(bf16), values, preferred_element_type=f32)
        outs.append(mixed / total)
        totals.append(top + jnp.log(total))
    return jnp.concatenate(outs, axis=1), jnp.concatenate(totals, axis=1)


def attend_kernel(heads, length, sink_ref, q_ref, k_ref, v_ref, w_ref, o_ref, low_ref, lse_ref, p_ref):
    rows = q_ref.shape[0]
    block = pl.program_id(0)

    def run(reach):
        joined, totals = attend_block(block, reach, heads, sink_ref, q_ref[...], k_ref, v_ref)
        o_ref[...] = joined
        joined_low = joined.astype(bf16)
        low_ref[...] = joined_low
        p_ref[...] = across(joined_low, w_ref[...]).astype(bf16)
        lse_ref[...] = totals

    each_reach(block, rows, length, run)


def attend(sinks, q, k, v, w):
    length, width = q.shape
    model = w.shape[0]
    heads = width // HEAD_DIMENSION
    rows = min(256, length)
    row = lambda i: (i, 0)
    fixed = lambda i: (0, 0)
    return pl.pallas_call(
        functools.partial(attend_kernel, heads, length),
        grid=(length // rows,),
        out_shape=(
            jax.ShapeDtypeStruct((length, width), f32),
            jax.ShapeDtypeStruct((length, width), bf16),
            jax.ShapeDtypeStruct((length, heads), f32),
            jax.ShapeDtypeStruct((length, model), bf16),
        ),
        in_specs=[
            pl.BlockSpec(memory_space=pltpu.SMEM),
            pl.BlockSpec((rows, width), row),
            pl.BlockSpec(k.shape, fixed),
            pl.BlockSpec(v.shape, fixed),
            pl.BlockSpec(w.shape, fixed),
        ],
        out_specs=(
            pl.BlockSpec((rows, width), row),
            pl.BlockSpec((rows, width), row),
            pl.BlockSpec((rows, heads), row),
            pl.BlockSpec((rows, model), row),
        ),
        compiler_params=pltpu.CompilerParams(vmem_limit_bytes=vmem_bytes),
        name="attend_rows",
    )(sinks, q, k, v, w)


def spread_kernel(x_ref, w_ref, o_ref):
    o_ref[...] = across(x_ref[...], w_ref[...]).astype(o_ref.dtype)


def spread_rows(x, w):
    count, width = x.shape
    rows = min(256, count)
    return pl.pallas_call(
        spread_kernel,
        grid=(count // rows,),
        out_shape=jax.ShapeDtypeStruct((count, w.shape[0]), bf16),
        in_specs=[
            pl.BlockSpec((rows, width), lambda i: (i, 0)),
            pl.BlockSpec(w.shape, lambda i: (0, 0)),
        ],
        out_specs=pl.BlockSpec((rows, w.shape[0]), lambda i: (i, 0)),
        compiler_params=pltpu.CompilerParams(vmem_limit_bytes=vmem_bytes),
        name="spread_rows",
    )(x, w)


def attend_back_block(block, reach, heads, sink_ref, q, k_ref, v_ref, o, lses, do, dk_acc, dv_acc, sink_acc):
    rows = q.shape[0]
    scale = 1.0 / math.sqrt(HEAD_DIMENSION)
    keys, values = k_ref[:reach], v_ref[:reach]
    row = block * rows + lax.broadcasted_iota(jnp.int32, (rows, reach), 0)
    allowed = lax.broadcasted_iota(jnp.int32, (rows, reach), 1) <= row
    parts, sink_parts = [], []
    key_sum = jnp.zeros((reach, HEAD_DIMENSION), f32)
    value_sum = jnp.zeros((reach, HEAD_DIMENSION), f32)
    for head in range(heads):
        span = slice(head * HEAD_DIMENSION, (head + 1) * HEAD_DIMENSION)
        query, grad = q[:, span], do[:, span]
        lse = lses[:, head : head + 1]
        delta = jnp.sum(grad.astype(f32) * o[:, span], axis=1, keepdims=True)
        scores = jnp.where(allowed, across(query, keys) * scale, masked_score)
        probs = jnp.exp(scores - lse)
        value_sum = value_sum + down(probs.astype(bf16), grad)
        score_grad = (probs * (across(grad, values) - delta)).astype(bf16)
        parts.append(jnp.dot(score_grad, keys, preferred_element_type=f32) * scale)
        key_sum = key_sum + down(score_grad, query)
        share = jnp.exp(sink_ref[0, head] - lse) * delta
        sink_parts.append(jnp.sum(share, axis=0, keepdims=True))
    dk_acc[:reach] += key_sum * scale
    dv_acc[:reach] += value_sum
    sink_acc[...] -= jnp.concatenate(sink_parts, axis=1)
    return jnp.concatenate(parts, axis=1)


def turned_back(dk, dv, cosine, sine):
    both = jnp.concatenate([dk, dv], axis=1)
    turned = turn(both, cosine, -sine)
    lane = lax.broadcasted_iota(jnp.int32, both.shape, 1)
    return jnp.where(lane < HEAD_DIMENSION, turned, both)


def attend_back_kernel(
    heads, length, sink_ref, q_ref, k_ref, v_ref, o_ref, lse_ref, do_ref, cos_ref, sin_ref,
    kcos_ref, ksin_ref, dq_ref, dkv_ref, dsink_ref, dk_acc, dv_acc, sink_acc,
):
    rows = q_ref.shape[0]
    block = pl.program_id(0)

    @pl.when(block == 0)
    def _():
        dk_acc[...] = jnp.zeros_like(dk_acc)
        dv_acc[...] = jnp.zeros_like(dv_acc)
        sink_acc[...] = jnp.zeros_like(sink_acc)

    def run(reach):
        dq = attend_back_block(
            block, reach, heads, sink_ref, q_ref[...], k_ref, v_ref, o_ref[...], lse_ref[...], do_ref[...],
            dk_acc, dv_acc, sink_acc,
        )
        wide = dq.shape[1]
        dq_ref[...] = turn(dq, spread(cos_ref[...], wide), -spread(sin_ref[...], wide)).astype(bf16)

    each_reach(block, rows, length, run)

    @pl.when(block == pl.num_programs(0) - 1)
    def _():
        dkv_ref[...] = turned_back(dk_acc[...], dv_acc[...], kcos_ref[...], ksin_ref[...]).astype(bf16)
        dsink_ref[...] = sink_acc[...]


def attend_back(sinks, q, k, v, o, lse, do, cosine, sine):
    length, width = q.shape
    heads = width // HEAD_DIMENSION
    rows = min(256, length)
    row = lambda i: (i, 0)
    fixed = lambda i: (0, 0)
    return pl.pallas_call(
        functools.partial(attend_back_kernel, heads, length),
        grid=(length // rows,),
        out_shape=(
            jax.ShapeDtypeStruct((length, width), bf16),
            jax.ShapeDtypeStruct((length, 2 * HEAD_DIMENSION), bf16),
            jax.ShapeDtypeStruct((1, heads), f32),
        ),
        in_specs=[
            pl.BlockSpec(memory_space=pltpu.SMEM),
            pl.BlockSpec((rows, width), row),
            pl.BlockSpec(k.shape, fixed),
            pl.BlockSpec(v.shape, fixed),
            pl.BlockSpec((rows, width), row),
            pl.BlockSpec((rows, heads), row),
            pl.BlockSpec((rows, width), row),
            pl.BlockSpec((rows, 128), row),
            pl.BlockSpec((rows, 128), row),
            pl.BlockSpec((length, 128), fixed),
            pl.BlockSpec((length, 128), fixed),
        ],
        out_specs=(
            pl.BlockSpec((rows, width), row),
            pl.BlockSpec((length, 2 * HEAD_DIMENSION), fixed),
            pl.BlockSpec((1, heads), fixed),
        ),
        scratch_shapes=[
            pltpu.VMEM((length, HEAD_DIMENSION), f32),
            pltpu.VMEM((length, HEAD_DIMENSION), f32),
            pltpu.VMEM((1, heads), f32),
        ],
        compiler_params=pltpu.CompilerParams(vmem_limit_bytes=vmem_bytes),
        name="attend_rows_back",
    )(sinks, q, k, v, o, lse, do, cosine, sine, cosine, sine)


def front_kernel(
    size, heads, kv_of,
    sink_ref, x_ref, wq_ref, kvw_ref, wt_ref, dy_ref, bias_ref, cos_ref, sin_ref,
    q_ref, k_ref, v_ref, o_ref, low_ref, lse_ref, rows_all, w_all, dy_all, out_ref,
    rows, send, blocks, w, part, dybuf, w_s, w_r, wx_s, wx_r, load_s, keep_s, *scratch,
):
    a = Around(size)
    one, two = len(RingGather.semaphores(size, False)), len(UnitGather.semaphores(size))
    ring = RingGather(a, False, x_ref, rows, *scratch[:one])
    gather = UnitGather(a, dy_ref, dybuf, scratch[one : one + two], dy_ref.shape[0] // 8)
    total = RingSum(a, False, part, out_ref, *scratch[one + two :])
    length, model = rows.shape
    weight_rows = wq_ref.shape[0]
    width = heads * HEAD_DIMENSION
    proj = width + 2 * HEAD_DIMENSION
    count = 256
    steps = length // count
    order = []
    for d in range(1, size // 2 + 1):
        order += [d] if 2 * d == size else [d, size - d]
    greet(ring.partners() + [a.across] + [a.at(d) for d in order if 1 < d < size - 1])
    ring.start()

    whole = weight_rows // 16 * 16
    send[:, whole:] = jnp.zeros((size, send.shape[1] - whole, send.shape[2]), bf16)
    for index in range(size):
        span = slice(index * width, (index + 1) * width)
        at = kv_of[index] * 2 * HEAD_DIMENSION
        send[index, :weight_rows, :width] = wq_ref[:, span]
        send[index, :weight_rows, width:proj] = kvw_ref[:, at : at + 2 * HEAD_DIMENSION]
        send[index, :weight_rows, proj:] = wt_ref[:, span]
    mine = a.seq * size + a.ctx
    spans = (pl.ds(0, proj), pl.ds(proj, width))
    sent, crossed = {}, {}

    def start_part(h):
        src = send.at[a.ctx, :, spans[h]]
        crossed[h, 0] = remote(src, blocks.at[mine, :, spans[h]], wx_s.at[h, 0], wx_r.at[h, 0], a.across)
        for d in order:
            src = send.at[a.index(d), :, spans[h]]
            sent[h, d] = remote(src, blocks.at[mine, :, spans[h]], w_s.at[h, d], w_r.at[h, d], a.at(d))

    def pass_part(h, times):
        for d in order:
            if (h, d) not in crossed and times > 0:
                sent[h, d].wait_recv()
                block = blocks.at[a.seq * size + a.index(-d), :, spans[h]]
                crossed[h, d] = remote(block, block, wx_s.at[h, d], wx_r.at[h, d], a.across)
                times -= 1

    def put_part(h):
        pass_part(h, size)
        for d in [0] + order:
            crossed[h, d].wait_recv()
        columns = slice(0, proj) if h == 0 else slice(proj, proj + width)
        for i in range(2 * size):
            w[i * weight_rows : (i + 1) * weight_rows, columns] = blocks[i, :weight_rows, columns]

    start_part(0)
    blocks[mine] = send[a.ctx]
    for k in range(size // 2):
        ring.step(k)
        pass_part(0, 2)
    start_part(1)
    ring.finish()
    gather.start()
    keep_rows = pltpu.make_async_copy(rows, rows_all, load_s.at[0])
    keep_rows.start()
    put_part(0)

    def project_step(i, carry):
        span = pl.ds(pl.multiple_of(i * count, count), count)
        y = jnp.dot(rows[span], w[:, :proj], preferred_element_type=f32) + bias_ref[...]
        cosine, sine = cos_ref[span], sin_ref[span]
        q_ref[span] = turn(y[:, :width], spread(cosine, width), spread(sine, width)).astype(bf16)
        kv = y[:, width:]
        k_ref[span] = turn(kv, cosine, sine)[:, :HEAD_DIMENSION].astype(bf16)
        v_ref[span] = kv[:, HEAD_DIMENSION:].astype(bf16)
        return carry

    lax.fori_loop(0, steps // 2, project_step, 0)
    gather.first()
    pass_part(1, 2)
    lax.fori_loop(steps // 2, steps, project_step, 0)
    pass_part(1, 2)
    gather.step(0)
    for i in range(steps):
        span = slice(i * count, (i + 1) * count)
        joined, totals = attend_block(i, (i + 1) * count, heads, sink_ref, q_ref[span], k_ref, v_ref)
        o_ref[span] = joined
        low_ref[span] = joined.astype(bf16)
        lse_ref[span] = totals
        pass_part(1, 2)
        if i == steps // 2:
            gather.step(1)
    put_part(1)
    keep_w = pltpu.make_async_copy(w, w_all, load_s.at[1])
    keep_w.start()

    def out_step(i, carry):
        span = pl.ds(pl.multiple_of(i * count, count), count)
        part[span] = across(low_ref[span], w[:, proj:]).astype(bf16)
        return carry

    lax.fori_loop(0, steps, out_step, 0)
    total.start()
    total.step(0)
    for k in range(1, size // 2):
        if k + 1 < size // 2:
            gather.step(k + 1)
        total.step(k)
    total.finish()
    kept = []
    for k in range(-1, size // 2):
        js = gather.after(k)
        gather.collect(js)
        for j in js:
            slot = gather.slot_of[j]
            copy = pltpu.make_async_copy(dybuf.at[slot], dy_all.at[slot], keep_s.at[slot])
            copy.start()
            kept.append(copy)
    gather.finish()
    for copy in kept + [keep_rows, keep_w]:
        copy.wait()
    for copy in list(sent.values()) + list(crossed.values()):
        copy.wait_send()


def front(sinks, x, wq, kvw, wt, dy, bias, cosine, sine, heads, kv_of, padded, size, ident):
    own, model = x.shape
    length = size * own
    width = heads * HEAD_DIMENSION
    block = (padded, 2 * width + 2 * HEAD_DIMENSION)
    dma = pltpu.SemaphoreType.DMA
    hbm = pl.BlockSpec(memory_space=pl.ANY)
    vmem = pl.BlockSpec(memory_space=pltpu.VMEM)
    return pl.pallas_call(
        functools.partial(front_kernel, size, heads, kv_of),
        out_shape=(
            jax.ShapeDtypeStruct((length, width), bf16),
            jax.ShapeDtypeStruct((length, HEAD_DIMENSION), bf16),
            jax.ShapeDtypeStruct((length, HEAD_DIMENSION), bf16),
            jax.ShapeDtypeStruct((length, width), f32),
            jax.ShapeDtypeStruct((length, width), bf16),
            jax.ShapeDtypeStruct((length, heads), f32),
            jax.ShapeDtypeStruct((length, model), bf16),
            jax.ShapeDtypeStruct((model, block[1]), bf16),
            jax.ShapeDtypeStruct((size, 2 * own, dy.shape[1]), bf16),
            jax.ShapeDtypeStruct((own, model), bf16),
        ),
        in_specs=[pl.BlockSpec(memory_space=pltpu.SMEM), hbm, vmem, vmem, vmem, hbm, vmem, vmem, vmem],
        out_specs=(vmem,) * 6 + (hbm, hbm, hbm, vmem),
        scratch_shapes=[
            pltpu.VMEM((length, model), bf16),
            pltpu.VMEM((size,) + block, bf16),
            pltpu.VMEM((2 * size,) + block, bf16),
            pltpu.VMEM((model, block[1]), bf16),
            pltpu.VMEM((length, model), bf16),
            pltpu.VMEM((size, 2 * own, dy.shape[1]), bf16),
            dma((2, size)),
            dma((2, size)),
            dma((2, size)),
            dma((2, size)),
            dma((2,)),
            dma((size,)),
        ]
        + RingGather.semaphores(size, False)
        + UnitGather.semaphores(size)
        + RingSum.scratch(size, False, own, model, bf16),
        compiler_params=pltpu.CompilerParams(
            collective_id=ident, has_side_effects=True, vmem_limit_bytes=vmem_most
        ),
        name="attend_front",
    )(sinks, x, wq, kvw, wt, dy, bias, cosine, sine)


def rear_kernel(
    size, heads, own_rows, weight_rows,
    sink_ref, act_ref, wd_ref, extra_ref, da_ref, rows_ref, w_ref, q_ref, k_ref, v_ref, o_ref, low_ref, lse_ref,
    cos_ref, sin_ref,
    out_ref, back_ref, g_ref, gain_ref, bias_ref, dsink_ref,
    act, wd, da, w, do, both, dk_acc, dv_acc, back, load_s, keep_s, *scratch,
):
    a = Around(size)
    few = len(RingGather.semaphores(size, False))
    gather = RingGather(a, False, da_ref, da, *scratch[:few])
    total = UnitSum(a, own_rows, act, wd, None, out_ref, scratch[few:], own_rows // 8)
    units = wd_ref.shape[0]
    length, model = da.shape
    width = heads * HEAD_DIMENSION
    proj = width + 2 * HEAD_DIMENSION
    count = 256
    steps = length // count
    blocks = 2 * size
    loads = [
        pltpu.make_async_copy(wd_ref, wd.at[pl.ds(0, units)], load_s.at[0]),
        pltpu.make_async_copy(act_ref, act, load_s.at[1]),
        pltpu.make_async_copy(w_ref, w, load_s.at[2]),
    ]
    greet([a.right, a.left, a.sibling, a.across])
    gather.start()
    for copy in loads:
        copy.start()
    wd[units:] = extra_ref[...]
    dk_acc[...] = jnp.zeros_like(dk_acc)
    dv_acc[...] = jnp.zeros_like(dv_acc)
    dsink_ref[...] = jnp.zeros_like(dsink_ref)
    low_rows = weight_rows // 16 * 16
    g_ref[:, :, low_rows:] = jnp.zeros((2, size, g_ref.shape[2] - low_rows, g_ref.shape[3]), bf16)

    def grad_step(i, carry):
        span = pl.ds(pl.multiple_of(i * count, count), count)
        do[span] = jnp.dot(da[span], w[:, proj:], preferred_element_type=f32).astype(bf16)
        return carry

    def attend_step(i):
        span = slice(i * count, (i + 1) * count)
        dq = attend_back_block(
            i, (i + 1) * count, heads, sink_ref, q_ref[span], k_ref, v_ref, o_ref[span], lse_ref[span], do[span],
            dk_acc, dv_acc, dsink_ref,
        )
        dq = turn(dq, spread(cos_ref[span], width), -spread(sin_ref[span], width))
        both[span, :width] = dq.astype(bf16)

    def back_copy(i):
        span = pl.ds(pl.multiple_of(i * count, count), count)
        return pltpu.make_async_copy(back.at[i % 2], back_ref.at[span], keep_s.at[i % 2])

    def back_step(i, carry):
        @pl.when(i >= 2)
        def _():
            back_copy(i - 2).wait()

        span = pl.ds(pl.multiple_of(i * count, count), count)
        back[i % 2] = across(both[span], w[:, :proj]).astype(bf16)
        back_copy(i).start()
        return carry

    for copy in loads[:2]:
        copy.wait()
    for k in range(size // 2):
        total.make(2 * (k + 1))
        gather.step(k)
    gather.finish()
    total.settle(size - 1)
    total.begin()
    loads[2].wait()
    lax.fori_loop(0, steps, grad_step, 0)
    grad_out = down(da[...], low_ref[...]).astype(bf16)
    again = pltpu.make_async_copy(rows_ref, da, load_s.at[3])
    again.start()
    for i in range(blocks):
        g_ref[lax.rem(i // size + a.seq, 2), i % size, :weight_rows, proj:] = grad_out[i * weight_rows : (i + 1) * weight_rows]
    todo = list(range(steps))
    attend_step(todo.pop())
    for k in range(1, size // 2):
        total.step(k)
        for _ in range(2 if k == 1 else 1):
            if todo:
                attend_step(todo.pop())
                if not todo:
                    turned = turned_back(dk_acc[...], dv_acc[...], cos_ref[...], sin_ref[...])
                    both[:, width:] = turned.astype(bf16)
                    lax.fori_loop(0, steps, back_step, 0)
    bias_ref[...] = jnp.sum(both[...].astype(f32), axis=0, keepdims=True)
    again.wait()
    grad_in = down(da[...], both[...])
    product = grad_in * w[:, :proj].astype(f32)
    high = product.astype(bf16)
    low = (product - high.astype(f32)).astype(bf16)
    ones = jnp.ones((16, proj), bf16)
    gain_ref[...] = (across(ones, high) + across(ones, low))[:1]
    grad_in = grad_in.astype(bf16)
    for i in range(blocks):
        g_ref[lax.rem(i // size + a.seq, 2), i % size, :weight_rows, :proj] = grad_in[i * weight_rows : (i + 1) * weight_rows]
    total.finish()
    for i in range(max(0, steps - 2), steps):
        back_copy(i).wait()


def rear(sinks, act, wd, extra, da, rows, w, q, k, v, o, low, lse, cosine, sine, weight_rows, padded, size, ident):
    length, width = q.shape
    heads = width // HEAD_DIMENSION
    own_rows, model = da.shape
    proj = width + 2 * HEAD_DIMENSION
    dma = pltpu.SemaphoreType.DMA
    hbm = pl.BlockSpec(memory_space=pl.ANY)
    vmem = pl.BlockSpec(memory_space=pltpu.VMEM)
    return pl.pallas_call(
        functools.partial(rear_kernel, size, heads, own_rows, weight_rows),
        out_shape=(
            jax.ShapeDtypeStruct((own_rows, model), bf16),
            jax.ShapeDtypeStruct((length, model), bf16),
            jax.ShapeDtypeStruct((2, size, padded, w.shape[1]), bf16),
            jax.ShapeDtypeStruct((1, model), f32),
            jax.ShapeDtypeStruct((1, proj), f32),
            jax.ShapeDtypeStruct((1, heads), f32),
        ),
        in_specs=[pl.BlockSpec(memory_space=pltpu.SMEM), hbm, hbm, vmem, hbm, hbm, hbm] + [vmem] * 8,
        out_specs=(vmem, hbm, vmem, vmem, vmem, vmem),
        scratch_shapes=[
            pltpu.VMEM(act.shape, bf16),
            pltpu.VMEM((act.shape[0], model), bf16),
            pltpu.VMEM((length, model), bf16),
            pltpu.VMEM(w.shape, bf16),
            pltpu.VMEM((length, width), bf16),
            pltpu.VMEM((length, proj), bf16),
            pltpu.VMEM((length, HEAD_DIMENSION), f32),
            pltpu.VMEM((length, HEAD_DIMENSION), f32),
            pltpu.VMEM((2, 256, model), bf16),
            dma((4,)),
            dma((2,)),
        ]
        + RingGather.semaphores(size, False)
        + UnitSum.scratch(size, own_rows, model, own_rows // 8),
        compiler_params=pltpu.CompilerParams(
            collective_id=ident, has_side_effects=True, vmem_limit_bytes=vmem_most
        ),
        name="attend_rear",
    )(sinks, act, wd, extra, da, rows, w, q, k, v, o, low, lse, cosine, sine)


def rms_norm(row_block, gain_vec):
    return (
        row_block
        * lax.rsqrt(jnp.mean(row_block * row_block, axis=-1, keepdims=True) + rms_eps)
        * gain_vec
    )


def rotary(length):
    half_size = HEAD_DIMENSION // 2
    frequency = rope_base ** (-2.0 * np.arange(half_size) / HEAD_DIMENSION)
    angles = np.arange(length)[:, None] * frequency[None, :]
    cosine, sine = np.cos(angles).astype(np.float32), np.sin(angles).astype(np.float32)
    return (
        jnp.asarray(np.concatenate([cosine] * 4, axis=1)),
        jnp.asarray(np.concatenate([-sine, sine, -sine, sine], axis=1)),
    )


def project_grad(left, right):
    return lax.dot_general(left, right, (((0,), (0,)), ((), ())), preferred_element_type=f32)


def on_device(
    tokens,
    gain_attn,
    w_query,
    b_query,
    key_value_weight,
    key_value_bias,
    sinks,
    w_out,
    b_out,
    gain_moe,
    w_router,
    b_router,
    routes,
    w_gate_up,
    b_gate_up,
    w_down,
    b_down,
    cotangent,
):
    tok_rows, model = tokens.shape
    ctx_size, ctx_rank = lax.axis_size("ctx"), lax.axis_index("ctx")
    seq_size, seq_rank = lax.axis_size("seq"), lax.axis_index("seq")
    tp_size, tp_rank = lax.axis_size("tp"), lax.axis_index("tp")
    local_heads = sinks.shape[0]
    kv_width = key_value_weight.shape[2]
    kv_heads = kv_width // HEAD_DIMENSION
    group = local_heads // kv_heads
    heads = local_heads // ctx_size
    width = heads * HEAD_DIMENSION
    experts = w_router.shape[1]
    weight_rows = w_query.shape[0]
    padded_rows = -(-weight_rows // 16) * 16
    length = ctx_size * tok_rows
    blocks = seq_size * ctx_size
    kernels = (
        seq_size == 2 and tp_size == 2 and tok_rows % 64 == 0
        and 3 * blocks * tok_rows * model * 2 <= vmem_bytes
    )

    kv_of = [(index * heads) // group for index in range(ctx_size)]
    kv_mine = (ctx_rank * heads) // group

    residual = tokens.astype(f32)
    normed_attn, attn_norm_back = jax.vjp(rms_norm, residual, gain_attn)
    normed_low = normed_attn.astype(bf16)
    if kernels:
        kv_cols = key_value_weight.reshape(weight_rows, 2, kv_heads, HEAD_DIMENSION)
        kv_cols = jnp.transpose(kv_cols, (0, 2, 1, 3)).reshape(weight_rows, -1)
    else:
        kv_split = key_value_weight.reshape(weight_rows, 2, kv_heads, HEAD_DIMENSION)
        send = []
        for index in range(ctx_size):
            cols = slice(index * width, (index + 1) * width)
            send.append(
                jnp.concatenate(
                    [
                        w_query[:, cols],
                        kv_split[:, 0, kv_of[index]],
                        kv_split[:, 1, kv_of[index]],
                        w_out[cols].T,
                    ],
                    axis=1,
                )
            )
        send = jnp.pad(jnp.stack(send), ((0, 0), (0, padded_rows - weight_rows), (0, 0)))
        rows_all, weights = plain_enter(normed_low, send)
    proj_width = width + 2 * HEAD_DIMENSION

    cosine, sine = rotary(length)
    bias = jnp.concatenate(
        [
            lax.dynamic_slice_in_dim(b_query, ctx_rank * width, width),
            lax.dynamic_slice_in_dim(key_value_bias[0], kv_mine * HEAD_DIMENSION, HEAD_DIMENSION),
            lax.dynamic_slice_in_dim(key_value_bias[1], kv_mine * HEAD_DIMENSION, HEAD_DIMENSION),
        ]
    )[None]
    sinks_mine = lax.dynamic_slice_in_dim(sinks, ctx_rank * heads, heads)[None]
    if kernels:
        dy_wide = -(-model // 128) * 128
        upstream_low = jnp.pad(cotangent, ((0, 0), (0, dy_wide - model)))
        query, keys, values, attended, attended_low, log_total, rows_all, weights, dy_all, attn_out = front(
            sinks_mine, normed_low, w_query, kv_cols, jnp.transpose(w_out), upstream_low, bias, cosine, sine, heads,
            kv_of, padded_rows, ctx_size, 2,
        )
    else:
        weights = weights[:, :weight_rows].reshape(model, 2 * width + 2 * HEAD_DIMENSION)
        w_in, w_back = weights[:, :proj_width], weights[:, proj_width:]
        query, keys, values = project(rows_all, w_in, bias, cosine, sine, heads)
        attended, attended_low, log_total, out_part = attend(sinks_mine, query, keys, values, w_back)
        attn_out = plain_sum(out_part, "ctx")
    hidden = residual + attn_out.astype(f32) + b_out

    normed_moe, moe_norm_back = jax.vjp(rms_norm, hidden, gain_moe)
    moe_input = normed_moe.astype(bf16)
    logits = jnp.dot(moe_input, w_router, preferred_element_type=f32) + b_router
    onehot = (routes[..., None] == jnp.arange(experts, dtype=jnp.int32)).astype(f32)
    chosen = jnp.sum(onehot * logits[:, None, :], axis=-1)
    gates = jax.nn.softmax(chosen, axis=-1)
    gate_table = jnp.sum(onehot * gates[..., None], axis=1)
    gate_high = lax.reduce_precision(gate_table, 8, 7)
    gate_low = (gate_table - gate_high).astype(bf16)
    wide = -(-(model + 2 * experts) // 128) * 128
    payload = jnp.concatenate(
        [moe_input, gate_high.astype(bf16), gate_low, jnp.zeros((tok_rows, wide - model - 2 * experts), bf16)],
        axis=1,
    )

    gate_up_rows = jnp.transpose(w_gate_up[0], (1, 2, 0)).reshape(-1, model)
    down_weight = w_down[0]
    units = down_weight.shape[0]
    splits = seq_size * tp_size
    lead = ((seq_rank == 0) & (tp_rank == 0)).astype(f32).reshape(1, 1)
    tail = model // 128 * 128
    at = jnp.arange(wide - tail)[None] + tail - model
    pick = ((at == ctx_rank) | (at == experts + ctx_rank)).astype(bf16)
    pick = jnp.concatenate([pick, jnp.zeros((15, wide - tail), bf16)])
    back_wide = -(-(model + 2 * splits * experts) // 128) * 128
    column = 2 * (ctx_rank * splits + seq_rank * tp_size + tp_rank)
    at = jnp.arange(back_wide - tail)[None] + tail - model
    place = jnp.concatenate([at == column, at == column + 1]).astype(bf16)
    place = jnp.concatenate([place, jnp.zeros((14, back_wide - tail), bf16)])

    def expert(rows, upstream):
        return expert_rows(
            lead, rows, upstream, gate_up_rows, b_gate_up[0].reshape(-1, 1), down_weight, b_down, pick, place
        )

    def weight_grads(rows, upstream, gated_act, proj_grad):
        return (
            jnp.dot(proj_grad, rows[:, :model], preferred_element_type=f32),
            jnp.dot(gated_act, upstream, preferred_element_type=f32),
        )

    if kernels:
        moe_all, gated_act, proj_grad, extra_rows, back_rows, gate_bias = expert_all(
            payload, dy_all, gate_up_rows, down_weight, b_gate_up[0].reshape(-1, 1), b_down, experts, back_wide,
            ctx_size, 3,
        )
        count = blocks * tok_rows
        gate_up_grad, down_grad, down_bias = weight_gradients(
            proj_grad, gated_act, moe_all.reshape(count, -1), dy_all.reshape(count, -1), model, units
        )
    else:
        pieces = blocks * tok_rows // math.gcd(blocks * tok_rows, 2048)

        def one_piece(total, packed):
            rows, upstream = (
                lax.all_gather(part, ("seq", "ctx"), axis=0, tiled=True) for part in packed
            )
            expert_part, back_part, gated_act, proj_grad, gate_bias, down_bias = expert(rows, upstream)
            more = weight_grads(rows, upstream, gated_act, proj_grad) + (gate_bias, down_bias)
            total = jax.tree.map(jnp.add, total, more)
            return total, (plain_sum(expert_part, ("seq", "ctx")), plain_sum(back_part, ("seq", "ctx")))

        start = tuple(
            jnp.zeros(shape, f32) for shape in ((2 * units, model), (units, model), (2 * units, 1), (1, model))
        )
        cut = lambda v: v.reshape(pieces, tok_rows // pieces, v.shape[1])
        total, (expert_out_sum, back_rows) = lax.scan(one_piece, start, (cut(payload), cut(cotangent)))
        gate_up_grad, down_grad, gate_bias, down_bias = total
        expert_out_sum, back_rows = (part.reshape(tok_rows, -1) for part in (expert_out_sum, back_rows))
    grad_w_gate_up = jnp.transpose(gate_up_grad.reshape(2, units, model), (2, 0, 1))[None]
    grad_b_gate_up = gate_bias.reshape(1, 2, units)
    grad_w_down = down_grad[None]
    grad_b_down = down_bias
    upstream = cotangent.astype(f32)
    gate_grad = back_rows[:, model : model + 2 * splits * experts].astype(f32)
    gate_grad = jnp.sum(gate_grad.reshape(tok_rows, experts, 2 * splits), axis=-1)
    gate_grad = jnp.sum(onehot * gate_grad[:, None], axis=-1)
    chosen_grad = gates * (gate_grad - jnp.sum(gates * gate_grad, axis=1, keepdims=True))
    logit_grad = jnp.sum(onehot * chosen_grad[..., None], axis=1).astype(bf16)
    grad_w_router = project_grad(logit_grad, moe_input)
    grad_b_router = jnp.sum(logit_grad, axis=0, dtype=f32)
    moe_grad = back_rows[:, :model].astype(f32) + across(logit_grad, w_router)
    hidden_norm_grad, grad_gain_moe = moe_norm_back(moe_grad)
    hidden_grad = upstream + hidden_norm_grad
    branch_grad = hidden_grad.astype(bf16)
    grad_b_out = jnp.sum(branch_grad, axis=0, dtype=f32)
    if kernels:
        expert_out_sum, input_rows, grads, gain_part, bias_part, dsinks = rear(
            sinks_mine, gated_act, down_weight, extra_rows, branch_grad, rows_all, weights, query, keys, values,
            attended, attended_low, log_total, cosine, sine, weight_rows, padded_rows, ctx_size, 5,
        )
        gain_part = gain_part[0] / gain_attn
        sum_q, sum_kv = bias_part[0, :width], bias_part[0, width:].reshape(2, HEAD_DIMENSION)
    else:
        branch_all = lax.all_gather(branch_grad, "ctx", axis=0, tiled=True)
        out_grad = jnp.dot(branch_all, w_back, preferred_element_type=f32).astype(bf16)
        dq, dkv, dsinks = attend_back(
            sinks_mine, query, keys, values, attended, log_total, out_grad, cosine, sine
        )
        both = jnp.concatenate([dq, dkv], axis=1)
        input_rows = spread_rows(both, w_in)
        grad_in = project_grad(rows_all, both)
        grad_out = project_grad(branch_all, attended_low)
        gain_part = jnp.sum(grad_in * w_in.astype(f32), axis=1) / gain_attn
        grads = jnp.concatenate([grad_in, grad_out], axis=1).astype(bf16).reshape(blocks, weight_rows, -1)
        grads = jnp.pad(grads, ((0, 0), (0, padded_rows - weight_rows), (0, 0)))
        sum_q = jnp.sum(dq, axis=0, dtype=f32)
        sum_kv = jnp.sum(dkv, axis=0, dtype=f32).reshape(2, HEAD_DIMENSION)
    mixed = (hidden + expert_out_sum.astype(f32)).astype(bf16)

    at_q = lax.dynamic_update_slice_in_dim(jnp.zeros_like(b_query), sum_q, ctx_rank * width, 0)
    at_kv = lax.dynamic_update_slice_in_dim(
        jnp.zeros_like(key_value_bias), sum_kv, kv_mine * HEAD_DIMENSION, 1
    )
    at_sinks = lax.dynamic_update_slice_in_dim(jnp.zeros_like(sinks), dsinks[0], ctx_rank * heads, 0)
    aligned = lambda n: -(-n // 128) * 128
    late, starts, at = [], [], 0
    for part in (at_q, at_kv.reshape(-1), at_sinks, grad_b_router):
        starts.append(at)
        late.append(jnp.pad(part, (0, aligned(part.shape[0]) - part.shape[0])))
        at += aligned(part.shape[0])
    late = jnp.pad(jnp.concatenate(late), (0, model - at))
    alike = jnp.concatenate([grad_gain_moe[None], grad_b_out[None], grad_w_router], axis=0)
    halves = alike.shape[0] // 2
    if kernels:
        part = lax.dynamic_slice_in_dim(alike, tp_rank * halves, halves)
        small = jnp.concatenate([gain_part[None], late[None], part], axis=0)
        small = jnp.pad(small, ((0, -small.shape[0] % 8), (0, 0)))
        normed_grad, kept, small = leave(input_rows, grads, small, halves, ctx_size, 7)
        owned = lax.all_to_all(kept, "ctx", split_axis=0, concat_axis=0, tiled=True)
        spans = [(0, 0)] + [(1, start) for start in starts] + [(2, 0), (3, 0), (4, 0)]
        shapes = [(1, model)] + [(1, v.size) for v in (at_q, at_kv, at_sinks, grad_b_router)]
        shapes += [(1, model), (1, model), (experts, model)]
        grad_w_query, grad_kv, grad_wt, *sums = settle_gradients(
            owned, small, width, weight_rows, kv_of, spans, shapes
        )
        grad_w_out = jnp.transpose(grad_wt)
        grad_kv = grad_kv.reshape(weight_rows, kv_heads, 2, HEAD_DIMENSION)
        grad_w_key_value = jnp.transpose(grad_kv, (0, 2, 1, 3)).reshape(weight_rows, 2, kv_width)
    else:
        small = jnp.concatenate([gain_part[None], late[None], alike], axis=0)
        normed_grad, owned, small = plain_leave(input_rows, grads, small)
        owned = owned[:, :weight_rows].astype(f32)
        grad_w_query = jnp.transpose(owned[:, :, :width], (1, 0, 2)).reshape(weight_rows, -1)
        grad_kv = owned[:, :, width:proj_width].reshape(kv_heads, -1, weight_rows, 2, HEAD_DIMENSION)
        grad_w_key_value = jnp.transpose(jnp.sum(grad_kv, axis=1), (1, 2, 0, 3)).reshape(
            weight_rows, 2, kv_width
        )
        grad_w_out = jnp.transpose(owned[:, :, proj_width:], (0, 2, 1)).reshape(-1, weight_rows)
        sums = [small[0]]
        sums += [small[1, at : at + v.size] for at, v in zip(starts, (at_q, at_kv, at_sinks, grad_b_router))]
        sums += [small[2], small[3], small[4:]]
    tokens_norm_grad, _ = attn_norm_back(normed_grad.astype(f32))
    grad_tokens = (hidden_grad + tokens_norm_grad).astype(bf16)

    return (
        mixed,
        grad_tokens,
        sums[0].reshape(gain_attn.shape),
        grad_w_query,
        sums[1].reshape(b_query.shape),
        grad_w_key_value,
        sums[2].reshape(key_value_bias.shape),
        sums[3].reshape(sinks.shape),
        grad_w_out,
        sums[6].reshape(b_out.shape),
        sums[5].reshape(gain_moe.shape),
        jnp.transpose(sums[7]),
        sums[4].reshape(b_router.shape),
        grad_w_gate_up,
        grad_b_gate_up,
        grad_w_down,
        grad_b_down,
    )


def solution(mesh):
    in_specs = (
        P(("seq", "ctx"), None),
        P(),
        P(("seq", "ctx"), "tp"),
        P("tp"),
        P(("seq", "ctx"), None, "tp"),
        P(None, "tp"),
        P("tp"),
        P("tp", ("seq", "ctx")),
        P(),
        P(),
        P(),
        P(),
        P(("seq", "ctx"), None),
        P("ctx", None, None, ("seq", "tp")),
        P("ctx", None, ("seq", "tp")),
        P("ctx", ("seq", "tp"), None),
        P("ctx", None),
        P(("seq", "ctx"), None),
    )
    out_specs = (
        P(("seq", "ctx"), None),
        P(("seq", "ctx"), None),
        P(),
        P(("seq", "ctx"), "tp"),
        P("tp"),
        P(("seq", "ctx"), None, "tp"),
        P(None, "tp"),
        P("tp"),
        P("tp", ("seq", "ctx")),
        P(),
        P(),
        P(),
        P(),
        P("ctx", None, None, ("seq", "tp")),
        P("ctx", None, ("seq", "tp")),
        P("ctx", ("seq", "tp"), None),
        P("ctx", None),
    )
    return jax.shard_map(
        on_device, mesh=mesh, in_specs=in_specs, out_specs=out_specs, check_vma=False
    )
```

```python
import functools
import math

import jax
import jax.numpy as jnp
import numpy as np
from jax import lax
from jax.experimental import pallas as pl
from jax.experimental.pallas import tpu as pltpu
from jax.sharding import PartitionSpec as P

HEAD_DIMENSION = 64

rms_eps = 1e-05
rope_base = 150000.0
clamp_limit = 7.0
glu_alpha = 1.702
masked_score = -1e30
vmem_bytes = 56 * 1024 * 1024
vmem_most = 63 * 1024 * 1024
bf16 = jnp.bfloat16
f32 = jnp.float32


def across(left, right):
    return lax.dot_general(left, right, (((1,), (1,)), ((), ())), preferred_element_type=f32)


def down(left, right):
    return lax.dot_general(left, right, (((0,), (0,)), ((), ())), preferred_element_type=f32)


def ring_place(index, size):
    half = index // 2
    return jnp.where(index % 2 == 0, half, size - 1 - half)


def ring_index(place, size):
    place = lax.rem(place + size, size)
    return jnp.where(place < size // 2, 2 * place, 2 * (size - 1 - place) + 1)


def greet(devices):
    barrier = pltpu.get_barrier_semaphore()
    for device in devices:
        pl.semaphore_signal(barrier, inc=1, device_id=device, device_id_type=pl.DeviceIdType.MESH)
    pl.semaphore_wait(barrier, len(devices))


def remote(src, dst, send_sem, recv_sem, device):
    copy = pltpu.make_async_remote_copy(
        src_ref=src,
        dst_ref=dst,
        send_sem=send_sem,
        recv_sem=recv_sem,
        device_id=device,
        device_id_type=pl.DeviceIdType.MESH,
    )
    copy.start()
    return copy


def rows_at(start, count):
    return pl.ds(pl.multiple_of(start, count), count)


class Around:
    def __init__(self, size):
        self.size = size
        self.seq = lax.axis_index("seq")
        self.ctx = lax.axis_index("ctx")
        self.core = lax.axis_index("tp")
        self.place = ring_place(self.ctx, size)
        self.right = (self.seq, ring_index(self.place + 1, size), self.core)
        self.left = (self.seq, ring_index(self.place - 1, size), self.core)
        self.across = (1 - self.seq, self.ctx, self.core)
        self.sibling = (self.seq, self.ctx, 1 - self.core)

    def index(self, offset):
        return ring_index(self.place + offset, self.size)

    def at(self, offset):
        return (self.seq, self.index(offset), self.core)


class RingGather:
    def __init__(self, around, both, x_ref, o_ref, ring_s, ring_r, cross_s, cross_r, core_s, core_r, loc):
        self.a, self.both, self.x, self.o = around, both, x_ref, o_ref
        self.rs, self.rr, self.cs, self.cr = ring_s, ring_r, cross_s, cross_r
        self.ts, self.tr, self.loc = core_s, core_r, loc
        self.rows = x_ref.shape[0]
        self.chunk = self.rows // 4
        size = around.size
        far, near = size // 2, size - 1 - size // 2
        if both:
            self.items = [(1, False, far, near), (0, False, near, far), (0, True, far, near)]
        else:
            self.items = [(0, False, far, near), (1, False, near, far)]

    def partners(self):
        a = self.a
        return [a.right, a.left, a.sibling] + ([a.across] if self.both else [])

    def spot(self, other, index, chunk):
        a = self.a
        if self.both:
            block = (1 - a.seq if other else a.seq) * a.size + index + a.core * 2 * a.size
            return rows_at(block * (2 * self.chunk) + chunk * self.chunk, self.chunk)
        return rows_at(index * self.rows + a.core * (2 * self.chunk) + chunk * self.chunk, self.chunk)

    def own(self, chunk):
        return self.x.at[rows_at(self.a.core * (2 * self.chunk) + chunk * self.chunk, self.chunk)]

    def hop(self, item, way, step, src, where):
        device = self.a.right if way == 0 else self.a.left
        copy = remote(
            src, self.o.at[where], self.rs.at[item, way, step], self.rr.at[item, way, step], device
        )
        self.ring[item, way, step] = copy
        self.sent.append(copy)

    def cross(self, slot, src, where):
        copy = remote(src, self.o.at[where], self.cs.at[slot], self.cr.at[slot], self.a.across)
        self.crossed[slot] = copy
        self.sent.append(copy)

    def share(self, where):
        slot = len(self.shared)
        src = self.o.at[where]
        copy = remote(src, src, self.ts.at[slot], self.tr.at[slot], self.a.sibling)
        self.shared.append(copy)
        self.sent.append(copy)

    def start(self):
        a = self.a
        self.ring, self.crossed, self.shared, self.sent = {}, {}, [], []
        if self.both:
            half = 2 * self.chunk
            block = a.seq * a.size + a.ctx
            pairs = [
                (self.x.at[pl.ds(core * half, half)], rows_at((core * 2 * a.size + block) * half, half))
                for core in range(2)
            ]
        else:
            pairs = [(self.x, rows_at(a.ctx * self.rows, self.rows))]
        self.local = [
            pltpu.make_async_copy(src, self.o.at[where], self.loc.at[at])
            for at, (src, where) in enumerate(pairs)
        ]
        for copy in self.local:
            copy.start()
        if self.both:
            self.cross(0, self.own(0), self.spot(False, a.ctx, 0))
        for item, (chunk, other, _, _) in enumerate(self.items):
            if not other:
                for way in range(2):
                    self.hop(item, way, 0, self.own(chunk), self.spot(False, a.ctx, chunk))
        self.landed = []
        if self.both:
            self.cross(1, self.own(1), self.spot(False, a.ctx, 1))
            self.landed.append((1, a.ctx))
            self.crossed[0].wait_recv()
            where = self.spot(True, a.ctx, 0)
            for way in range(2):
                self.hop(2, way, 0, self.o.at[where], where)
            self.share(where)

    def step(self, k):
        a = self.a
        for item, (chunk, other, right, left) in enumerate(self.items):
            for way, hops in ((0, right), (1, left)):
                if k >= hops:
                    continue
                self.ring[item, way, k].wait_recv()
                index = a.index(-(k + 1) if way == 0 else k + 1)
                where = self.spot(other, index, chunk)
                if k + 1 < hops:
                    self.hop(item, way, k + 1, self.o.at[where], where)
                if self.both and item == 0:
                    slot = 1 + len(self.landed)
                    self.cross(slot, self.o.at[where], where)
                    self.landed.append((slot, index))
                self.share(where)

    def finish(self):
        for slot, index in self.landed:
            self.crossed[slot].wait_recv()
            self.share(self.spot(True, index, 1))
        for copy in self.shared:
            copy.wait_recv()
        for copy in self.sent:
            copy.wait_send()
        for copy in self.local:
            copy.wait()

    @staticmethod
    def semaphores(size, both):
        items = 3 if both else 2
        shares = 2 * (size - 1) + (2 * size if both else 0)
        dma = pltpu.SemaphoreType.DMA
        return [
            dma((items, 2, size // 2)),
            dma((items, 2, size // 2)),
            dma((1 + size,)),
            dma((1 + size,)),
            dma((shares,)),
            dma((shares,)),
            dma((2,)),
        ]


def gather_kernel(size, both, *refs):
    if both:
        x_ref, half_ref, o_ref, whole_ref, held, half_s, half_r, half_l, *sems = refs
    else:
        x_ref, o_ref, *sems = refs
    ring = RingGather(Around(size), both, x_ref, o_ref, *sems)
    greet(ring.partners())
    ring.start()
    if both:
        where = whole_ref.at[rows_at(ring.a.core * half_ref.shape[0], half_ref.shape[0])]
        other = remote(half_ref, where, half_s, half_r, ring.a.sibling)
        here = pltpu.make_async_copy(half_ref, held, half_l.at[0])
        here.start()
        here.wait()
        here = pltpu.make_async_copy(held, where, half_l.at[1])
        here.start()
    for k in range(size // 2):
        ring.step(k)
    ring.finish()
    if both:
        here.wait()
        other.wait()


def ring_gather(x, size, ident, half=None):
    hbm = pl.BlockSpec(memory_space=pl.ANY)
    both = half is not None
    blocks = (2 if both else 1) * size
    shapes = [jax.ShapeDtypeStruct((blocks * x.shape[0], x.shape[1]), x.dtype)]
    if both:
        shapes.append(jax.ShapeDtypeStruct((2 * half.shape[0], half.shape[1]), half.dtype))
    dma = pltpu.SemaphoreType.DMA
    extra = [pltpu.VMEM(half.shape, half.dtype), dma(()), dma(()), dma((2,))] if both else []
    out = pl.pallas_call(
        functools.partial(gather_kernel, size, both),
        out_shape=shapes,
        in_specs=[hbm, hbm] if both else [hbm],
        out_specs=[hbm] * len(shapes),
        scratch_shapes=extra + RingGather.semaphores(size, both),
        compiler_params=pltpu.CompilerParams(
            collective_id=ident, has_side_effects=True, vmem_limit_bytes=vmem_bytes
        ),
        name="gather_all" if both else "gather_ctx",
    )(*((x, half) if both else (x,)))
    return out if both else out[0]


class RingSum:
    def __init__(
        self, around, both, p_ref, o_ref, acc, met, ringbuf, crossbuf, lastbuf,
        ring_s, ring_r, cross_s, cross_r, core_s, core_r, out_s, out_r, loc,
    ):
        self.a, self.both, self.p, self.o = around, both, p_ref, o_ref
        self.acc, self.met, self.ringbuf = acc, met, ringbuf
        self.crossbuf, self.lastbuf = crossbuf, lastbuf
        self.rs, self.rr, self.cs, self.cr = ring_s, ring_r, cross_s, cross_r
        self.ts, self.tr, self.os, self.or_, self.loc = core_s, core_r, out_s, out_r, loc
        self.rows = o_ref.shape[0]
        self.half, self.chunk = self.rows // 2, self.rows // 4
        size = around.size
        far, near = size // 2, size - 1 - size // 2
        if both:
            self.items = [(0, 1, far, near), (0, 0, near, far), (1, 0, far, near)]
        else:
            self.items = [(0, 0, far, near), (1, 0, near, far)]
        order = []
        for d in range(size // 2, 0, -1):
            order += [d] if 2 * d == size else [d, size - d]
        self.order = order + [0]

    def partners(self):
        a = self.a
        return [a.right, a.left, a.sibling] + ([a.across] if self.both else [])

    def spot(self, other, offset, core):
        a = self.a
        block = a.index(offset)
        if self.both:
            block = core * 2 * a.size + (1 - a.seq if other else a.seq) * a.size + block
        else:
            block = 2 * block + core
        return rows_at(block * self.half, self.half)

    def start(self):
        a = self.a
        self.pending, self.sent, self.ring, self.crossed = {}, [], {}, {}
        for other in ((1, 0) if self.both else (0,)):
            for j in self.order:
                away = remote(
                    self.p.at[self.spot(other, j, 1 - a.core)],
                    self.met.at[other, j],
                    self.ts.at[other, j],
                    self.tr.at[other, j],
                    a.sibling,
                )
                here = pltpu.make_async_copy(
                    self.p.at[self.spot(other, j, a.core)], self.acc.at[other, j], self.loc.at[other, j]
                )
                here.start()
                self.pending[other, j] = (away, here)
                self.sent.append(away)
        if self.both:
            for j in self.order:
                self.ready(1, j)
                self.crossed[j] = remote(
                    self.part(self.acc, 1, j, 1), self.crossbuf.at[j], self.cs.at[j], self.cr.at[j], a.across
                )
                self.sent.append(self.crossed[j])

    def part(self, ref, other, j, chunk):
        return ref.at[other, j, pl.ds(chunk * self.chunk, self.chunk)]

    def ready(self, other, j):
        if (other, j) in self.pending:
            away, here = self.pending.pop((other, j))
            away.wait_recv()
            here.wait()
            self.add(self.acc.at[other, j], self.met.at[other, j])

    def add(self, into, more):
        into[...] = (into[...].astype(f32) + more[...].astype(f32)).astype(into.dtype)

    def prepare(self, other, j, chunk):
        self.ready(other, j)
        if self.both and chunk == 1 and j in self.crossed:
            self.crossed.pop(j).wait_recv()
            self.add(self.part(self.acc, 0, j, 1), self.crossbuf.at[j])

    def step(self, k):
        a = self.a
        for item, (chunk, other, right, left) in enumerate(self.items):
            for way, hops in ((0, right), (1, left)):
                d = hops - k
                if d < 1:
                    continue
                j = d if way == 0 else a.size - d
                self.prepare(other, j, chunk)
                block = self.part(self.acc, other, j, chunk)
                if k > 0:
                    self.ring[item, way, d].wait_recv()
                    self.add(block, self.ringbuf.at[item, way, d])
                copy = remote(
                    block,
                    self.ringbuf.at[item, way, d - 1],
                    self.rs.at[item, way, d - 1],
                    self.rr.at[item, way, d - 1],
                    a.right if way == 0 else a.left,
                )
                self.ring[item, way, d - 1] = copy
                self.sent.append(copy)

    def finish(self):
        a = self.a
        last = []
        for item, (chunk, other, _, _) in enumerate(self.items):
            self.prepare(other, 0, chunk)
            block = self.part(self.acc, other, 0, chunk)
            for way in range(2):
                self.ring[item, way, 0].wait_recv()
                self.add(block, self.ringbuf.at[item, way, 0])
            if other:
                slot = a.size
                final = remote(block, self.lastbuf, self.cs.at[slot], self.cr.at[slot], a.across)
                self.sent.append(final)
            else:
                last.append((chunk, block))
        for chunk, block in sorted(last, key=lambda entry: -entry[0]):
            if self.both and chunk == 0:
                final.wait_recv()
                self.add(block, self.lastbuf)
            where = rows_at(a.core * self.half + chunk * self.chunk, self.chunk)
            self.o[where] = block[...]
            copy = remote(
                self.o.at[where], self.o.at[where], self.os.at[chunk], self.or_.at[chunk], a.sibling
            )
            self.sent.append(copy)
            last_copy = copy
            self.outs = getattr(self, "outs", []) + [last_copy]
        for copy in self.outs:
            copy.wait_recv()
        for copy in self.sent:
            copy.wait_send()

    @staticmethod
    def scratch(size, both, rows, width, dtype):
        items = 3 if both else 2
        plane = 2 if both else 1
        half, chunk = rows // 2, rows // 4
        dma = pltpu.SemaphoreType.DMA
        few = size if both else 1
        return [
            pltpu.VMEM((plane, size, half, width), dtype),
            pltpu.VMEM((plane, size, half, width), dtype),
            pltpu.VMEM((items, 2, size // 2, chunk, width), dtype),
            pltpu.VMEM((few, chunk, width), dtype),
            pltpu.VMEM((chunk, width), dtype),
            dma((items, 2, size // 2)),
            dma((items, 2, size // 2)),
            dma((few + 1,)),
            dma((few + 1,)),
            dma((plane, size)),
            dma((plane, size)),
            dma((2,)),
            dma((2,)),
            dma((plane, size)),
        ]


def sum_kernel(size, both, p_ref, o_ref, *scratch):
    ring = RingSum(Around(size), both, p_ref, o_ref, *scratch)
    greet(ring.partners())
    ring.start()
    for k in range(size // 2):
        ring.step(k)
    ring.finish()


def ring_sum(p, size, both, ident):
    blocks = (2 if both else 1) * size
    rows, width = p.shape[0] // blocks, p.shape[1]
    return pl.pallas_call(
        functools.partial(sum_kernel, size, both),
        out_shape=jax.ShapeDtypeStruct((rows, width), p.dtype),
        in_specs=[pl.BlockSpec(memory_space=pl.ANY)],
        out_specs=pl.BlockSpec(memory_space=pltpu.VMEM),
        scratch_shapes=RingSum.scratch(size, both, rows, width, p.dtype),
        compiler_params=pltpu.CompilerParams(
            collective_id=ident, has_side_effects=True, vmem_limit_bytes=vmem_bytes
        ),
        name="sum_all" if both else "sum_ctx",
    )(p)


def leave_kernel(
    size, halves, p_ref, g_ref, v_ref, o_ref, go_ref, vo_ref, gmet, vmet, g_s, g_r, gl, v_s, v_r, *scratch
):
    a = Around(size)
    ring = RingSum(a, False, p_ref, o_ref, *scratch)
    pair = a.ctx + 1 - 2 * (a.ctx % 2)
    peers = [(a.seq, lax.rem(a.ctx + 2 * d, size), a.core) for d in range(1, size // 2)]
    load = pltpu.make_async_copy(g_ref.at[0], go_ref, gl)
    greet([a.right, a.left, a.sibling, a.across, (a.seq, pair, a.core)] + peers)
    swaps = [remote(v_ref, vmet.at[0], v_s.at[0], v_r.at[0], a.across)]
    crossed = [remote(g_ref.at[1, i], gmet.at[i], g_s.at[i], g_r.at[i], a.across) for i in range(size)]
    ring.start()
    load.start()
    last = 3 + size // 2

    def take(first, upto):
        for i in range(first, upto):
            crossed[i].wait_recv()
            ring.add(go_ref.at[i], gmet.at[i])

    for k in range(size // 2):
        ring.step(k)
        if k == 0:
            swaps[0].wait()
            vmet[1] = v_ref[...] + vmet[0]
            swaps = [remote(vmet.at[1], vmet.at[2], v_s.at[1], v_r.at[1], (a.seq, pair, a.core))]
            load.wait()
        elif k == 1:
            swaps[0].wait()
            vmet[3] = vmet[1] + vmet[2]
            swaps = [
                remote(vmet.at[3], vmet.at[3 + d], v_s.at[1 + d], v_r.at[1 + d], peers[d - 1])
                for d in range(1, size // 2)
            ]
        take(2 * k, 2 * k + 1 if k == size // 2 - 1 else 2 * (k + 1))
    for copy in swaps:
        copy.wait()
    total = vmet[3]
    for d in range(1, size // 2):
        total = total + vmet[3 + d]
    vmet[last] = total
    copy = remote(vmet.at[last], vmet.at[last + 1], v_s.at[size // 2 + 1], v_r.at[size // 2 + 1], a.sibling)
    ring.finish()
    take(size - 1, size)
    copy.wait()
    own, other = vmet[last], vmet[last + 1]
    vo_ref[...] = jnp.zeros_like(vo_ref)
    vo_ref[0:1] = own[0:1] + other[0:1]
    vo_ref[1:2] = own[1:2]
    core = lax.broadcasted_iota(jnp.int32, (halves, own.shape[1]), 0) * 0 + a.core
    first, second = own[2 : 2 + halves], other[2 : 2 + halves]
    vo_ref[2 : 2 + halves] = jnp.where(core == 0, first, second)
    vo_ref[2 + halves : 2 + 2 * halves] = jnp.where(core == 0, second, first)
    for copy in crossed:
        copy.wait_send()


def leave(p, g, small, halves, size, ident):
    rows, model = p.shape[0] // size, p.shape[1]
    dma = pltpu.SemaphoreType.DMA
    hbm = pl.BlockSpec(memory_space=pl.ANY)
    vmem = pl.BlockSpec(memory_space=pltpu.VMEM)
    steps = size // 2 + 2
    out_rows = -(-(2 + 2 * halves) // 8) * 8
    return pl.pallas_call(
        functools.partial(leave_kernel, size, halves),
        out_shape=(
            jax.ShapeDtypeStruct((rows, model), p.dtype),
            jax.ShapeDtypeStruct(g.shape[1:], g.dtype),
            jax.ShapeDtypeStruct((out_rows, small.shape[1]), small.dtype),
        ),
        in_specs=[hbm, hbm, vmem],
        out_specs=(vmem, vmem, vmem),
        scratch_shapes=[
            pltpu.VMEM(g.shape[1:], g.dtype),
            pltpu.VMEM((size // 2 + 5,) + small.shape, small.dtype),
            dma((size,)),
            dma((size,)),
            dma(()),
            dma((steps,)),
            dma((steps,)),
        ]
        + RingSum.scratch(size, False, rows, model, p.dtype),
        compiler_params=pltpu.CompilerParams(
            collective_id=ident, has_side_effects=True, vmem_limit_bytes=vmem_bytes
        ),
        name="leave_rows",
    )(p, g, small)


def settle_kernel(width, kv_of, spans, g_ref, v_ref, q_ref, kv_ref, wo_ref, *small_refs):
    proj = width + 2 * HEAD_DIMENSION
    weight_rows = q_ref.shape[0]
    by_head = {}
    for index, head_at in enumerate(kv_of):
        block = g_ref[index, :weight_rows].astype(f32)
        span = slice(index * width, (index + 1) * width)
        q_ref[:, span] = block[:, :width]
        wo_ref[:, span] = block[:, proj:]
        piece = block[:, width:proj]
        by_head[head_at] = by_head[head_at] + piece if head_at in by_head else piece
    for head_at, piece in by_head.items():
        kv_ref[:, head_at * 2 * HEAD_DIMENSION : (head_at + 1) * 2 * HEAD_DIMENSION] = piece
    for ref, (row, start) in zip(small_refs, spans):
        ref[...] = v_ref[row : row + ref.shape[0], start : start + ref.shape[1]]


def settle_gradients(g, v, width, weight_rows, kv_of, spans, shapes):
    kv_wide = (max(kv_of) + 1) * 2 * HEAD_DIMENSION
    large = [(weight_rows, len(kv_of) * width), (weight_rows, kv_wide), (weight_rows, len(kv_of) * width)]
    vmem = pl.BlockSpec(memory_space=pltpu.VMEM)
    return pl.pallas_call(
        functools.partial(settle_kernel, width, kv_of, spans),
        out_shape=[jax.ShapeDtypeStruct(shape, f32) for shape in large + shapes],
        in_specs=[vmem] * 2,
        out_specs=[vmem] * (3 + len(shapes)),
        compiler_params=pltpu.CompilerParams(vmem_limit_bytes=vmem_bytes),
        name="settle_gradients",
    )(g, v)


def plain_enter(x, w):
    rows = lax.all_gather(x, "ctx", axis=0, tiled=True)
    mine = lax.all_to_all(w, "ctx", split_axis=0, concat_axis=0, tiled=True)
    return rows, lax.all_gather(mine, "seq", axis=0, tiled=True)


def plain_sum(p, axes):
    part = lax.psum_scatter(p, axes, scatter_dimension=0, tiled=True)
    return lax.psum(part, "tp")


def plain_leave(p, g, small):
    kept = lax.psum_scatter(g, "seq", scatter_dimension=0, tiled=True)
    owned = lax.all_to_all(kept, "ctx", split_axis=0, concat_axis=0, tiled=True)
    small = jnp.concatenate([lax.psum(small[:1], "tp"), small[1:]])
    return plain_sum(p, "ctx"), owned, lax.psum(small, ("seq", "ctx"))


def expert_kernel(
    units, model, lead_ref, x_ref, dy_ref, wt_ref, bias_ref, wd_ref, bd_ref, pick_ref, place_ref,
    out_ref, back_ref, act_ref, dgu_ref, gbias_ref, dbias_ref,
):
    step = pl.program_id(0)
    tail = model // 128 * 128
    rows = x_ref.shape[0]
    x = x_ref[:, :model]
    dy = dy_ref[...]
    ends = x_ref[:, tail:]
    gate_row = across(pick_ref[...], ends)[:1]
    gate_col = across(ends, pick_ref[...])[:, :1]

    gate = clamp_limit * jnp.tanh((across(wt_ref[:units], x) + bias_ref[:units]) / clamp_limit)
    up = clamp_limit * jnp.tanh((across(wt_ref[units:], x) + bias_ref[units:]) / clamp_limit)
    squash = jax.nn.sigmoid(glu_alpha * gate)
    swish = gate * squash
    act = (up + 1.0) * swish
    out = down(act.astype(bf16), wd_ref[...]) + lead_ref[0, 0] * bd_ref[...]
    out_ref[...] = (gate_col * out).astype(bf16)

    act_grad = across(wd_ref[...], dy)
    high = bd_ref[...].astype(bf16)
    low = (bd_ref[...] - high.astype(f32)).astype(bf16)
    bias_dot = across(jnp.concatenate([high, low] + [jnp.zeros_like(high)] * 14, axis=0), dy)
    gate_grad = jnp.sum(act * act_grad, axis=0, keepdims=True) + lead_ref[0, 0] * (
        bias_dot[0:1] + bias_dot[1:2]
    )
    gate_grad = jnp.where(gate_row > 0, gate_grad, 0.0)
    act_grad = act_grad * gate_row
    slope = 1.0 - (gate / clamp_limit) * (gate / clamp_limit)
    dgate = (
        act_grad * (up + 1.0) * (squash + glu_alpha * swish * (1.0 - squash)) * slope
    ).astype(bf16)
    dup = (act_grad * swish * (1.0 - (up / clamp_limit) * (up / clamp_limit))).astype(bf16)
    act_ref[...] = (act * gate_row).astype(bf16)
    dgu_ref[:units] = dgate
    dgu_ref[units:] = dup

    back = down(dgate, wt_ref[:units]) + down(dup, wt_ref[units:])
    back_ref[:, :model] = back.astype(bf16)
    top = gate_grad.astype(bf16)
    rest = (gate_grad - top.astype(f32)).astype(bf16)
    sent = jnp.concatenate([top, rest] + [jnp.zeros_like(top)] * 14, axis=0)
    ends_out = down(sent, place_ref[...]).astype(bf16)
    back_ref[:, model:] = ends_out[:, model - tail :]

    @pl.when(step == 0)
    def _():
        gbias_ref[...] = jnp.zeros_like(gbias_ref)
        dbias_ref[...] = jnp.zeros_like(dbias_ref)

    gbias_ref[:units] += jnp.sum(dgate.astype(f32), axis=1, keepdims=True)
    gbias_ref[units:] += jnp.sum(dup.astype(f32), axis=1, keepdims=True)
    gate_high = gate_row.astype(bf16)
    gate_low = (gate_row - gate_high.astype(f32)).astype(bf16)
    gates = jnp.concatenate([gate_high, gate_low] + [jnp.zeros_like(gate_high)] * 14, axis=0)
    sums = jnp.dot(gates, dy, preferred_element_type=f32)
    dbias_ref[...] += sums[0:1] + sums[1:2]


def expert_rows(lead, x, dy, wt, bias, wd, bd, pick, place):
    count, wide = x.shape
    model = dy.shape[1]
    units = wd.shape[0]
    rows = min(256, count)
    tail = model // 128 * 128
    back_wide = tail + place.shape[1]
    row = lambda i: (i, 0)
    col = lambda i: (0, i)
    fixed = lambda i: (0, 0)
    whole = lambda v: pl.BlockSpec(v.shape, fixed)
    return pl.pallas_call(
        functools.partial(expert_kernel, units, model),
        grid=(count // rows,),
        out_shape=(
            jax.ShapeDtypeStruct((count, model), bf16),
            jax.ShapeDtypeStruct((count, back_wide), bf16),
            jax.ShapeDtypeStruct((units, count), bf16),
            jax.ShapeDtypeStruct((2 * units, count), bf16),
            jax.ShapeDtypeStruct((2 * units, 1), f32),
            jax.ShapeDtypeStruct((1, model), f32),
        ),
        in_specs=[
            pl.BlockSpec(memory_space=pltpu.SMEM),
            pl.BlockSpec((rows, wide), row),
            pl.BlockSpec((rows, model), row),
            whole(wt),
            whole(bias),
            whole(wd),
            whole(bd),
            whole(pick),
            whole(place),
        ],
        out_specs=(
            pl.BlockSpec((rows, model), row),
            pl.BlockSpec((rows, back_wide), row),
            pl.BlockSpec((units, rows), col),
            pl.BlockSpec((2 * units, rows), col),
            pl.BlockSpec((2 * units, 1), fixed),
            pl.BlockSpec((1, model), fixed),
        ),
        compiler_params=pltpu.CompilerParams(vmem_limit_bytes=vmem_bytes),
        name="expert_rows",
    )(lead, x, dy, wt, bias, wd, bd, pick, place)


def unit_order(size):
    order = [size // 2]
    for d in range(size // 2 - 1, 0, -1):
        order += [d, size - d]
    return order + [0]


def unit_slots(size):
    return {j: slot for slot, j in enumerate(unit_order(size))}


class UnitGather:
    def __init__(self, around, x_ref, buf, sems, first):
        self.a, self.x, self.buf = around, x_ref, buf
        self.own_s, self.ring_s, self.ring_r, self.cross_s, self.cross_r, self.core_s, self.core_r = sems
        self.rows = x_ref.shape[0]
        self.half = self.rows // 2
        self.starts, self.counts = (0, first), (first, self.half - first)
        size = around.size
        far, near = size // 2, size - 1 - size // 2
        self.items = [(1, 0, far, near), (0, 0, near, far), (0, 1, far, near)]
        self.slot_of = unit_slots(size)
        self.sent, self.ring, self.crossed, self.shared = [], {}, {}, {}

    @staticmethod
    def semaphores(size):
        dma = pltpu.SemaphoreType.DMA
        return [
            dma((2,)),
            dma((3, 2, size // 2)),
            dma((3, 2, size // 2)),
            dma((size + 1,)),
            dma((size + 1,)),
            dma((size, 2, 2)),
            dma((size, 2, 2)),
        ]

    def spot(self, j, other, core, piece):
        start = other * self.rows + core * self.half + self.starts[piece]
        return self.buf.at[self.slot_of[j], pl.ds(start, self.counts[piece])]

    def hop(self, item, way, k, src):
        a = self.a
        piece, other, _, _ = self.items[item]
        j = a.size - (k + 1) if way == 0 else k + 1
        copy = remote(
            src, self.spot(j, other, 0, piece), self.ring_s.at[item, way, k], self.ring_r.at[item, way, k],
            a.right if way == 0 else a.left,
        )
        self.ring[item, way, k] = copy
        self.sent.append(copy)

    def cross(self, j, piece, src):
        at = self.slot_of[j] if piece else self.a.size
        copy = remote(src, self.spot(j, 1, 0, piece), self.cross_s.at[at], self.cross_r.at[at], self.a.across)
        self.crossed[j, piece] = copy
        self.sent.append(copy)

    def share(self, j, other, piece):
        at = (self.slot_of[j], other, piece)
        copy = remote(
            self.spot(j, other, 0, piece), self.spot(j, other, 1, piece), self.core_s.at[at],
            self.core_r.at[at], self.a.sibling,
        )
        self.shared[j, other, piece] = copy
        self.sent.append(copy)

    def start(self):
        a, half = self.a, self.half

        def own(core, start, count):
            return self.x.at[pl.ds(pl.multiple_of(core * half + start, 16), count)]

        pieces = [own(a.core, start, count) for start, count in zip(self.starts, self.counts)]
        self.cross(0, 0, pieces[0])
        for item in range(2):
            for way in range(2):
                self.hop(item, way, 0, pieces[self.items[item][0]])
        self.cross(0, 1, pieces[1])
        self.mine = [
            pltpu.make_async_copy(
                own(a.core if here == 0 else 1 - a.core, 0, half),
                self.buf.at[self.slot_of[0], pl.ds(here * half, half)],
                self.own_s.at[here],
            )
            for here in range(2)
        ]
        for copy in self.mine:
            copy.start()

    def first(self):
        self.crossed[0, 0].wait_recv()
        for way in range(2):
            self.hop(2, way, 0, self.spot(0, 1, 0, 0))
        self.share(0, 1, 0)
        self.crossed[0, 1].wait_recv()
        self.share(0, 1, 1)

    def step(self, k):
        size = self.a.size
        for item, (piece, other, right, left) in enumerate(self.items):
            for way, hops in ((0, right), (1, left)):
                if k >= hops:
                    continue
                self.ring[item, way, k].wait_recv()
                j = size - (k + 1) if way == 0 else k + 1
                if k + 1 < hops:
                    self.hop(item, way, k + 1, self.spot(j, other, 0, piece))
                if item == 0:
                    self.cross(j, 1, self.spot(j, 0, 0, 1))
                self.share(j, other, piece)

    def after(self, k):
        if k < 0:
            return [0]
        return [k + 1] if 2 * (k + 1) == self.a.size else [k + 1, self.a.size - (k + 1)]

    def collect(self, js):
        for j in js:
            if j == 0:
                for copy in self.mine:
                    copy.wait()
            else:
                self.crossed[j, 1].wait_recv()
                self.share(j, 1, 1)
        for j in js:
            for key in [(j, 0, 0), (j, 0, 1), (j, 1, 0), (j, 1, 1)]:
                if key in self.shared:
                    self.shared[key].wait_recv()

    def finish(self):
        for copy in self.sent:
            copy.wait_send()


class UnitSum:
    def __init__(self, around, rows, lhs, w, ends, o_ref, scratch, first):
        (
            self.acc, self.own, self.out, self.ringbuf, self.crossbuf, self.lastbuf,
            self.ring_s, self.ring_r, self.cross_s, self.cross_r, self.core_s, self.core_r,
            self.out_s, self.out_r,
        ) = scratch
        self.a, self.rows, self.lhs, self.w, self.ends, self.o = around, rows, lhs, w, ends, o_ref
        self.half = rows // 2
        self.starts, self.counts = (0, first), (first, self.half - first)
        size = around.size
        far, near = size // 2, size - 1 - size // 2
        self.items = [(0, 1, far, near), (0, 0, near, far), (1, 0, far, near)]
        self.slot_of = unit_slots(size)
        self.ring, self.sent, self.joined, self.made = {}, [], set(), 0

    @staticmethod
    def scratch(size, rows, width, first):
        half = rows // 2
        dma = pltpu.SemaphoreType.DMA
        return [
            pltpu.VMEM((2, size, half, width), bf16),
            pltpu.VMEM((2, 2, half, width), bf16),
            pltpu.VMEM((2, 2, half, width), bf16),
            pltpu.VMEM((2, size // 2, half + first, width), bf16),
            pltpu.VMEM((size, half - first, width), bf16),
            pltpu.VMEM((first, width), bf16),
            dma((3, 2, size // 2)),
            dma((3, 2, size // 2)),
            dma((size + 1,)),
            dma((size + 1,)),
            dma((2, size)),
            dma((2, size)),
            dma((2,)),
            dma((2,)),
        ]

    def arrived(self, item, way, d):
        first, second = self.counts
        start, count = ((0, first), (first, first), (2 * first, second))[item]
        return self.ringbuf.at[way, d, pl.ds(start, count)]

    def handed(self, slot, other):
        return pltpu.make_async_remote_copy(
            src_ref=self.out.at[slot % 2, other],
            dst_ref=self.acc.at[other, slot],
            send_sem=self.core_s.at[other, slot],
            recv_sem=self.core_r.at[other, slot],
            device_id=self.a.sibling,
            device_id_type=pl.DeviceIdType.MESH,
        )

    def over(self, slot):
        return pltpu.make_async_remote_copy(
            src_ref=self.acc.at[1, slot, pl.ds(self.starts[1], self.counts[1])],
            dst_ref=self.crossbuf.at[slot],
            send_sem=self.cross_s.at[slot],
            recv_sem=self.cross_r.at[slot],
            device_id=self.a.across,
            device_id_type=pl.DeviceIdType.MESH,
        )

    def add(self, into, more):
        into[...] = (into[...].astype(f32) + more[...].astype(f32)).astype(bf16)

    def settle(self, slot):
        for other in range(2):
            self.handed(slot, other).wait_recv()
            self.add(self.acc.at[other, slot], self.own.at[slot % 2, other])
        self.over(slot).start()

    def produce(self, slot, carry):
        @pl.when(slot >= 2)
        def _():
            for other in range(2):
                self.handed(slot - 2, other).wait_send()

        rows, half = self.rows, self.half
        model = self.w.shape[1]
        columns = pl.ds(pl.multiple_of(slot * 2 * rows, 2 * rows), 2 * rows)
        y = down(self.lhs[:, columns], self.w[...])
        spots = [(other, place, into) for other in range(2) for place, into in ((0, self.own), (half, self.out))]
        for other, place, into in spots:
            start = other * rows + place
            into[slot % 2, other, :, :model] = y[start : start + half].astype(bf16)
        if self.ends is not None:
            dg_ref, place_ref = self.ends
            ends = down(dg_ref[:, columns], place_ref[...])[:, model % 128 :].astype(bf16)
            for other, place, into in spots:
                start = other * rows + place
                into[slot % 2, other, :, model:] = ends[start : start + half]
        for other in range(2):
            self.handed(slot, other).start()

        @pl.when(slot >= 1)
        def _():
            self.settle(slot - 1)

        return carry

    def make(self, upto):
        upto = min(upto, self.a.size)
        if upto > self.made:
            lax.fori_loop(self.made, upto, self.produce, 0)
            self.made = upto

    def part(self, other, j, piece):
        return self.acc.at[other, self.slot_of[j], pl.ds(self.starts[piece], self.counts[piece])]

    def join(self, j):
        if j not in self.joined:
            self.joined.add(j)
            self.over(self.slot_of[j]).wait_recv()
            self.add(self.part(0, j, 1), self.crossbuf.at[self.slot_of[j]])

    def begin(self):
        self.make(2)
        self.leave(0, 0)
        self.make(3)
        self.leave(1, 0)
        self.leave(0, 1)
        self.make(4)
        self.leave(2, 0)
        self.leave(1, 1)
        self.leave(2, 1)

    def leave(self, slot, piece):
        for item, (part, other, right, left) in enumerate(self.items):
            for way, d in ((0, right), (1, left)):
                j = d if way == 0 else self.a.size - d
                if part == piece and self.slot_of[j] == slot:
                    if piece == 1:
                        self.join(j)
                    self.send(item, way, d, self.part(other, j, piece))

    def send(self, item, way, d, block):
        copy = remote(
            block, self.arrived(item, way, d - 1), self.ring_s.at[item, way, d - 1],
            self.ring_r.at[item, way, d - 1], self.a.right if way == 0 else self.a.left,
        )
        self.ring[item, way, d - 1] = copy
        self.sent.append(copy)

    def step(self, k):
        a = self.a
        for item, (piece, other, right, left) in enumerate(self.items):
            for way, hops in ((0, right), (1, left)):
                d = hops - k
                if d < 1:
                    continue
                j = d if way == 0 else a.size - d
                if piece == 1:
                    self.join(j)
                block = self.part(other, j, piece)
                self.ring[item, way, d].wait_recv()
                self.add(block, self.arrived(item, way, d))
                self.send(item, way, d, block)

    def finish(self):
        a, size = self.a, self.a.size
        last = []
        for item, (piece, other, _, _) in enumerate(self.items):
            if piece == 1:
                self.join(0)
            block = self.part(other, 0, piece)
            for way in range(2):
                self.ring[item, way, 0].wait_recv()
                self.add(block, self.arrived(item, way, 0))
            if other:
                final = remote(block, self.lastbuf, self.cross_s.at[size], self.cross_r.at[size], a.across)
                self.sent.append(final)
            else:
                last.append((piece, block))
        outs = []
        for piece, block in sorted(last, key=lambda entry: -entry[0]):
            if piece == 0:
                final.wait_recv()
                self.add(block, self.lastbuf)
            start = pl.multiple_of(a.core * self.half + self.starts[piece], 16)
            where = self.o.at[pl.ds(start, self.counts[piece])]
            where[...] = block[...]
            outs.append(remote(where, where, self.out_s.at[piece], self.out_r.at[piece], a.sibling))
        for copy in outs:
            copy.wait()
        for copy in self.sent:
            copy.wait_send()
        for slot in range(size):
            self.over(slot).wait_send()
        for slot in range(size - 2, size):
            for other in range(2):
                self.handed(slot, other).wait_send()


def expert_kernel_all(
    size, units, model, experts,
    x_ref, dy_all, wt_ref, wd_ref, bias_ref, bd_ref,
    x_all, act_all, dgu_all, extra_all, o_ref, gbias_ref,
    xbuf, dybuf, wt, wd, act_buf, dgu_buf, dg_ref, pick_ref, place_ref, load_s, dy_s, keep_s, *scratch,
):
    a = Around(size)
    tail = model // 128 * 128
    few = len(UnitGather.semaphores(size))
    gather = UnitGather(a, x_ref, xbuf, scratch[:few], x_ref.shape[0] // 8)
    total = UnitSum(
        a, x_ref.shape[0], dgu_buf, wt, (dg_ref, place_ref), o_ref, scratch[few:], x_ref.shape[0] // 4
    )
    lane = lax.broadcasted_iota(jnp.int32, pick_ref.shape, 1) + tail - model
    line = lax.broadcasted_iota(jnp.int32, pick_ref.shape, 0)
    wanted = (lane == a.ctx) | (lane == experts + a.ctx)
    pick_ref[...] = jnp.where((line == 0) & wanted, 1.0, 0.0).astype(bf16)
    lane = lax.broadcasted_iota(jnp.int32, place_ref.shape, 1) + tail - model
    line = lax.broadcasted_iota(jnp.int32, place_ref.shape, 0)
    column = 2 * (4 * a.ctx + 2 * a.seq + a.core)
    place_ref[...] = jnp.where((line < 2) & (lane == column + line), 1.0, 0.0).astype(bf16)
    rows = x_ref.shape[0]
    wide = x_ref.shape[1]
    slot_of = gather.slot_of

    loads = [
        pltpu.make_async_copy(wt_ref, wt, load_s.at[0]),
        pltpu.make_async_copy(wd_ref, wd.at[pl.ds(0, units)], load_s.at[1]),
    ]
    greet([a.right, a.left, a.sibling, a.across])
    gather.start()

    def fetch(js):
        for j in js:
            slot = slot_of[j]
            copy = pltpu.make_async_copy(dy_all.at[slot], dybuf.at[slot % 2], dy_s.at[slot])
            copy.start()
            fetched[j] = copy

    fetched = {}
    for copy in loads:
        copy.start()
    fetch(gather.after(-1))
    lead = jnp.where((a.seq == 0) & (a.core == 0), 1.0, 0.0)
    bias = bd_ref[...] * lead
    bias_high = bias.astype(bf16)
    bias_low = (bias - bias_high.astype(f32)).astype(bf16)
    wd[units:] = jnp.concatenate([bias_high, bias_low, bias_high] + [jnp.zeros_like(bias_high)] * 13, axis=0)
    keep_extra = pltpu.make_async_copy(wd.at[pl.ds(units, 16)], extra_all, load_s.at[2])
    keep_extra.start()
    gbias_ref[...] = jnp.zeros_like(gbias_ref)

    def unit(slot, carry):
        x = xbuf[slot, :, :model]
        dy = dybuf[lax.rem(slot, 2), :, :model]
        ends = xbuf[slot, :, tail:wide]
        columns = pl.ds(pl.multiple_of(slot * 2 * rows, 2 * rows), 2 * rows)
        gate_row = across(pick_ref[...], ends)[:1]
        gate_tanh = jnp.tanh((across(wt[:units], x) + bias_ref[:units]) * (1.0 / clamp_limit))
        up_tanh = jnp.tanh((across(wt[units:], x) + bias_ref[units:]) * (1.0 / clamp_limit))
        squash = 0.5 + 0.5 * jnp.tanh((0.5 * glu_alpha * clamp_limit) * gate_tanh)
        swish = clamp_limit * gate_tanh * squash
        up = clamp_limit * up_tanh + 1.0
        act = up * swish
        act_grad = across(wd[...], dy)
        bias_dot = act_grad[units : units + 1] + act_grad[units + 1 : units + 2]
        act_grad = act_grad[:units]
        gate_grad = jnp.sum(act * act_grad, axis=0, keepdims=True) + bias_dot
        gate_grad = jnp.where(gate_row > 0, gate_grad, 0.0)
        act_grad = act_grad * gate_row
        slope = (squash + glu_alpha * swish * (1.0 - squash)) * (1.0 - gate_tanh * gate_tanh)
        dgate = (act_grad * up * slope).astype(bf16)
        dup = (act_grad * swish * (1.0 - up_tanh * up_tanh)).astype(bf16)
        dgu_buf[:units, columns] = dgate
        dgu_buf[units:, columns] = dup
        gbias_ref[:units] += jnp.sum(dgate.astype(f32), axis=1, keepdims=True)
        gbias_ref[units:] += jnp.sum(dup.astype(f32), axis=1, keepdims=True)
        high = gate_row.astype(bf16)
        low = (gate_row - high.astype(f32)).astype(bf16)
        act_buf[:units, columns] = (act * gate_row).astype(bf16)
        act_buf[units:, columns] = jnp.concatenate([high, high, low] + [jnp.zeros_like(high)] * 13, axis=0)
        top = gate_grad.astype(bf16)
        rest = (gate_grad - top.astype(f32)).astype(bf16)
        dg_ref[:, columns] = jnp.concatenate([top, rest] + [jnp.zeros_like(top)] * 14, axis=0)
        return carry

    kept = []

    def compute(js):
        gather.collect(js)
        for j in js:
            fetched[j].wait()
        slots = [slot_of[j] for j in js]
        lax.fori_loop(slots[0], slots[-1] + 1, unit, 0)
        for slot in slots:
            columns = pl.ds(slot * 2 * rows, 2 * rows)
            for at, (src, dst) in enumerate(
                (
                    (xbuf.at[slot], x_all.at[slot]),
                    (act_buf.at[:, columns], act_all.at[:, columns]),
                    (dgu_buf.at[:, columns], dgu_all.at[:, columns]),
                )
            ):
                kept.append(pltpu.make_async_copy(src, dst, keep_s.at[at, slot]))

    gather.first()
    for copy in loads:
        copy.wait()
    for k in range(size // 2):
        gather.step(k)
        compute(gather.after(k - 1))
        fetch(gather.after(k))
    compute(gather.after(size // 2 - 1))
    total.begin()
    for copy in kept:
        copy.start()
    gather.finish()
    total.make(6)
    for k in range(1, size // 2):
        if k == size // 2 - 1:
            total.settle(size - 1)
        total.step(k)
        total.make(6 + 2 * k)
    total.finish()
    for copy in kept:
        copy.wait()
    keep_extra.wait()


def expert_all(x, dy, wt, wd, bias, bd, experts, width, size, ident):
    rows, wide = x.shape
    units, model = wd.shape
    deep = units + 16
    count = 2 * size * rows
    tail = model // 128 * 128
    dma = pltpu.SemaphoreType.DMA
    hbm = pl.BlockSpec(memory_space=pl.ANY)
    vmem = pl.BlockSpec(memory_space=pltpu.VMEM)
    return pl.pallas_call(
        functools.partial(expert_kernel_all, size, units, model, experts),
        out_shape=(
            jax.ShapeDtypeStruct((size, 2 * rows, wide), bf16),
            jax.ShapeDtypeStruct((deep, count), bf16),
            jax.ShapeDtypeStruct((2 * units, count), bf16),
            jax.ShapeDtypeStruct((16, model), bf16),
            jax.ShapeDtypeStruct((rows, width), bf16),
            jax.ShapeDtypeStruct((2 * units, 1), f32),
        ),
        in_specs=[hbm, hbm, hbm, hbm, vmem, vmem],
        out_specs=(hbm, hbm, hbm, hbm, vmem, vmem),
        scratch_shapes=[
            pltpu.VMEM((size, 2 * rows, wide), bf16),
            pltpu.VMEM((2,) + dy.shape[1:], bf16),
            pltpu.VMEM((2 * units, model), bf16),
            pltpu.VMEM((deep, model), bf16),
            pltpu.VMEM((deep, count), bf16),
            pltpu.VMEM((2 * units, count), bf16),
            pltpu.VMEM((16, count), bf16),
            pltpu.VMEM((16, wide - tail), bf16),
            pltpu.VMEM((16, width - tail), bf16),
            dma((3,)),
            dma((size,)),
            dma((3, size)),
        ]
        + UnitGather.semaphores(size)
        + UnitSum.scratch(size, rows, width, rows // 4),
        compiler_params=pltpu.CompilerParams(
            collective_id=ident, has_side_effects=True, vmem_limit_bytes=vmem_most
        ),
        name="expert_all",
    )(x, dy, wt, wd, bias, bd)


def weights_kernel(model, first_ref, second_ref, x_ref, dy_ref, one_ref, two_ref, extra_ref):
    units = two_ref.shape[0]
    one_ref[...] = jnp.dot(first_ref[...], x_ref[...], preferred_element_type=f32)
    both = jnp.dot(second_ref[...], dy_ref[...], preferred_element_type=f32)
    two_ref[...] = both[:units]
    extra_ref[...] = both[units : units + 1] + both[units + 2 : units + 3]


def weight_gradients(first, second, x, dy, model, units):
    count = x.shape[0]
    cols = 384
    col = lambda i: (0, i)
    fixed = lambda i: (0, 0)
    once = pl.Buffered(1)
    return pl.pallas_call(
        functools.partial(weights_kernel, model),
        grid=(-(-model // cols),),
        out_shape=(
            jax.ShapeDtypeStruct((first.shape[0], model), f32),
            jax.ShapeDtypeStruct((units, model), f32),
            jax.ShapeDtypeStruct((1, model), f32),
        ),
        in_specs=[
            pl.BlockSpec(first.shape, fixed, pipeline_mode=once),
            pl.BlockSpec(second.shape, fixed, pipeline_mode=once),
            pl.BlockSpec((count, cols), col),
            pl.BlockSpec((count, cols), col),
        ],
        out_specs=(
            pl.BlockSpec((first.shape[0], cols), col),
            pl.BlockSpec((units, cols), col),
            pl.BlockSpec((1, cols), col),
        ),
        compiler_params=pltpu.CompilerParams(vmem_limit_bytes=vmem_bytes),
        cost_estimate=pl.CostEstimate(
            flops=2 * count * (first.shape[0] + second.shape[0]) * model,
            bytes_accessed=4 * (first.shape[0] + second.shape[0]) * model + 4 * count * model,
            transcendentals=0,
        ),
        name="weight_gradients",
    )(first, second, x, dy)


def turn(x, cosine, sine):
    half = HEAD_DIMENSION // 2
    width = x.shape[-1]
    if width % 128:
        starts = [start for at in range(0, width, 2 * half) for start in (at + half, at)]
        swapped = jnp.concatenate([x[:, start : start + half] for start in starts], axis=1)
    else:
        lane = lax.broadcasted_iota(jnp.int32, x.shape, 1)
        swapped = jnp.where(
            lane % HEAD_DIMENSION < half, pltpu.roll(x, width - half, 1), pltpu.roll(x, half, 1)
        )
    return x * cosine + swapped * sine


def spread(table, width):
    pieces = [table] * (width // 128) + ([table[:, : width % 128]] if width % 128 else [])
    return jnp.concatenate(pieces, axis=1) if len(pieces) > 1 else pieces[0]


def project_kernel(heads, x_ref, w_ref, b_ref, cos_ref, sin_ref, q_ref, k_ref, v_ref):
    width = heads * HEAD_DIMENSION
    y = jnp.dot(x_ref[...], w_ref[...], preferred_element_type=f32) + b_ref[...]
    cosine, sine = cos_ref[...], sin_ref[...]
    pad = 128
    q_ref[...] = turn(y[:, :width], spread(cosine, width), spread(sine, width)).astype(bf16)
    kv = y[:, width : width + pad]
    k_ref[...] = turn(kv, cosine, sine)[:, :HEAD_DIMENSION].astype(bf16)
    v_ref[...] = kv[:, HEAD_DIMENSION:].astype(bf16)


def project(x, w, bias, cosine, sine, heads):
    length, model = x.shape
    rows = min(256, length)
    width = heads * HEAD_DIMENSION
    row = lambda i: (i, 0)
    fixed = lambda i: (0, 0)
    return pl.pallas_call(
        functools.partial(project_kernel, heads),
        grid=(length // rows,),
        out_shape=(
            jax.ShapeDtypeStruct((length, width), bf16),
            jax.ShapeDtypeStruct((length, HEAD_DIMENSION), bf16),
            jax.ShapeDtypeStruct((length, HEAD_DIMENSION), bf16),
        ),
        in_specs=[
            pl.BlockSpec((rows, model), row),
            pl.BlockSpec(w.shape, fixed),
            pl.BlockSpec(bias.shape, fixed),
            pl.BlockSpec((rows, 128), row),
            pl.BlockSpec((rows, 128), row),
        ],
        out_specs=(
            pl.BlockSpec((rows, width), row),
            pl.BlockSpec((rows, HEAD_DIMENSION), row),
            pl.BlockSpec((rows, HEAD_DIMENSION), row),
        ),
        compiler_params=pltpu.CompilerParams(vmem_limit_bytes=vmem_bytes),
        name="project_rows",
    )(x, w, bias, cosine, sine)


def each_reach(block, rows, length, run):
    classes = min(4, length // rows)
    per = length // rows // classes
    for level in range(classes):
        pl.when(block // per == level)(functools.partial(run, (level + 1) * per * rows))


def attend_block(block, reach, heads, sink_ref, q, k_ref, v_ref):
    rows = q.shape[0]
    scale = 1.0 / math.sqrt(HEAD_DIMENSION)
    keys, values = k_ref[:reach], v_ref[:reach]
    row = block * rows + lax.broadcasted_iota(jnp.int32, (rows, reach), 0)
    allowed = lax.broadcasted_iota(jnp.int32, (rows, reach), 1) <= row
    outs, totals = [], []
    for head in range(heads):
        query = q[:, head * HEAD_DIMENSION : (head + 1) * HEAD_DIMENSION]
        scores = jnp.where(allowed, across(query, keys) * scale, masked_score)
        sink = sink_ref[0, head]
        top = jnp.maximum(jnp.max(scores, axis=1, keepdims=True), sink)
        weights = jnp.exp(scores - top)
        total = jnp.sum(weights, axis=1, keepdims=True) + jnp.exp(sink - top)
        mixed = jnp.dot(weights.astype(bf16), values, preferred_element_type=f32)
        outs.append(mixed / total)
        totals.append(top + jnp.log(total))
    return jnp.concatenate(outs, axis=1), jnp.concatenate(totals, axis=1)


def attend_kernel(heads, length, sink_ref, q_ref, k_ref, v_ref, w_ref, o_ref, low_ref, lse_ref, p_ref):
    rows = q_ref.shape[0]
    block = pl.program_id(0)

    def run(reach):
        joined, totals = attend_block(block, reach, heads, sink_ref, q_ref[...], k_ref, v_ref)
        o_ref[...] = joined
        joined_low = joined.astype(bf16)
        low_ref[...] = joined_low
        p_ref[...] = across(joined_low, w_ref[...]).astype(bf16)
        lse_ref[...] = totals

    each_reach(block, rows, length, run)


def attend(sinks, q, k, v, w):
    length, width = q.shape
    model = w.shape[0]
    heads = width // HEAD_DIMENSION
    rows = min(256, length)
    row = lambda i: (i, 0)
    fixed = lambda i: (0, 0)
    return pl.pallas_call(
        functools.partial(attend_kernel, heads, length),
        grid=(length // rows,),
        out_shape=(
            jax.ShapeDtypeStruct((length, width), f32),
            jax.ShapeDtypeStruct((length, width), bf16),
            jax.ShapeDtypeStruct((length, heads), f32),
            jax.ShapeDtypeStruct((length, model), bf16),
        ),
        in_specs=[
            pl.BlockSpec(memory_space=pltpu.SMEM),
            pl.BlockSpec((rows, width), row),
            pl.BlockSpec(k.shape, fixed),
            pl.BlockSpec(v.shape, fixed),
            pl.BlockSpec(w.shape, fixed),
        ],
        out_specs=(
            pl.BlockSpec((rows, width), row),
            pl.BlockSpec((rows, width), row),
            pl.BlockSpec((rows, heads), row),
            pl.BlockSpec((rows, model), row),
        ),
        compiler_params=pltpu.CompilerParams(vmem_limit_bytes=vmem_bytes),
        name="attend_rows",
    )(sinks, q, k, v, w)


def spread_kernel(x_ref, w_ref, o_ref):
    o_ref[...] = across(x_ref[...], w_ref[...]).astype(o_ref.dtype)


def spread_rows(x, w):
    count, width = x.shape
    rows = min(256, count)
    return pl.pallas_call(
        spread_kernel,
        grid=(count // rows,),
        out_shape=jax.ShapeDtypeStruct((count, w.shape[0]), bf16),
        in_specs=[
            pl.BlockSpec((rows, width), lambda i: (i, 0)),
            pl.BlockSpec(w.shape, lambda i: (0, 0)),
        ],
        out_specs=pl.BlockSpec((rows, w.shape[0]), lambda i: (i, 0)),
        compiler_params=pltpu.CompilerParams(vmem_limit_bytes=vmem_bytes),
        name="spread_rows",
    )(x, w)


def attend_back_block(block, reach, heads, sink_ref, q, k_ref, v_ref, o, lses, do, dk_acc, dv_acc, sink_acc):
    rows = q.shape[0]
    scale = 1.0 / math.sqrt(HEAD_DIMENSION)
    keys, values = k_ref[:reach], v_ref[:reach]
    row = block * rows + lax.broadcasted_iota(jnp.int32, (rows, reach), 0)
    allowed = lax.broadcasted_iota(jnp.int32, (rows, reach), 1) <= row
    parts, sink_parts = [], []
    key_sum = jnp.zeros((reach, HEAD_DIMENSION), f32)
    value_sum = jnp.zeros((reach, HEAD_DIMENSION), f32)
    for head in range(heads):
        span = slice(head * HEAD_DIMENSION, (head + 1) * HEAD_DIMENSION)
        query, grad = q[:, span], do[:, span]
        lse = lses[:, head : head + 1]
        delta = jnp.sum(grad.astype(f32) * o[:, span], axis=1, keepdims=True)
        scores = jnp.where(allowed, across(query, keys) * scale, masked_score)
        probs = jnp.exp(scores - lse)
        value_sum = value_sum + down(probs.astype(bf16), grad)
        score_grad = (probs * (across(grad, values) - delta)).astype(bf16)
        parts.append(jnp.dot(score_grad, keys, preferred_element_type=f32) * scale)
        key_sum = key_sum + down(score_grad, query)
        share = jnp.exp(sink_ref[0, head] - lse) * delta
        sink_parts.append(jnp.sum(share, axis=0, keepdims=True))
    dk_acc[:reach] += key_sum * scale
    dv_acc[:reach] += value_sum
    sink_acc[...] -= jnp.concatenate(sink_parts, axis=1)
    return jnp.concatenate(parts, axis=1)


def turned_back(dk, dv, cosine, sine):
    both = jnp.concatenate([dk, dv], axis=1)
    turned = turn(both, cosine, -sine)
    lane = lax.broadcasted_iota(jnp.int32, both.shape, 1)
    return jnp.where(lane < HEAD_DIMENSION, turned, both)


def attend_back_kernel(
    heads, length, sink_ref, q_ref, k_ref, v_ref, o_ref, lse_ref, do_ref, cos_ref, sin_ref,
    kcos_ref, ksin_ref, dq_ref, dkv_ref, dsink_ref, dk_acc, dv_acc, sink_acc,
):
    rows = q_ref.shape[0]
    block = pl.program_id(0)

    @pl.when(block == 0)
    def _():
        dk_acc[...] = jnp.zeros_like(dk_acc)
        dv_acc[...] = jnp.zeros_like(dv_acc)
        sink_acc[...] = jnp.zeros_like(sink_acc)

    def run(reach):
        dq = attend_back_block(
            block, reach, heads, sink_ref, q_ref[...], k_ref, v_ref, o_ref[...], lse_ref[...], do_ref[...],
            dk_acc, dv_acc, sink_acc,
        )
        wide = dq.shape[1]
        dq_ref[...] = turn(dq, spread(cos_ref[...], wide), -spread(sin_ref[...], wide)).astype(bf16)

    each_reach(block, rows, length, run)

    @pl.when(block == pl.num_programs(0) - 1)
    def _():
        dkv_ref[...] = turned_back(dk_acc[...], dv_acc[...], kcos_ref[...], ksin_ref[...]).astype(bf16)
        dsink_ref[...] = sink_acc[...]


def attend_back(sinks, q, k, v, o, lse, do, cosine, sine):
    length, width = q.shape
    heads = width // HEAD_DIMENSION
    rows = min(256, length)
    row = lambda i: (i, 0)
    fixed = lambda i: (0, 0)
    return pl.pallas_call(
        functools.partial(attend_back_kernel, heads, length),
        grid=(length // rows,),
        out_shape=(
            jax.ShapeDtypeStruct((length, width), bf16),
            jax.ShapeDtypeStruct((length, 2 * HEAD_DIMENSION), bf16),
            jax.ShapeDtypeStruct((1, heads), f32),
        ),
        in_specs=[
            pl.BlockSpec(memory_space=pltpu.SMEM),
            pl.BlockSpec((rows, width), row),
            pl.BlockSpec(k.shape, fixed),
            pl.BlockSpec(v.shape, fixed),
            pl.BlockSpec((rows, width), row),
            pl.BlockSpec((rows, heads), row),
            pl.BlockSpec((rows, width), row),
            pl.BlockSpec((rows, 128), row),
            pl.BlockSpec((rows, 128), row),
            pl.BlockSpec((length, 128), fixed),
            pl.BlockSpec((length, 128), fixed),
        ],
        out_specs=(
            pl.BlockSpec((rows, width), row),
            pl.BlockSpec((length, 2 * HEAD_DIMENSION), fixed),
            pl.BlockSpec((1, heads), fixed),
        ),
        scratch_shapes=[
            pltpu.VMEM((length, HEAD_DIMENSION), f32),
            pltpu.VMEM((length, HEAD_DIMENSION), f32),
            pltpu.VMEM((1, heads), f32),
        ],
        compiler_params=pltpu.CompilerParams(vmem_limit_bytes=vmem_bytes),
        name="attend_rows_back",
    )(sinks, q, k, v, o, lse, do, cosine, sine, cosine, sine)


def front_kernel(
    size, heads, kv_of,
    sink_ref, x_ref, wq_ref, kvw_ref, wt_ref, dy_ref, bias_ref, cos_ref, sin_ref,
    q_ref, k_ref, v_ref, o_ref, low_ref, lse_ref, rows_all, w_all, dy_all, out_ref,
    rows, send, blocks, w, part, dybuf, w_s, w_r, wx_s, wx_r, load_s, keep_s, *scratch,
):
    a = Around(size)
    one, two = len(RingGather.semaphores(size, False)), len(UnitGather.semaphores(size))
    ring = RingGather(a, False, x_ref, rows, *scratch[:one])
    gather = UnitGather(a, dy_ref, dybuf, scratch[one : one + two], dy_ref.shape[0] // 8)
    total = RingSum(a, False, part, out_ref, *scratch[one + two :])
    length, model = rows.shape
    weight_rows = wq_ref.shape[0]
    width = heads * HEAD_DIMENSION
    proj = width + 2 * HEAD_DIMENSION
    count = 256
    steps = length // count
    order = []
    for d in range(1, size // 2 + 1):
        order += [d] if 2 * d == size else [d, size - d]
    greet(ring.partners() + [a.across] + [a.at(d) for d in order if 1 < d < size - 1])
    ring.start()

    whole = weight_rows // 16 * 16
    send[:, whole:] = jnp.zeros((size, send.shape[1] - whole, send.shape[2]), bf16)
    for index in range(size):
        span = slice(index * width, (index + 1) * width)
        at = kv_of[index] * 2 * HEAD_DIMENSION
        send[index, :weight_rows, :width] = wq_ref[:, span]
        send[index, :weight_rows, width:proj] = kvw_ref[:, at : at + 2 * HEAD_DIMENSION]
        send[index, :weight_rows, proj:] = wt_ref[:, span]
    mine = a.seq * size + a.ctx
    spans = (pl.ds(0, proj), pl.ds(proj, width))
    sent, crossed = {}, {}

    def start_part(h):
        src = send.at[a.ctx, :, spans[h]]
        crossed[h, 0] = remote(src, blocks.at[mine, :, spans[h]], wx_s.at[h, 0], wx_r.at[h, 0], a.across)
        for d in order:
            src = send.at[a.index(d), :, spans[h]]
            sent[h, d] = remote(src, blocks.at[mine, :, spans[h]], w_s.at[h, d], w_r.at[h, d], a.at(d))

    def pass_part(h, times):
        for d in order:
            if (h, d) not in crossed and times > 0:
                sent[h, d].wait_recv()
                block = blocks.at[a.seq * size + a.index(-d), :, spans[h]]
                crossed[h, d] = remote(block, block, wx_s.at[h, d], wx_r.at[h, d], a.across)
                times -= 1

    def put_part(h):
        pass_part(h, size)
        for d in [0] + order:
            crossed[h, d].wait_recv()
        columns = slice(0, proj) if h == 0 else slice(proj, proj + width)
        for i in range(2 * size):
            w[i * weight_rows : (i + 1) * weight_rows, columns] = blocks[i, :weight_rows, columns]

    start_part(0)
    blocks[mine] = send[a.ctx]
    for k in range(size // 2):
        ring.step(k)
        pass_part(0, 2)
    start_part(1)
    ring.finish()
    gather.start()
    keep_rows = pltpu.make_async_copy(rows, rows_all, load_s.at[0])
    keep_rows.start()
    put_part(0)

    def project_step(i, carry):
        span = pl.ds(pl.multiple_of(i * count, count), count)
        y = jnp.dot(rows[span], w[:, :proj], preferred_element_type=f32) + bias_ref[...]
        cosine, sine = cos_ref[span], sin_ref[span]
        q_ref[span] = turn(y[:, :width], spread(cosine, width), spread(sine, width)).astype(bf16)
        kv = y[:, width:]
        k_ref[span] = turn(kv, cosine, sine)[:, :HEAD_DIMENSION].astype(bf16)
        v_ref[span] = kv[:, HEAD_DIMENSION:].astype(bf16)
        return carry

    lax.fori_loop(0, steps // 2, project_step, 0)
    gather.first()
    pass_part(1, 2)
    lax.fori_loop(steps // 2, steps, project_step, 0)
    pass_part(1, 2)
    gather.step(0)
    for i in range(steps):
        span = slice(i * count, (i + 1) * count)
        joined, totals = attend_block(i, (i + 1) * count, heads, sink_ref, q_ref[span], k_ref, v_ref)
        o_ref[span] = joined
        low_ref[span] = joined.astype(bf16)
        lse_ref[span] = totals
        pass_part(1, 2)
        if i == steps // 2:
            gather.step(1)
    put_part(1)
    keep_w = pltpu.make_async_copy(w, w_all, load_s.at[1])
    keep_w.start()

    def out_step(i, carry):
        span = pl.ds(pl.multiple_of(i * count, count), count)
        part[span] = across(low_ref[span], w[:, proj:]).astype(bf16)
        return carry

    lax.fori_loop(0, steps, out_step, 0)
    total.start()
    total.step(0)
    for k in range(1, size // 2):
        if k + 1 < size // 2:
            gather.step(k + 1)
        total.step(k)
    total.finish()
    kept = []
    for k in range(-1, size // 2):
        js = gather.after(k)
        gather.collect(js)
        for j in js:
            slot = gather.slot_of[j]
            copy = pltpu.make_async_copy(dybuf.at[slot], dy_all.at[slot], keep_s.at[slot])
            copy.start()
            kept.append(copy)
    gather.finish()
    for copy in kept + [keep_rows, keep_w]:
        copy.wait()
    for copy in list(sent.values()) + list(crossed.values()):
        copy.wait_send()


def front(sinks, x, wq, kvw, wt, dy, bias, cosine, sine, heads, kv_of, padded, size, ident):
    own, model = x.shape
    length = size * own
    width = heads * HEAD_DIMENSION
    block = (padded, 2 * width + 2 * HEAD_DIMENSION)
    dma = pltpu.SemaphoreType.DMA
    hbm = pl.BlockSpec(memory_space=pl.ANY)
    vmem = pl.BlockSpec(memory_space=pltpu.VMEM)
    return pl.pallas_call(
        functools.partial(front_kernel, size, heads, kv_of),
        out_shape=(
            jax.ShapeDtypeStruct((length, width), bf16),
            jax.ShapeDtypeStruct((length, HEAD_DIMENSION), bf16),
            jax.ShapeDtypeStruct((length, HEAD_DIMENSION), bf16),
            jax.ShapeDtypeStruct((length, width), f32),
            jax.ShapeDtypeStruct((length, width), bf16),
            jax.ShapeDtypeStruct((length, heads), f32),
            jax.ShapeDtypeStruct((length, model), bf16),
            jax.ShapeDtypeStruct((model, block[1]), bf16),
            jax.ShapeDtypeStruct((size, 2 * own, dy.shape[1]), bf16),
            jax.ShapeDtypeStruct((own, model), bf16),
        ),
        in_specs=[pl.BlockSpec(memory_space=pltpu.SMEM), hbm, vmem, vmem, vmem, hbm, vmem, vmem, vmem],
        out_specs=(vmem,) * 6 + (hbm, hbm, hbm, vmem),
        scratch_shapes=[
            pltpu.VMEM((length, model), bf16),
            pltpu.VMEM((size,) + block, bf16),
            pltpu.VMEM((2 * size,) + block, bf16),
            pltpu.VMEM((model, block[1]), bf16),
            pltpu.VMEM((length, model), bf16),
            pltpu.VMEM((size, 2 * own, dy.shape[1]), bf16),
            dma((2, size)),
            dma((2, size)),
            dma((2, size)),
            dma((2, size)),
            dma((2,)),
            dma((size,)),
        ]
        + RingGather.semaphores(size, False)
        + UnitGather.semaphores(size)
        + RingSum.scratch(size, False, own, model, bf16),
        compiler_params=pltpu.CompilerParams(
            collective_id=ident, has_side_effects=True, vmem_limit_bytes=vmem_most
        ),
        name="attend_front",
    )(sinks, x, wq, kvw, wt, dy, bias, cosine, sine)


def rear_kernel(
    size, heads, own_rows, weight_rows,
    sink_ref, act_ref, wd_ref, extra_ref, da_ref, rows_ref, w_ref, q_ref, k_ref, v_ref, o_ref, low_ref, lse_ref,
    cos_ref, sin_ref,
    out_ref, back_ref, g_ref, gain_ref, bias_ref, dsink_ref,
    act, wd, da, w, do, both, dk_acc, dv_acc, back, load_s, keep_s, *scratch,
):
    a = Around(size)
    few = len(RingGather.semaphores(size, False))
    gather = RingGather(a, False, da_ref, da, *scratch[:few])
    total = UnitSum(a, own_rows, act, wd, None, out_ref, scratch[few:], own_rows // 8)
    units = wd_ref.shape[0]
    length, model = da.shape
    width = heads * HEAD_DIMENSION
    proj = width + 2 * HEAD_DIMENSION
    count = 256
    steps = length // count
    blocks = 2 * size
    loads = [
        pltpu.make_async_copy(wd_ref, wd.at[pl.ds(0, units)], load_s.at[0]),
        pltpu.make_async_copy(act_ref, act, load_s.at[1]),
        pltpu.make_async_copy(w_ref, w, load_s.at[2]),
    ]
    greet([a.right, a.left, a.sibling, a.across])
    gather.start()
    for copy in loads:
        copy.start()
    wd[units:] = extra_ref[...]
    dk_acc[...] = jnp.zeros_like(dk_acc)
    dv_acc[...] = jnp.zeros_like(dv_acc)
    dsink_ref[...] = jnp.zeros_like(dsink_ref)
    low_rows = weight_rows // 16 * 16
    g_ref[:, :, low_rows:] = jnp.zeros((2, size, g_ref.shape[2] - low_rows, g_ref.shape[3]), bf16)

    def grad_step(i, carry):
        span = pl.ds(pl.multiple_of(i * count, count), count)
        do[span] = jnp.dot(da[span], w[:, proj:], preferred_element_type=f32).astype(bf16)
        return carry

    def attend_step(i):
        span = slice(i * count, (i + 1) * count)
        dq = attend_back_block(
            i, (i + 1) * count, heads, sink_ref, q_ref[span], k_ref, v_ref, o_ref[span], lse_ref[span], do[span],
            dk_acc, dv_acc, dsink_ref,
        )
        dq = turn(dq, spread(cos_ref[span], width), -spread(sin_ref[span], width))
        both[span, :width] = dq.astype(bf16)

    def back_copy(i):
        span = pl.ds(pl.multiple_of(i * count, count), count)
        return pltpu.make_async_copy(back.at[i % 2], back_ref.at[span], keep_s.at[i % 2])

    def back_step(i, carry):
        @pl.when(i >= 2)
        def _():
            back_copy(i - 2).wait()

        span = pl.ds(pl.multiple_of(i * count, count), count)
        back[i % 2] = across(both[span], w[:, :proj]).astype(bf16)
        back_copy(i).start()
        return carry

    for copy in loads[:2]:
        copy.wait()
    for k in range(size // 2):
        total.make(2 * (k + 1))
        gather.step(k)
        if k == size // 2 - 2:
            total.begin()
    gather.finish()
    total.settle(size - 1)
    loads[2].wait()
    lax.fori_loop(0, steps, grad_step, 0)
    grad_out = down(da[...], low_ref[...]).astype(bf16)
    again = pltpu.make_async_copy(rows_ref, da, load_s.at[3])
    again.start()
    for i in range(blocks):
        g_ref[lax.rem(i // size + a.seq, 2), i % size, :weight_rows, proj:] = grad_out[i * weight_rows : (i + 1) * weight_rows]
    todo = list(range(steps))
    attend_step(todo.pop())
    for k in range(1, size // 2):
        total.step(k)
        for _ in range(2 if k == 1 else 1):
            if todo:
                attend_step(todo.pop())
                if not todo:
                    turned = turned_back(dk_acc[...], dv_acc[...], cos_ref[...], sin_ref[...])
                    both[:, width:] = turned.astype(bf16)
                    lax.fori_loop(0, steps, back_step, 0)
    bias_ref[...] = jnp.sum(both[...].astype(f32), axis=0, keepdims=True)
    again.wait()
    grad_in = down(da[...], both[...])
    product = grad_in * w[:, :proj].astype(f32)
    high = product.astype(bf16)
    low = (product - high.astype(f32)).astype(bf16)
    ones = jnp.ones((16, proj), bf16)
    gain_ref[...] = (across(ones, high) + across(ones, low))[:1]
    grad_in = grad_in.astype(bf16)
    for i in range(blocks):
        g_ref[lax.rem(i // size + a.seq, 2), i % size, :weight_rows, :proj] = grad_in[i * weight_rows : (i + 1) * weight_rows]
    total.finish()
    for i in range(max(0, steps - 2), steps):
        back_copy(i).wait()


def rear(sinks, act, wd, extra, da, rows, w, q, k, v, o, low, lse, cosine, sine, weight_rows, padded, size, ident):
    length, width = q.shape
    heads = width // HEAD_DIMENSION
    own_rows, model = da.shape
    proj = width + 2 * HEAD_DIMENSION
    dma = pltpu.SemaphoreType.DMA
    hbm = pl.BlockSpec(memory_space=pl.ANY)
    vmem = pl.BlockSpec(memory_space=pltpu.VMEM)
    return pl.pallas_call(
        functools.partial(rear_kernel, size, heads, own_rows, weight_rows),
        out_shape=(
            jax.ShapeDtypeStruct((own_rows, model), bf16),
            jax.ShapeDtypeStruct((length, model), bf16),
            jax.ShapeDtypeStruct((2, size, padded, w.shape[1]), bf16),
            jax.ShapeDtypeStruct((1, model), f32),
            jax.ShapeDtypeStruct((1, proj), f32),
            jax.ShapeDtypeStruct((1, heads), f32),
        ),
        in_specs=[pl.BlockSpec(memory_space=pltpu.SMEM), hbm, hbm, vmem, hbm, hbm, hbm] + [vmem] * 8,
        out_specs=(vmem, hbm, vmem, vmem, vmem, vmem),
        scratch_shapes=[
            pltpu.VMEM(act.shape, bf16),
            pltpu.VMEM((act.shape[0], model), bf16),
            pltpu.VMEM((length, model), bf16),
            pltpu.VMEM(w.shape, bf16),
            pltpu.VMEM((length, width), bf16),
            pltpu.VMEM((length, proj), bf16),
            pltpu.VMEM((length, HEAD_DIMENSION), f32),
            pltpu.VMEM((length, HEAD_DIMENSION), f32),
            pltpu.VMEM((2, 256, model), bf16),
            dma((4,)),
            dma((2,)),
        ]
        + RingGather.semaphores(size, False)
        + UnitSum.scratch(size, own_rows, model, own_rows // 8),
        compiler_params=pltpu.CompilerParams(
            collective_id=ident, has_side_effects=True, vmem_limit_bytes=vmem_most
        ),
        name="attend_rear",
    )(sinks, act, wd, extra, da, rows, w, q, k, v, o, low, lse, cosine, sine)


def rms_norm(row_block, gain_vec):
    return (
        row_block
        * lax.rsqrt(jnp.mean(row_block * row_block, axis=-1, keepdims=True) + rms_eps)
        * gain_vec
    )


def rotary(length):
    half_size = HEAD_DIMENSION // 2
    frequency = rope_base ** (-2.0 * np.arange(half_size) / HEAD_DIMENSION)
    angles = np.arange(length)[:, None] * frequency[None, :]
    cosine, sine = np.cos(angles).astype(np.float32), np.sin(angles).astype(np.float32)
    return (
        jnp.asarray(np.concatenate([cosine] * 4, axis=1)),
        jnp.asarray(np.concatenate([-sine, sine, -sine, sine], axis=1)),
    )


def project_grad(left, right):
    return lax.dot_general(left, right, (((0,), (0,)), ((), ())), preferred_element_type=f32)


def on_device(
    tokens,
    gain_attn,
    w_query,
    b_query,
    key_value_weight,
    key_value_bias,
    sinks,
    w_out,
    b_out,
    gain_moe,
    w_router,
    b_router,
    routes,
    w_gate_up,
    b_gate_up,
    w_down,
    b_down,
    cotangent,
):
    tok_rows, model = tokens.shape
    ctx_size, ctx_rank = lax.axis_size("ctx"), lax.axis_index("ctx")
    seq_size, seq_rank = lax.axis_size("seq"), lax.axis_index("seq")
    tp_size, tp_rank = lax.axis_size("tp"), lax.axis_index("tp")
    local_heads = sinks.shape[0]
    kv_width = key_value_weight.shape[2]
    kv_heads = kv_width // HEAD_DIMENSION
    group = local_heads // kv_heads
    heads = local_heads // ctx_size
    width = heads * HEAD_DIMENSION
    experts = w_router.shape[1]
    weight_rows = w_query.shape[0]
    padded_rows = -(-weight_rows // 16) * 16
    length = ctx_size * tok_rows
    blocks = seq_size * ctx_size
    kernels = (
        seq_size == 2 and tp_size == 2 and tok_rows % 64 == 0
        and 3 * blocks * tok_rows * model * 2 <= vmem_bytes
    )

    kv_of = [(index * heads) // group for index in range(ctx_size)]
    kv_mine = (ctx_rank * heads) // group

    residual = tokens.astype(f32)
    normed_attn, attn_norm_back = jax.vjp(rms_norm, residual, gain_attn)
    normed_low = normed_attn.astype(bf16)
    if kernels:
        kv_cols = key_value_weight.reshape(weight_rows, 2, kv_heads, HEAD_DIMENSION)
        kv_cols = jnp.transpose(kv_cols, (0, 2, 1, 3)).reshape(weight_rows, -1)
    else:
        kv_split = key_value_weight.reshape(weight_rows, 2, kv_heads, HEAD_DIMENSION)
        send = []
        for index in range(ctx_size):
            cols = slice(index * width, (index + 1) * width)
            send.append(
                jnp.concatenate(
                    [
                        w_query[:, cols],
                        kv_split[:, 0, kv_of[index]],
                        kv_split[:, 1, kv_of[index]],
                        w_out[cols].T,
                    ],
                    axis=1,
                )
            )
        send = jnp.pad(jnp.stack(send), ((0, 0), (0, padded_rows - weight_rows), (0, 0)))
        rows_all, weights = plain_enter(normed_low, send)
    proj_width = width + 2 * HEAD_DIMENSION

    cosine, sine = rotary(length)
    bias = jnp.concatenate(
        [
            lax.dynamic_slice_in_dim(b_query, ctx_rank * width, width),
            lax.dynamic_slice_in_dim(key_value_bias[0], kv_mine * HEAD_DIMENSION, HEAD_DIMENSION),
            lax.dynamic_slice_in_dim(key_value_bias[1], kv_mine * HEAD_DIMENSION, HEAD_DIMENSION),
        ]
    )[None]
    sinks_mine = lax.dynamic_slice_in_dim(sinks, ctx_rank * heads, heads)[None]
    if kernels:
        dy_wide = -(-model // 128) * 128
        upstream_low = jnp.pad(cotangent, ((0, 0), (0, dy_wide - model)))
        query, keys, values, attended, attended_low, log_total, rows_all, weights, dy_all, attn_out = front(
            sinks_mine, normed_low, w_query, kv_cols, jnp.transpose(w_out), upstream_low, bias, cosine, sine, heads,
            kv_of, padded_rows, ctx_size, 2,
        )
    else:
        weights = weights[:, :weight_rows].reshape(model, 2 * width + 2 * HEAD_DIMENSION)
        w_in, w_back = weights[:, :proj_width], weights[:, proj_width:]
        query, keys, values = project(rows_all, w_in, bias, cosine, sine, heads)
        attended, attended_low, log_total, out_part = attend(sinks_mine, query, keys, values, w_back)
        attn_out = plain_sum(out_part, "ctx")
    hidden = residual + attn_out.astype(f32) + b_out

    normed_moe, moe_norm_back = jax.vjp(rms_norm, hidden, gain_moe)
    moe_input = normed_moe.astype(bf16)
    logits = jnp.dot(moe_input, w_router, preferred_element_type=f32) + b_router
    onehot = (routes[..., None] == jnp.arange(experts, dtype=jnp.int32)).astype(f32)
    chosen = jnp.sum(onehot * logits[:, None, :], axis=-1)
    gates = jax.nn.softmax(chosen, axis=-1)
    gate_table = jnp.sum(onehot * gates[..., None], axis=1)
    gate_high = lax.reduce_precision(gate_table, 8, 7)
    gate_low = (gate_table - gate_high).astype(bf16)
    wide = -(-(model + 2 * experts) // 128) * 128
    payload = jnp.concatenate(
        [moe_input, gate_high.astype(bf16), gate_low, jnp.zeros((tok_rows, wide - model - 2 * experts), bf16)],
        axis=1,
    )

    gate_up_rows = jnp.transpose(w_gate_up[0], (1, 2, 0)).reshape(-1, model)
    down_weight = w_down[0]
    units = down_weight.shape[0]
    splits = seq_size * tp_size
    lead = ((seq_rank == 0) & (tp_rank == 0)).astype(f32).reshape(1, 1)
    tail = model // 128 * 128
    at = jnp.arange(wide - tail)[None] + tail - model
    pick = ((at == ctx_rank) | (at == experts + ctx_rank)).astype(bf16)
    pick = jnp.concatenate([pick, jnp.zeros((15, wide - tail), bf16)])
    back_wide = -(-(model + 2 * splits * experts) // 128) * 128
    column = 2 * (ctx_rank * splits + seq_rank * tp_size + tp_rank)
    at = jnp.arange(back_wide - tail)[None] + tail - model
    place = jnp.concatenate([at == column, at == column + 1]).astype(bf16)
    place = jnp.concatenate([place, jnp.zeros((14, back_wide - tail), bf16)])

    def expert(rows, upstream):
        return expert_rows(
            lead, rows, upstream, gate_up_rows, b_gate_up[0].reshape(-1, 1), down_weight, b_down, pick, place
        )

    def weight_grads(rows, upstream, gated_act, proj_grad):
        return (
            jnp.dot(proj_grad, rows[:, :model], preferred_element_type=f32),
            jnp.dot(gated_act, upstream, preferred_element_type=f32),
        )

    if kernels:
        moe_all, gated_act, proj_grad, extra_rows, back_rows, gate_bias = expert_all(
            payload, dy_all, gate_up_rows, down_weight, b_gate_up[0].reshape(-1, 1), b_down, experts, back_wide,
            ctx_size, 3,
        )
        count = blocks * tok_rows
        gate_up_grad, down_grad, down_bias = weight_gradients(
            proj_grad, gated_act, moe_all.reshape(count, -1), dy_all.reshape(count, -1), model, units
        )
    else:
        pieces = blocks * tok_rows // math.gcd(blocks * tok_rows, 2048)

        def one_piece(total, packed):
            rows, upstream = (
                lax.all_gather(part, ("seq", "ctx"), axis=0, tiled=True) for part in packed
            )
            expert_part, back_part, gated_act, proj_grad, gate_bias, down_bias = expert(rows, upstream)
            more = weight_grads(rows, upstream, gated_act, proj_grad) + (gate_bias, down_bias)
            total = jax.tree.map(jnp.add, total, more)
            return total, (plain_sum(expert_part, ("seq", "ctx")), plain_sum(back_part, ("seq", "ctx")))

        start = tuple(
            jnp.zeros(shape, f32) for shape in ((2 * units, model), (units, model), (2 * units, 1), (1, model))
        )
        cut = lambda v: v.reshape(pieces, tok_rows // pieces, v.shape[1])
        total, (expert_out_sum, back_rows) = lax.scan(one_piece, start, (cut(payload), cut(cotangent)))
        gate_up_grad, down_grad, gate_bias, down_bias = total
        expert_out_sum, back_rows = (part.reshape(tok_rows, -1) for part in (expert_out_sum, back_rows))
    grad_w_gate_up = jnp.transpose(gate_up_grad.reshape(2, units, model), (2, 0, 1))[None]
    grad_b_gate_up = gate_bias.reshape(1, 2, units)
    grad_w_down = down_grad[None]
    grad_b_down = down_bias
    upstream = cotangent.astype(f32)
    gate_grad = back_rows[:, model : model + 2 * splits * experts].astype(f32)
    gate_grad = jnp.sum(gate_grad.reshape(tok_rows, experts, 2 * splits), axis=-1)
    gate_grad = jnp.sum(onehot * gate_grad[:, None], axis=-1)
    chosen_grad = gates * (gate_grad - jnp.sum(gates * gate_grad, axis=1, keepdims=True))
    logit_grad = jnp.sum(onehot * chosen_grad[..., None], axis=1).astype(bf16)
    grad_w_router = project_grad(logit_grad, moe_input)
    grad_b_router = jnp.sum(logit_grad, axis=0, dtype=f32)
    moe_grad = back_rows[:, :model].astype(f32) + across(logit_grad, w_router)
    hidden_norm_grad, grad_gain_moe = moe_norm_back(moe_grad)
    hidden_grad = upstream + hidden_norm_grad
    branch_grad = hidden_grad.astype(bf16)
    grad_b_out = jnp.sum(branch_grad, axis=0, dtype=f32)
    if kernels:
        expert_out_sum, input_rows, grads, gain_part, bias_part, dsinks = rear(
            sinks_mine, gated_act, down_weight, extra_rows, branch_grad, rows_all, weights, query, keys, values,
            attended, attended_low, log_total, cosine, sine, weight_rows, padded_rows, ctx_size, 5,
        )
        gain_part = gain_part[0] / gain_attn
        sum_q, sum_kv = bias_part[0, :width], bias_part[0, width:].reshape(2, HEAD_DIMENSION)
    else:
        branch_all = lax.all_gather(branch_grad, "ctx", axis=0, tiled=True)
        out_grad = jnp.dot(branch_all, w_back, preferred_element_type=f32).astype(bf16)
        dq, dkv, dsinks = attend_back(
            sinks_mine, query, keys, values, attended, log_total, out_grad, cosine, sine
        )
        both = jnp.concatenate([dq, dkv], axis=1)
        input_rows = spread_rows(both, w_in)
        grad_in = project_grad(rows_all, both)
        grad_out = project_grad(branch_all, attended_low)
        gain_part = jnp.sum(grad_in * w_in.astype(f32), axis=1) / gain_attn
        grads = jnp.concatenate([grad_in, grad_out], axis=1).astype(bf16).reshape(blocks, weight_rows, -1)
        grads = jnp.pad(grads, ((0, 0), (0, padded_rows - weight_rows), (0, 0)))
        sum_q = jnp.sum(dq, axis=0, dtype=f32)
        sum_kv = jnp.sum(dkv, axis=0, dtype=f32).reshape(2, HEAD_DIMENSION)
    mixed = (hidden + expert_out_sum.astype(f32)).astype(bf16)

    at_q = lax.dynamic_update_slice_in_dim(jnp.zeros_like(b_query), sum_q, ctx_rank * width, 0)
    at_kv = lax.dynamic_update_slice_in_dim(
        jnp.zeros_like(key_value_bias), sum_kv, kv_mine * HEAD_DIMENSION, 1
    )
    at_sinks = lax.dynamic_update_slice_in_dim(jnp.zeros_like(sinks), dsinks[0], ctx_rank * heads, 0)
    aligned = lambda n: -(-n // 128) * 128
    late, starts, at = [], [], 0
    for part in (at_q, at_kv.reshape(-1), at_sinks, grad_b_router):
        starts.append(at)
        late.append(jnp.pad(part, (0, aligned(part.shape[0]) - part.shape[0])))
        at += aligned(part.shape[0])
    late = jnp.pad(jnp.concatenate(late), (0, model - at))
    alike = jnp.concatenate([grad_gain_moe[None], grad_b_out[None], grad_w_router], axis=0)
    halves = alike.shape[0] // 2
    if kernels:
        part = lax.dynamic_slice_in_dim(alike, tp_rank * halves, halves)
        small = jnp.concatenate([gain_part[None], late[None], part], axis=0)
        small = jnp.pad(small, ((0, -small.shape[0] % 8), (0, 0)))
        normed_grad, kept, small = leave(input_rows, grads, small, halves, ctx_size, 7)
        owned = lax.all_to_all(kept, "ctx", split_axis=0, concat_axis=0, tiled=True)
        spans = [(0, 0)] + [(1, start) for start in starts] + [(2, 0), (3, 0), (4, 0)]
        shapes = [(1, model)] + [(1, v.size) for v in (at_q, at_kv, at_sinks, grad_b_router)]
        shapes += [(1, model), (1, model), (experts, model)]
        grad_w_query, grad_kv, grad_wt, *sums = settle_gradients(
            owned, small, width, weight_rows, kv_of, spans, shapes
        )
        grad_w_out = jnp.transpose(grad_wt)
        grad_kv = grad_kv.reshape(weight_rows, kv_heads, 2, HEAD_DIMENSION)
        grad_w_key_value = jnp.transpose(grad_kv, (0, 2, 1, 3)).reshape(weight_rows, 2, kv_width)
    else:
        small = jnp.concatenate([gain_part[None], late[None], alike], axis=0)
        normed_grad, owned, small = plain_leave(input_rows, grads, small)
        owned = owned[:, :weight_rows].astype(f32)
        grad_w_query = jnp.transpose(owned[:, :, :width], (1, 0, 2)).reshape(weight_rows, -1)
        grad_kv = owned[:, :, width:proj_width].reshape(kv_heads, -1, weight_rows, 2, HEAD_DIMENSION)
        grad_w_key_value = jnp.transpose(jnp.sum(grad_kv, axis=1), (1, 2, 0, 3)).reshape(
            weight_rows, 2, kv_width
        )
        grad_w_out = jnp.transpose(owned[:, :, proj_width:], (0, 2, 1)).reshape(-1, weight_rows)
        sums = [small[0]]
        sums += [small[1, at : at + v.size] for at, v in zip(starts, (at_q, at_kv, at_sinks, grad_b_router))]
        sums += [small[2], small[3], small[4:]]
    tokens_norm_grad, _ = attn_norm_back(normed_grad.astype(f32))
    grad_tokens = (hidden_grad + tokens_norm_grad).astype(bf16)

    return (
        mixed,
        grad_tokens,
        sums[0].reshape(gain_attn.shape),
        grad_w_query,
        sums[1].reshape(b_query.shape),
        grad_w_key_value,
        sums[2].reshape(key_value_bias.shape),
        sums[3].reshape(sinks.shape),
        grad_w_out,
        sums[6].reshape(b_out.shape),
        sums[5].reshape(gain_moe.shape),
        jnp.transpose(sums[7]),
        sums[4].reshape(b_router.shape),
        grad_w_gate_up,
        grad_b_gate_up,
        grad_w_down,
        grad_b_down,
    )


def solution(mesh):
    in_specs = (
        P(("seq", "ctx"), None),
        P(),
        P(("seq", "ctx"), "tp"),
        P("tp"),
        P(("seq", "ctx"), None, "tp"),
        P(None, "tp"),
        P("tp"),
        P("tp", ("seq", "ctx")),
        P(),
        P(),
        P(),
        P(),
        P(("seq", "ctx"), None),
        P("ctx", None, None, ("seq", "tp")),
        P("ctx", None, ("seq", "tp")),
        P("ctx", ("seq", "tp"), None),
        P("ctx", None),
        P(("seq", "ctx"), None),
    )
    out_specs = (
        P(("seq", "ctx"), None),
        P(("seq", "ctx"), None),
        P(),
        P(("seq", "ctx"), "tp"),
        P("tp"),
        P(("seq", "ctx"), None, "tp"),
        P(None, "tp"),
        P("tp"),
        P("tp", ("seq", "ctx")),
        P(),
        P(),
        P(),
        P(),
        P("ctx", None, None, ("seq", "tp")),
        P("ctx", None, ("seq", "tp")),
        P("ctx", ("seq", "tp"), None),
        P("ctx", None),
    )
    return jax.shard_map(
        on_device, mesh=mesh, in_specs=in_specs, out_specs=out_specs, check_vma=False
    )
```
